32 devices in a mesh: leaf: 8 (over z, x), group: 4 (over y, core).
Axes of the slice: x: 2, y: 2, z: 4, core: 2. Of those that a mesh axis runs over, the one named last changes fastest.
Arguments:
- q_two: float32 [65536, 256], P(('group', 'leaf'))
- q_one: float32 [65536, 256], P(('group', 'leaf'))
- sources: float32 [65536, 256], P(('group', 'leaf'))
- coupling_two: float32 [2, 256, 256], replicated, as said below
- coupling_one: float32 [256, 256], replicated, as said below
Outputs:
- panel_one: float32 [65536, 256], P(('group', 'leaf'))
- solution: float32 [65536, 256], P(('group', 'leaf'))
Inputs may be any that keep to these rules, and one draw needn't show every extreme that they name: coupling_two[0], coupling_two[1] and coupling_one are symmetric and positive definite. `coupling_one`: symmetric and positive definite.
All inputs are finite; a program needn't handle non-finite values.
Results may differ from the reference program's by a relative error of at most 0.00019.
Values sent between devices are 32-bit elements; how exact they have to be, the bound alone decides.
No kernel may reach another device: no remote copies, remote signals or barrier semaphores. Data moves between devices by JAX's collectives and lax.ppermute only.
A program may use at most 64 MiB of HBM per device.

```python
import math
import jax
import jax.numpy as jnp
from jax import lax

LEAF = 2048
R = 256
POINTS = 65536


def noise_draw(key):
    return jax.random.normal(key, (POINTS, R), jnp.float32)


def panel_parts(key):
    base_key = jax.random.fold_in(key, 7301)
    keys = jax.random.split(base_key, 6)
    first = noise_draw(keys[0])
    first = first + 0.6 * jnp.roll(first, 1, axis=1)
    second = noise_draw(keys[1])
    second = second + 0.6 * jnp.roll(second, 1, axis=1)
    third = noise_draw(keys[2])
    unit_two = first
    unit_one = 0.8 * first + 0.6 * second
    unit_src = 0.6 * unit_two + 0.4 * unit_one + 0.7 * third
    positions = jnp.arange(POINTS)
    per_quarter = POINTS // 4 // LEAF
    leaf_pos = (positions // LEAF % per_quarter).astype(jnp.float32)
    rising = jnp.exp(math.log(3.0) * leaf_pos / max(per_quarter - 1, 1))
    rough = jnp.exp(jax.random.uniform(keys[3], (POINTS,), jnp.float32, 0.0, math.log(3.3)))
    row_scale = (rising * rough)[:, None]
    col_two = jnp.exp(jax.random.uniform(keys[4], (R,), jnp.float32, 0.0, math.log(3.0)))[None, :]
    col_one = jnp.exp(jax.random.uniform(keys[5], (R,), jnp.float32, 0.0, math.log(3.0)))[None, :]
    unit = 1.0 / math.sqrt(POINTS / 2 * 17.0)
    panel_two = unit_two * row_scale * col_two * unit
    panel_one = unit_one * row_scale * col_one * unit
    fields = unit_src * row_scale / 3.0
    return (panel_two, panel_one, fields)


def definite_draw(key, count):
    keys = jax.random.split(key, 2)
    values = jax.random.uniform(keys[0], (count, R, R), jnp.float32, -1.0, 1.0)
    upper = jnp.triu(values, 1)
    off_diag = (upper + jnp.swapaxes(upper, 1, 2)) / R
    diag_vals = 1.05 + jnp.exp(jax.random.uniform(keys[1], (count, R), jnp.float32, math.log(0.2), math.log(2.0)))
    return off_diag + jnp.eye(R, dtype=jnp.float32)[None, :, :] * diag_vals[:, :, None]


def draw_q_two(key, part):
    return panel_parts(key)[0]


def draw_q_one(key, part):
    return panel_parts(key)[1]


def draw_sources(key, part):
    return panel_parts(key)[2]


def draw_coupling_two(key, part):
    return definite_draw(jax.random.fold_in(key, 501), 2)


def draw_coupling_one(key, part):
    return definite_draw(jax.random.fold_in(key, 502), 1)[0]


def setup_inputs(seed: int = 0) -> dict:
    arg_keys = jax.random.split(jax.random.key(seed), 6)
    return {
        "q_two": draw_q_two(jax.random.fold_in(arg_keys[5], 71), 0),
        "q_one": draw_q_one(jax.random.fold_in(arg_keys[5], 71), 0),
        "sources": draw_sources(jax.random.fold_in(arg_keys[5], 71), 0),
        "coupling_two": draw_coupling_two(jax.random.fold_in(arg_keys[5], 71), 0),
        "coupling_one": draw_coupling_one(jax.random.fold_in(arg_keys[5], 71), 0),
    }


HIGH = lax.Precision.HIGHEST

def gram_of(left, right):
    return lax.dot_general(left.astype(jnp.float32), right.astype(jnp.float32), (((0,), (0,)), ((), ())), precision=HIGH, preferred_element_type=jnp.float32)

def times_matrix(left, right):
    return jnp.dot(left.astype(jnp.float32), right.astype(jnp.float32), precision=HIGH, preferred_element_type=jnp.float32)

def definite_solve(matrix, target):
    factor = jnp.linalg.cholesky(matrix)
    lower_part = lax.linalg.triangular_solve(factor, target, left_side=True, lower=True)
    return lax.linalg.triangular_solve(factor, lower_part, left_side=True, lower=True, transpose_a=True)

def reference(q_two, q_one, sources, coupling_two, coupling_one):
    half_rows = POINTS // 2
    panels = []
    fields = []
    for which in range(2):
        block_two = q_two[which * half_rows:(which + 1) * half_rows]
        block_one = q_one[which * half_rows:(which + 1) * half_rows]
        block_src = sources[which * half_rows:(which + 1) * half_rows]
        gram_two = gram_of(block_two, block_two)
        cross = gram_of(block_two, block_one)
        projected = gram_of(block_two, block_src)
        solved = definite_solve(coupling_two[which] + gram_two, jnp.concatenate([cross, projected], axis=1))
        update = times_matrix(block_two, solved)
        panels.append(block_one - update[:, :R])
        fields.append(block_src - update[:, R:])
    panel_one = jnp.concatenate(panels, axis=0)
    level_field = jnp.concatenate(fields, axis=0)
    gram_one = gram_of(q_one, panel_one)
    proj_one = gram_of(q_one, level_field)
    weights = definite_solve(coupling_one + gram_one, proj_one)
    solution = level_field - times_matrix(panel_one, weights)
    return (panel_one, solution)
```

```python
import functools

import jax
import jax.numpy as jnp
from jax import lax
from jax.experimental import pallas as pl
from jax.experimental.pallas import tpu as pltpu
from jax.sharding import PartitionSpec as P

HIGH = lax.Precision.HIGHEST
AXES = ("leaf", "group")
F32 = jnp.float32
BF16 = jnp.bfloat16
R = 256
LANES = 128
PANEL = 32
TILE = 512
VMEM_LIMIT = 40 * 1024 * 1024
TERMS = 2304
TOP = 896


def split2(x):
    high = x.astype(BF16)
    return high, (x - high.astype(F32)).astype(BF16)


def split3(x):
    high = x.astype(BF16)
    rest = x - high.astype(F32)
    mid = rest.astype(BF16)
    return high, mid, (rest - mid.astype(F32)).astype(BF16)


def dot(left, right):
    return jnp.dot(left, right, preferred_element_type=F32)


def dot_t(left, right):
    return lax.dot_general(left, right, (((0,), (0,)), ((), ())), preferred_element_type=F32)


def dot_full(left, right):
    return jnp.dot(left, right, precision=HIGH, preferred_element_type=F32)


def dot_t_full(left, right):
    return lax.dot_general(
        left, right, (((0,), (0,)), ((), ())), precision=HIGH, preferred_element_type=F32
    )


def store_symmetric(ref, row, block):
    ref[row : row + 128, :] = block[:128, :128]
    ref[row + 128 : row + 256, :] = block[128:, :128]
    ref[row + 256 : row + 384, :] = block[128:, 128:]


def store_square(ref, row, block):
    ref[row : row + 256, :] = block[:, :128]
    ref[row + 256 : row + 512, :] = block[:, 128:]


def load_symmetric(ref, row):
    lower = ref[row + 128 : row + 256, :]
    top = jnp.concatenate([ref[row : row + 128, :], lower.T], axis=1)
    bottom = jnp.concatenate([lower, ref[row + 256 : row + 384, :]], axis=1)
    return jnp.concatenate([top, bottom], axis=0)


def load_square(ref, row):
    return jnp.concatenate([ref[row : row + 256, :], ref[row + 256 : row + 512, :]], axis=1)


def gram_kernel(q_two, q_one, sources, out, acc):
    step = pl.program_id(0)

    @pl.when(step == 0)
    def _():
        acc[...] = jnp.zeros_like(acc)

    h2, l2 = split2(q_two[...])
    h1, l1 = split2(q_one[...])
    hs, ls = split2(sources[...])
    acc[0] += dot_t(h2, h2)
    acc[1] += dot_t(h2, l2)
    acc[2] += dot_t(h2, h1) + dot_t(h2, l1) + dot_t(l2, h1)
    acc[3] += dot_t(h2, hs) + dot_t(h2, ls) + dot_t(l2, hs)
    acc[4] += dot_t(h1, h1)
    acc[5] += dot_t(h1, l1)
    acc[6] += dot_t(h1, hs) + dot_t(h1, ls) + dot_t(l1, hs)

    @pl.when(step == pl.num_programs(0) - 1)
    def _():
        cross2 = acc[1]
        store_symmetric(out, 0, acc[0] + cross2 + cross2.T)
        store_square(out, 384, acc[2])
        store_square(out, 896, acc[3])
        cross1 = acc[5]
        store_symmetric(out, 1408, acc[4] + cross1 + cross1.T)
        store_square(out, 1792, acc[6])


def gram_terms(q_two, q_one, sources):
    rows = q_two.shape[0]
    spec = pl.BlockSpec((TILE, R), lambda i: (i, 0))
    return pl.pallas_call(
        gram_kernel,
        grid=(rows // TILE,),
        in_specs=[spec, spec, spec],
        out_specs=pl.BlockSpec((TERMS, LANES), lambda i: (0, 0)),
        out_shape=jax.ShapeDtypeStruct((TERMS, LANES), F32),
        scratch_shapes=[pltpu.VMEM((7, R, R), F32)],
        compiler_params=pltpu.CompilerParams(vmem_limit_bytes=VMEM_LIMIT),
        name="gram",
    )(q_two, q_one, sources)


def spread_lane(x, lane):
    return jnp.broadcast_to(x[:, lane : lane + 1], (8, LANES))


def spread_row(x, row):
    return jnp.broadcast_to(x[row : row + 1, :], (8, LANES))


def reciprocal(x):
    y = pl.reciprocal(x, approx=True)
    y = y * (2.0 - x * y)
    return y * (2.0 - x * y)


def eliminate(diag, rows):
    lane = lax.broadcasted_iota(jnp.int32, (8, LANES), 1)
    sub = lax.broadcasted_iota(jnp.int32, (8, LANES), 0)
    for k in range(0, PANEL, 2):
        at, s = k // 8, k % 8
        c1 = [spread_lane(d, k) for d in diag]
        c2 = [spread_lane(d, k + 1) for d in diag]
        a = spread_row(c1[at], s)
        b = spread_row(c1[at], s + 1)
        c = spread_row(c2[at], s + 1)
        inv = reciprocal(a * c - b * b)
        e, f, g = c * inv, b * inv, a * inv
        first, second = lane == k, lane == k + 1
        either = first | second
        r1 = jnp.where(first, 1.0, jnp.where(second, 0.0, spread_row(diag[at], s)))
        r2 = jnp.where(first, 0.0, jnp.where(second, 1.0, spread_row(diag[at], s + 1)))
        p1 = [spread_row(x, s) for x in rows[at]]
        p2 = [spread_row(x, s + 1) for x in rows[at]]
        n1, n2 = e * r1 - f * r2, g * r2 - f * r1
        m1 = [e * x - f * y for x, y in zip(p1, p2)]
        m2 = [g * y - f * x for x, y in zip(p1, p2)]
        for i in range(4):
            base = jnp.where(either, 0.0, diag[i])
            x = list(rows[i])
            u, v = c1[i], c2[i]
            if i == at:
                own1, own2 = sub == s, sub == s + 1
                own = own1 | own2
                base = jnp.where(own, 0.0, base)
                x = [jnp.where(own, 0.0, y) for y in x]
                u = jnp.where(own1, -1.0, jnp.where(own2, 0.0, u))
                v = jnp.where(own2, -1.0, jnp.where(own1, 0.0, v))
            diag[i] = base - u * n1 - v * n2
            rows[i] = [y - u * m - v * n for y, m, n in zip(x, m1, m2)]
    return diag, rows


def stack_left(x):
    h, m, l = split3(x)
    return jnp.concatenate([h, h, m, h, l, m], axis=0)


def stack_right(x):
    h, m, l = split3(x)
    return jnp.concatenate([h, m, h, l, h, m], axis=0)


def invert(matrix, work):
    eye = lax.broadcasted_iota(jnp.int32, (R, R), 0) == lax.broadcasted_iota(jnp.int32, (R, R), 1)
    diagonal = jnp.where(eye, matrix, 0.0)
    scale_row = lax.rsqrt(jnp.sum(diagonal, axis=0, keepdims=True))
    scale_col = lax.rsqrt(jnp.sum(diagonal, axis=1, keepdims=True))
    work[...] = matrix * scale_col * scale_row
    lanes = lax.broadcasted_iota(jnp.int32, (PANEL, R), 1)
    lanes_all = lax.broadcasted_iota(jnp.int32, (R, R), 1)

    def sweep(j, carry):
        start = pl.multiple_of(j * PANEL, PANEL)
        panel = work[pl.ds(start, PANEL), :]
        shift = lax.rem(j, 4) * PANEL
        half = jnp.where(j < 4, panel[:, :LANES], panel[:, LANES:])
        diag = pltpu.roll(half, lax.rem(LANES - shift, LANES), axis=1)
        diag_parts = [diag[8 * i : 8 * i + 8, :] for i in range(4)]
        row_parts = [
            [panel[8 * i : 8 * i + 8, :LANES], panel[8 * i : 8 * i + 8, LANES:]] for i in range(4)
        ]
        diag_parts, row_parts = eliminate(diag_parts, row_parts)
        inverse = pltpu.roll(jnp.concatenate(diag_parts, axis=0), shift, axis=1)
        inverse = jnp.concatenate([inverse, inverse], axis=1)
        product = jnp.concatenate([jnp.concatenate(x, axis=1) for x in row_parts], axis=0)
        inside = (lanes >= start) & (lanes < start + PANEL)
        swept = jnp.where(inside, -inverse, product)
        change = dot_t(stack_left(panel), stack_right(swept))
        inside_all = (lanes_all >= start) & (lanes_all < start + PANEL)
        work[...] = jnp.where(inside_all, 0.0, work[...]) - change
        work[pl.ds(start, PANEL), :] = swept
        return carry

    lax.fori_loop(0, R // PANEL, sweep, 0)
    return -(work[...] * scale_col * scale_row)


def level_kernel(terms, coupling, x_out, y_out, top_out, work):
    half = lax.axis_index("group") // 2
    inverse = invert(coupling[half] + load_symmetric(terms, 0), work)
    cross = load_square(terms, 384)
    x = dot_full(inverse, cross)
    y = dot_full(inverse, load_square(terms, 896))
    x_out[...] = x
    y_out[...] = y
    store_symmetric(top_out, 0, load_symmetric(terms, 1408) - dot_t_full(cross, x))
    store_square(top_out, 384, load_square(terms, 1792) - dot_t_full(cross, y))


def level_solve(terms, coupling):
    square = jax.ShapeDtypeStruct((R, R), F32)
    return pl.pallas_call(
        level_kernel,
        out_shape=(square, square, jax.ShapeDtypeStruct((TOP, LANES), F32)),
        scratch_shapes=[pltpu.VMEM((R, R), F32)],
        compiler_params=pltpu.CompilerParams(vmem_limit_bytes=VMEM_LIMIT),
        name="level_solve",
    )(terms, coupling)


def root_kernel(top, coupling, x, y, w_out, z_out, work):
    inverse = invert(coupling[...] + load_symmetric(top, 0), work)
    w = dot_full(inverse, load_square(top, 384))
    w_out[...] = w
    z_out[...] = y[...] - dot_full(x[...], w)


def root_solve(top, coupling, x, y):
    square = jax.ShapeDtypeStruct((R, R), F32)
    return pl.pallas_call(
        root_kernel,
        out_shape=(square, square),
        scratch_shapes=[pltpu.VMEM((R, R), F32)],
        compiler_params=pltpu.CompilerParams(vmem_limit_bytes=VMEM_LIMIT),
        name="root_solve",
    )(top, coupling, x, y)


def dot_three(lh, ll, rh, rl):
    return dot(lh, rh) + (dot(lh, rl) + dot(ll, rh))


def panel_kernel(q_two, q_one, x, out):
    out[...] = q_one[...] - dot_three(*split2(q_two[...]), *split2(x[...]))


def field_kernel(q_two, q_one, sources, w, z, out):
    change = dot_three(*split2(q_one[...]), *split2(w[...]))
    change += dot_three(*split2(q_two[...]), *split2(z[...]))
    out[...] = sources[...] - change


def update(kernel, tall, square, name):
    rows = tall[0].shape[0]
    spec = pl.BlockSpec((TILE, R), lambda i: (i, 0))
    whole = pl.BlockSpec((R, R), lambda i: (0, 0))
    return pl.pallas_call(
        kernel,
        grid=(rows // TILE,),
        in_specs=[spec] * len(tall) + [whole] * len(square),
        out_specs=spec,
        out_shape=jax.ShapeDtypeStruct((rows, R), F32),
        compiler_params=pltpu.CompilerParams(vmem_limit_bytes=VMEM_LIMIT),
        name=name,
    )(*tall, *square)


def exchange(x, mask):
    count = lax.axis_size(AXES)
    return lax.ppermute(x, AXES, [(i, i ^ mask) for i in range(count)])


def code_of(index, bits):
    code = 0
    for place, bit in enumerate(bits):
        code = code | ((index >> bit) & 1) << place
    return code


def mask_of(code, bits):
    return sum(1 << bit for place, bit in enumerate(bits) if code >> place & 1)


def reduce_scatter(x, index, bits):
    count = 1 << len(bits)
    mine = code_of(index, bits)
    parts = x.reshape(count, x.shape[0] // count, x.shape[1])
    got = lax.dynamic_index_in_dim(parts, mine, 0, keepdims=False)
    arrived = []
    for other in range(1, count):
        part = lax.dynamic_index_in_dim(parts, mine ^ other, 0, keepdims=False)
        arrived.append(exchange(part, mask_of(other, bits)))
    for part in arrived:
        got = got + part
    return got


def all_gather(x, index, bits):
    count = 1 << len(bits)
    mine = code_of(index, bits)
    pieces = [x] + [exchange(x, mask_of(other, bits)) for other in range(1, count)]
    out = jnp.zeros((count,) + x.shape, x.dtype)
    for other, piece in enumerate(pieces):
        out = lax.dynamic_update_index_in_dim(out, piece, mine ^ other, 0)
    return out.reshape(count * x.shape[0], x.shape[1])


def per_device(q_two, q_one, sources, coupling_two, coupling_one):
    leaf_bits = lax.axis_size("leaf").bit_length() - 1
    index = lax.axis_index(AXES)
    stages = [[0]]
    for low in range(2, leaf_bits + 2, 3):
        stages.append(list(range(low, min(low + 3, leaf_bits + 2))))
    terms = gram_terms(q_two, q_one, sources)
    for bits in stages:
        terms = reduce_scatter(terms, index, bits)
    for bits in reversed(stages):
        terms = all_gather(terms, index, bits)
    x, y, top = level_solve(terms, coupling_two)
    mine = index & 1
    parts = top.reshape(2, TOP // 2, LANES)
    part = lax.dynamic_index_in_dim(parts, mine, 0, keepdims=False)
    part = part + exchange(part, 2)
    top = all_gather(part, index, [0])
    panel_one = update(panel_kernel, [q_two, q_one], [x], "panel")
    w, z = root_solve(top, coupling_one, x, y)
    solution = update(field_kernel, [q_two, q_one, sources], [w, z], "field")
    return (panel_one, solution)


def solution(mesh):
    placed = P(("group", "leaf"), None)
    return jax.shard_map(
        per_device,
        mesh=mesh,
        in_specs=(placed, placed, placed, P(), P()),
        out_specs=(placed, placed),
        check_vma=False,
    )
```

```python
import functools

import jax
import jax.numpy as jnp
from jax import lax
from jax.experimental import pallas as pl
from jax.experimental.pallas import tpu as pltpu
from jax.sharding import PartitionSpec as P

HIGH = lax.Precision.HIGHEST
AXES = ("leaf", "group")
F32 = jnp.float32
BF16 = jnp.bfloat16
R = 256
LANES = 128
PANEL = 32
TILE = 512
VMEM_LIMIT = 40 * 1024 * 1024
TERMS = 2304
TOP = 896


def split2(x):
    high = x.astype(BF16)
    return high, (x - high.astype(F32)).astype(BF16)


def split3(x):
    high = x.astype(BF16)
    rest = x - high.astype(F32)
    mid = rest.astype(BF16)
    return high, mid, (rest - mid.astype(F32)).astype(BF16)


def dot(left, right):
    return jnp.dot(left, right, preferred_element_type=F32)


def dot_t(left, right):
    return lax.dot_general(left, right, (((0,), (0,)), ((), ())), preferred_element_type=F32)


def dot_full(left, right):
    return jnp.dot(left, right, precision=HIGH, preferred_element_type=F32)


def dot_t_full(left, right):
    return lax.dot_general(
        left, right, (((0,), (0,)), ((), ())), precision=HIGH, preferred_element_type=F32
    )


def store_symmetric(ref, row, block):
    ref[row : row + 128, :] = block[:128, :128]
    ref[row + 128 : row + 256, :] = block[128:, :128]
    ref[row + 256 : row + 384, :] = block[128:, 128:]


def store_square(ref, row, block):
    ref[row : row + 256, :] = block[:, :128]
    ref[row + 256 : row + 512, :] = block[:, 128:]


def load_symmetric(ref, row):
    lower = ref[row + 128 : row + 256, :]
    top = jnp.concatenate([ref[row : row + 128, :], lower.T], axis=1)
    bottom = jnp.concatenate([lower, ref[row + 256 : row + 384, :]], axis=1)
    return jnp.concatenate([top, bottom], axis=0)


def load_square(ref, row):
    return jnp.concatenate([ref[row : row + 256, :], ref[row + 256 : row + 512, :]], axis=1)


def gram_kernel(q_two, q_one, sources, out, acc):
    step = pl.program_id(0)

    @pl.when(step == 0)
    def _():
        acc[...] = jnp.zeros_like(acc)

    h2, l2 = split2(q_two[...])
    h1, l1 = split2(q_one[...])
    hs, ls = split2(sources[...])
    acc[0] += dot_t(h2, h2)
    acc[1] += dot_t(h2, l2)
    acc[2] += dot_t(h2, h1) + dot_t(h2, l1) + dot_t(l2, h1)
    acc[3] += dot_t(h2, hs) + dot_t(h2, ls) + dot_t(l2, hs)
    acc[4] += dot_t(h1, h1)
    acc[5] += dot_t(h1, l1)
    acc[6] += dot_t(h1, hs) + dot_t(h1, ls) + dot_t(l1, hs)

    @pl.when(step == pl.num_programs(0) - 1)
    def _():
        cross2 = acc[1]
        store_symmetric(out, 0, acc[0] + cross2 + cross2.T)
        store_square(out, 384, acc[2])
        store_square(out, 896, acc[3])
        cross1 = acc[5]
        store_symmetric(out, 1408, acc[4] + cross1 + cross1.T)
        store_square(out, 1792, acc[6])


def gram_terms(q_two, q_one, sources):
    rows = q_two.shape[0]
    spec = pl.BlockSpec((TILE, R), lambda i: (i, 0))
    return pl.pallas_call(
        gram_kernel,
        grid=(rows // TILE,),
        in_specs=[spec, spec, spec],
        out_specs=pl.BlockSpec((TERMS, LANES), lambda i: (0, 0)),
        out_shape=jax.ShapeDtypeStruct((TERMS, LANES), F32),
        scratch_shapes=[pltpu.VMEM((7, R, R), F32)],
        compiler_params=pltpu.CompilerParams(vmem_limit_bytes=60 * 1024 * 1024),
        name="gram",
    )(q_two, q_one, sources)


def spread_lane(x, lane):
    return jnp.broadcast_to(x[:, lane : lane + 1], (8, LANES))


def spread_row(x, row):
    return jnp.broadcast_to(x[row : row + 1, :], (8, LANES))


def reciprocal(x):
    y = pl.reciprocal(x, approx=True)
    y = y * (2.0 - x * y)
    return y * (2.0 - x * y)


def eliminate(diag, rows):
    lane = lax.broadcasted_iota(jnp.int32, (8, LANES), 1)
    sub = lax.broadcasted_iota(jnp.int32, (8, LANES), 0)
    for k in range(0, PANEL, 2):
        at, s = k // 8, k % 8
        c1 = [spread_lane(d, k) for d in diag]
        c2 = [spread_lane(d, k + 1) for d in diag]
        a = spread_row(c1[at], s)
        b = spread_row(c1[at], s + 1)
        c = spread_row(c2[at], s + 1)
        inv = reciprocal(a * c - b * b)
        e, f, g = c * inv, b * inv, a * inv
        first, second = lane == k, lane == k + 1
        either = first | second
        r1 = jnp.where(first, 1.0, jnp.where(second, 0.0, spread_row(diag[at], s)))
        r2 = jnp.where(first, 0.0, jnp.where(second, 1.0, spread_row(diag[at], s + 1)))
        p1 = [spread_row(x, s) for x in rows[at]]
        p2 = [spread_row(x, s + 1) for x in rows[at]]
        n1, n2 = e * r1 - f * r2, g * r2 - f * r1
        m1 = [e * x - f * y for x, y in zip(p1, p2)]
        m2 = [g * y - f * x for x, y in zip(p1, p2)]
        for i in range(4):
            base = jnp.where(either, 0.0, diag[i])
            x = list(rows[i])
            u, v = c1[i], c2[i]
            if i == at:
                own1, own2 = sub == s, sub == s + 1
                own = own1 | own2
                base = jnp.where(own, 0.0, base)
                x = [jnp.where(own, 0.0, y) for y in x]
                u = jnp.where(own1, -1.0, jnp.where(own2, 0.0, u))
                v = jnp.where(own2, -1.0, jnp.where(own1, 0.0, v))
            diag[i] = base - u * n1 - v * n2
            rows[i] = [y - u * m - v * n for y, m, n in zip(x, m1, m2)]
    return diag, rows


def stack_left(x):
    h, m, l = split3(x)
    return jnp.concatenate([h, h, m, h, l, m], axis=0)


def stack_right(x):
    h, m, l = split3(x)
    return jnp.concatenate([h, m, h, l, h, m], axis=0)


def invert(matrix, work):
    eye = lax.broadcasted_iota(jnp.int32, (R, R), 0) == lax.broadcasted_iota(jnp.int32, (R, R), 1)
    diagonal = jnp.where(eye, matrix, 0.0)
    scale_row = lax.rsqrt(jnp.sum(diagonal, axis=0, keepdims=True))
    scale_col = lax.rsqrt(jnp.sum(diagonal, axis=1, keepdims=True))
    work[...] = matrix * scale_col * scale_row
    lanes = lax.broadcasted_iota(jnp.int32, (PANEL, R), 1)
    lanes_all = lax.broadcasted_iota(jnp.int32, (R, R), 1)

    def sweep(j, carry):
        start = pl.multiple_of(j * PANEL, PANEL)
        panel = work[pl.ds(start, PANEL), :]
        shift = lax.rem(j, 4) * PANEL
        half = jnp.where(j < 4, panel[:, :LANES], panel[:, LANES:])
        diag = pltpu.roll(half, lax.rem(LANES - shift, LANES), axis=1)
        diag_parts = [diag[8 * i : 8 * i + 8, :] for i in range(4)]
        row_parts = [
            [panel[8 * i : 8 * i + 8, :LANES], panel[8 * i : 8 * i + 8, LANES:]] for i in range(4)
        ]
        diag_parts, row_parts = eliminate(diag_parts, row_parts)
        inverse = pltpu.roll(jnp.concatenate(diag_parts, axis=0), shift, axis=1)
        inverse = jnp.concatenate([inverse, inverse], axis=1)
        product = jnp.concatenate([jnp.concatenate(x, axis=1) for x in row_parts], axis=0)
        inside = (lanes >= start) & (lanes < start + PANEL)
        swept = jnp.where(inside, -inverse, product)
        change = dot_t(stack_left(panel), stack_right(swept))
        inside_all = (lanes_all >= start) & (lanes_all < start + PANEL)
        work[...] = jnp.where(inside_all, 0.0, work[...]) - change
        work[pl.ds(start, PANEL), :] = swept
        return carry

    lax.fori_loop(0, R // PANEL, sweep, 0)
    return -(work[...] * scale_col * scale_row)


def level_kernel(terms, coupling, x_out, y_out, top_out, work):
    half = lax.axis_index("group") // 2
    inverse = invert(coupling[half] + load_symmetric(terms, 0), work)
    cross = load_square(terms, 384)
    x = dot_full(inverse, cross)
    y = dot_full(inverse, load_square(terms, 896))
    x_out[...] = x
    y_out[...] = y
    store_symmetric(top_out, 0, load_symmetric(terms, 1408) - dot_t_full(cross, x))
    store_square(top_out, 384, load_square(terms, 1792) - dot_t_full(cross, y))


def level_solve(terms, coupling):
    square = jax.ShapeDtypeStruct((R, R), F32)
    return pl.pallas_call(
        level_kernel,
        out_shape=(square, square, jax.ShapeDtypeStruct((TOP, LANES), F32)),
        scratch_shapes=[pltpu.VMEM((R, R), F32)],
        compiler_params=pltpu.CompilerParams(vmem_limit_bytes=VMEM_LIMIT),
        name="level_solve",
    )(terms, coupling)


def root_kernel(top, coupling, x, y, w_out, z_out, work):
    inverse = invert(coupling[...] + load_symmetric(top, 0), work)
    w = dot_full(inverse, load_square(top, 384))
    w_out[...] = w
    z_out[...] = y[...] - dot_full(x[...], w)


def root_solve(top, coupling, x, y):
    square = jax.ShapeDtypeStruct((R, R), F32)
    return pl.pallas_call(
        root_kernel,
        out_shape=(square, square),
        scratch_shapes=[pltpu.VMEM((R, R), F32)],
        compiler_params=pltpu.CompilerParams(vmem_limit_bytes=VMEM_LIMIT),
        name="root_solve",
    )(top, coupling, x, y)


def dot_three(lh, ll, rh, rl):
    return dot(lh, rh) + (dot(lh, rl) + dot(ll, rh))


def panel_kernel(q_two, q_one, x, out):
    out[...] = q_one[...] - dot_three(*split2(q_two[...]), *split2(x[...]))


def field_kernel(q_two, q_one, sources, w, z, out):
    change = dot_three(*split2(q_one[...]), *split2(w[...]))
    change += dot_three(*split2(q_two[...]), *split2(z[...]))
    out[...] = sources[...] - change


def update(kernel, tall, square, name):
    rows = tall[0].shape[0]
    spec = pl.BlockSpec((TILE, R), lambda i: (i, 0))
    whole = pl.BlockSpec((R, R), lambda i: (0, 0))
    return pl.pallas_call(
        kernel,
        grid=(rows // TILE,),
        in_specs=[spec] * len(tall) + [whole] * len(square),
        out_specs=spec,
        out_shape=jax.ShapeDtypeStruct((rows, R), F32),
        compiler_params=pltpu.CompilerParams(vmem_limit_bytes=VMEM_LIMIT),
        name=name,
    )(*tall, *square)


def exchange(x, mask):
    count = lax.axis_size(AXES)
    return lax.ppermute(x, AXES, [(i, i ^ mask) for i in range(count)])


def code_of(index, bits):
    code = 0
    for place, bit in enumerate(bits):
        code = code | ((index >> bit) & 1) << place
    return code


def mask_of(code, bits):
    return sum(1 << bit for place, bit in enumerate(bits) if code >> place & 1)


def reduce_scatter(x, index, bits):
    count = 1 << len(bits)
    mine = code_of(index, bits)
    parts = x.reshape(count, x.shape[0] // count, x.shape[1])
    got = lax.dynamic_index_in_dim(parts, mine, 0, keepdims=False)
    arrived = []
    for other in range(1, count):
        part = lax.dynamic_index_in_dim(parts, mine ^ other, 0, keepdims=False)
        arrived.append(exchange(part, mask_of(other, bits)))
    for part in arrived:
        got = got + part
    return got


def all_gather(x, index, bits):
    count = 1 << len(bits)
    mine = code_of(index, bits)
    pieces = [x] + [exchange(x, mask_of(other, bits)) for other in range(1, count)]
    out = jnp.zeros((count,) + x.shape, x.dtype)
    for other, piece in enumerate(pieces):
        out = lax.dynamic_update_index_in_dim(out, piece, mine ^ other, 0)
    return out.reshape(count * x.shape[0], x.shape[1])


def scatter_leaf(x):
    count = lax.axis_size("leaf")
    parts = x.reshape(count, x.shape[0] // count, x.shape[1])
    return jnp.sum(lax.all_to_all(parts, "leaf", 0, 0), axis=0)


def gather_leaf(x):
    count = lax.axis_size("leaf")
    parts = jnp.broadcast_to(x[None], (count,) + x.shape)
    return lax.all_to_all(parts, "leaf", 0, 0).reshape(count * x.shape[0], x.shape[1])


def per_device(q_two, q_one, sources, coupling_two, coupling_one):
    index = lax.axis_index(AXES)
    terms = gram_terms(q_two, q_one, sources)
    terms = reduce_scatter(terms, index, [0])
    terms = gather_leaf(scatter_leaf(terms))
    terms = all_gather(terms, index, [0])
    x, y, top = level_solve(terms, coupling_two)
    mine = index & 1
    parts = top.reshape(2, TOP // 2, LANES)
    part = lax.dynamic_index_in_dim(parts, mine, 0, keepdims=False)
    part = part + exchange(part, 2)
    top = all_gather(part, index, [0])
    panel_one = update(panel_kernel, [q_two, q_one], [x], "panel")
    w, z = root_solve(top, coupling_one, x, y)
    solution = update(field_kernel, [q_two, q_one, sources], [w, z], "field")
    return (panel_one, solution)


def solution(mesh):
    placed = P(("group", "leaf"), None)
    return jax.shard_map(
        per_device,
        mesh=mesh,
        in_specs=(placed, placed, placed, P(), P()),
        out_specs=(placed, placed),
        check_vma=False,
    )
```

```python
import functools

import jax
import jax.numpy as jnp
from jax import lax
from jax.experimental import pallas as pl
from jax.experimental.pallas import tpu as pltpu
from jax.sharding import PartitionSpec as P

HIGH = lax.Precision.HIGHEST
AXES = ("leaf", "group")
F32 = jnp.float32
BF16 = jnp.bfloat16
R = 256
LANES = 128
PANEL = 32
TILE = 512
VMEM_LIMIT = 40 * 1024 * 1024
TERMS = 2304
TOP = 896


def split2(x):
    high = x.astype(BF16)
    return high, (x - high.astype(F32)).astype(BF16)


def split3(x):
    high = x.astype(BF16)
    rest = x - high.astype(F32)
    mid = rest.astype(BF16)
    return high, mid, (rest - mid.astype(F32)).astype(BF16)


def dot(left, right):
    return jnp.dot(left, right, preferred_element_type=F32)


def dot_t(left, right):
    return lax.dot_general(left, right, (((0,), (0,)), ((), ())), preferred_element_type=F32)


def dot_full(left, right):
    return jnp.dot(left, right, precision=HIGH, preferred_element_type=F32)


def dot_t_full(left, right):
    return lax.dot_general(
        left, right, (((0,), (0,)), ((), ())), precision=HIGH, preferred_element_type=F32
    )


def store_symmetric(ref, row, block):
    ref[row : row + 128, :] = block[:128, :128]
    ref[row + 128 : row + 256, :] = block[128:, :128]
    ref[row + 256 : row + 384, :] = block[128:, 128:]


def store_square(ref, row, block):
    ref[row : row + 256, :] = block[:, :128]
    ref[row + 256 : row + 512, :] = block[:, 128:]


def load_symmetric(ref, row):
    lower = ref[row + 128 : row + 256, :]
    top = jnp.concatenate([ref[row : row + 128, :], lower.T], axis=1)
    bottom = jnp.concatenate([lower, ref[row + 256 : row + 384, :]], axis=1)
    return jnp.concatenate([top, bottom], axis=0)


def load_square(ref, row):
    return jnp.concatenate([ref[row : row + 256, :], ref[row + 256 : row + 512, :]], axis=1)


def gram_kernel(q_two, q_one, sources, out, acc):
    step = pl.program_id(0)

    @pl.when(step == 0)
    def _():
        acc[...] = jnp.zeros_like(acc)

    h2, l2 = split2(q_two[...])
    h1, l1 = split2(q_one[...])
    hs, ls = split2(sources[...])
    acc[0] += dot_t(h2, h2)
    acc[1] += dot_t(h2, l2)
    acc[2] += dot_t(h2, h1) + dot_t(h2, l1) + dot_t(l2, h1)
    acc[3] += dot_t(h2, hs) + dot_t(h2, ls) + dot_t(l2, hs)
    acc[4] += dot_t(h1, h1)
    acc[5] += dot_t(h1, l1)
    acc[6] += dot_t(h1, hs) + dot_t(h1, ls) + dot_t(l1, hs)

    @pl.when(step == pl.num_programs(0) - 1)
    def _():
        cross2 = acc[1]
        store_symmetric(out, 0, acc[0] + cross2 + cross2.T)
        store_square(out, 384, acc[2])
        store_square(out, 896, acc[3])
        cross1 = acc[5]
        store_symmetric(out, 1408, acc[4] + cross1 + cross1.T)
        store_square(out, 1792, acc[6])


def gram_terms(q_two, q_one, sources):
    rows = q_two.shape[0]
    spec = pl.BlockSpec((TILE, R), lambda i: (i, 0))
    return pl.pallas_call(
        gram_kernel,
        grid=(rows // TILE,),
        in_specs=[spec, spec, spec],
        out_specs=pl.BlockSpec((TERMS, LANES), lambda i: (0, 0)),
        out_shape=jax.ShapeDtypeStruct((TERMS, LANES), F32),
        scratch_shapes=[pltpu.VMEM((7, R, R), F32)],
        compiler_params=pltpu.CompilerParams(vmem_limit_bytes=60 * 1024 * 1024),
        name="gram",
    )(q_two, q_one, sources)


def spread_lane(x, lane):
    return jnp.broadcast_to(x[:, lane : lane + 1], (8, LANES))


def eliminate(block, cols, rows):
    lane = lax.broadcasted_iota(jnp.int32, (8, LANES), 1)
    sub = lax.broadcasted_iota(jnp.int32, (8, LANES), 0)
    count = len(block)
    for t in range(count):
        own = [spread_lane(block[t], 8 * t + j) for j in range(8)]
        for j in range(8):
            cols[64 * t + 8 * j : 64 * t + 8 * j + 8, :] = own[j]
        rows[8 * t : 8 * t + 8, :] = block[t]
        entry = {}
        for i in range(8):
            for j in range(i + 1):
                at = 64 * t + 8 * j + i
                entry[i, j] = jnp.broadcast_to(cols[at : at + 1, :], (8, LANES))
        entry = sweep_small(entry)
        inverse = lambda i, j: entry[max(i, j), min(i, j)]
        inside = (lane >= 8 * t) & (lane < 8 * t + 8)
        old = []
        for j in range(8):
            row = jnp.broadcast_to(rows[8 * t + j : 8 * t + j + 1, :], (8, LANES))
            old.append(jnp.where(inside, jnp.where(lane == 8 * t + j, 1.0, 0.0), row))
        new = [tree_sum([inverse(i, j) * old[j] for j in range(8)]) for i in range(8)]
        for g in range(count):
            if g == t:
                continue
            base = jnp.where(inside, 0.0, block[g])
            terms = [spread_lane(block[g], 8 * t + j) * new[j] for j in range(8)]
            block[g] = base - tree_sum(terms)
        merged = new[0]
        for j in range(1, 8):
            merged = jnp.where(sub == j, new[j], merged)
        block[t] = merged
    return block


def tree_sum(terms):
    while len(terms) > 1:
        terms = [
            terms[i] + terms[i + 1] if i + 1 < len(terms) else terms[i]
            for i in range(0, len(terms), 2)
        ]
    return terms[0]


def sweep_small(entry):
    entry = dict(entry)
    get = lambda i, j: entry[max(i, j), min(i, j)]
    for k in range(0, 8, 2):
        a, b, c = get(k, k), get(k + 1, k), get(k + 1, k + 1)
        inv = pl.reciprocal(a * c - b * b, approx=True)
        e, f, g = c * inv, b * inv, a * inv
        others = [i for i in range(8) if i not in (k, k + 1)]
        left = {i: (get(i, k), get(i, k + 1)) for i in others}
        swept = {i: (e * u - f * v, g * v - f * u) for i, (u, v) in left.items()}
        for i in others:
            for j in others:
                if j <= i:
                    u, v = left[i]
                    m, n = swept[j]
                    entry[i, j] = entry[i, j] - (u * m + v * n)
        for i in others:
            entry[max(i, k), min(i, k)] = swept[i][0]
            entry[max(i, k + 1), min(i, k + 1)] = swept[i][1]
        entry[k, k], entry[k + 1, k], entry[k + 1, k + 1] = -e, f, -g
    return {key: -value for key, value in entry.items()}


def invert_half(matrix, cols, rows):
    block = eliminate([matrix[8 * i : 8 * i + 8, :] for i in range(LANES // 8)], cols, rows)
    return jnp.concatenate(block, axis=0)


def invert(matrix, cols, rows):
    eye = lax.broadcasted_iota(jnp.int32, (R, R), 0) == lax.broadcasted_iota(jnp.int32, (R, R), 1)
    diagonal = jnp.where(eye, matrix, 0.0)
    scale_row = lax.rsqrt(jnp.sum(diagonal, axis=0, keepdims=True))
    scale_col = lax.rsqrt(jnp.sum(diagonal, axis=1, keepdims=True))
    matrix = matrix * scale_col * scale_row
    side = matrix[:LANES, LANES:]
    first = invert_half(matrix[:LANES, :LANES], cols, rows)
    across = dot_full(first, side)
    second = invert_half(matrix[LANES:, LANES:] - dot_t_full(side, across), cols, rows)
    corner = -dot_full(across, second)
    first = first - dot_full(corner, across.T)
    top = jnp.concatenate([first, corner], axis=1)
    bottom = jnp.concatenate([corner.T, second], axis=1)
    return jnp.concatenate([top, bottom], axis=0) * scale_col * scale_row


SCRATCH = [pltpu.VMEM((1024, LANES), F32), pltpu.VMEM((LANES, LANES), F32)]


def level_kernel(terms, coupling, x_out, y_out, top_out, cols, rows):
    half = lax.axis_index("group") // 2
    inverse = invert(coupling[half] + load_symmetric(terms, 0), cols, rows)
    cross = load_square(terms, 384)
    x = dot_full(inverse, cross)
    y = dot_full(inverse, load_square(terms, 896))
    x_out[...] = x
    y_out[...] = y
    store_symmetric(top_out, 0, load_symmetric(terms, 1408) - dot_t_full(cross, x))
    store_square(top_out, 384, load_square(terms, 1792) - dot_t_full(cross, y))


def level_solve(terms, coupling):
    square = jax.ShapeDtypeStruct((R, R), F32)
    return pl.pallas_call(
        level_kernel,
        out_shape=(square, square, jax.ShapeDtypeStruct((TOP, LANES), F32)),
        scratch_shapes=SCRATCH,
        compiler_params=pltpu.CompilerParams(vmem_limit_bytes=VMEM_LIMIT),
        name="level_solve",
    )(terms, coupling)


def root_kernel(top, coupling, x, y, w_out, z_out, cols, rows):
    inverse = invert(coupling[...] + load_symmetric(top, 0), cols, rows)
    w = dot_full(inverse, load_square(top, 384))
    w_out[...] = w
    z_out[...] = y[...] - dot_full(x[...], w)


def root_solve(top, coupling, x, y):
    square = jax.ShapeDtypeStruct((R, R), F32)
    return pl.pallas_call(
        root_kernel,
        out_shape=(square, square),
        scratch_shapes=SCRATCH,
        compiler_params=pltpu.CompilerParams(vmem_limit_bytes=VMEM_LIMIT),
        name="root_solve",
    )(top, coupling, x, y)


def dot_three(lh, ll, rh, rl):
    return dot(lh, rh) + (dot(lh, rl) + dot(ll, rh))


def panel_kernel(q_two, q_one, x, out):
    out[...] = q_one[...] - dot_three(*split2(q_two[...]), *split2(x[...]))


def field_kernel(q_two, q_one, sources, w, z, out):
    change = dot_three(*split2(q_one[...]), *split2(w[...]))
    change += dot_three(*split2(q_two[...]), *split2(z[...]))
    out[...] = sources[...] - change


def update(kernel, tall, square, name):
    rows = tall[0].shape[0]
    spec = pl.BlockSpec((TILE, R), lambda i: (i, 0))
    whole = pl.BlockSpec((R, R), lambda i: (0, 0))
    return pl.pallas_call(
        kernel,
        grid=(rows // TILE,),
        in_specs=[spec] * len(tall) + [whole] * len(square),
        out_specs=spec,
        out_shape=jax.ShapeDtypeStruct((rows, R), F32),
        compiler_params=pltpu.CompilerParams(vmem_limit_bytes=VMEM_LIMIT),
        name=name,
    )(*tall, *square)


def exchange(x, mask):
    count = lax.axis_size(AXES)
    return lax.ppermute(x, AXES, [(i, i ^ mask) for i in range(count)])


def code_of(index, bits):
    code = 0
    for place, bit in enumerate(bits):
        code = code | ((index >> bit) & 1) << place
    return code


def mask_of(code, bits):
    return sum(1 << bit for place, bit in enumerate(bits) if code >> place & 1)


def reduce_scatter(x, index, bits):
    count = 1 << len(bits)
    mine = code_of(index, bits)
    parts = x.reshape(count, x.shape[0] // count, x.shape[1])
    got = lax.dynamic_index_in_dim(parts, mine, 0, keepdims=False)
    arrived = []
    for other in range(1, count):
        part = lax.dynamic_index_in_dim(parts, mine ^ other, 0, keepdims=False)
        arrived.append(exchange(part, mask_of(other, bits)))
    for part in arrived:
        got = got + part
    return got


def all_gather(x, index, bits):
    count = 1 << len(bits)
    mine = code_of(index, bits)
    pieces = [x] + [exchange(x, mask_of(other, bits)) for other in range(1, count)]
    out = jnp.zeros((count,) + x.shape, x.dtype)
    for other, piece in enumerate(pieces):
        out = lax.dynamic_update_index_in_dim(out, piece, mine ^ other, 0)
    return out.reshape(count * x.shape[0], x.shape[1])


def scatter_leaf(x):
    count = lax.axis_size("leaf")
    parts = x.reshape(count, x.shape[0] // count, x.shape[1])
    return jnp.sum(lax.all_to_all(parts, "leaf", 0, 0), axis=0)


def gather_leaf(x):
    count = lax.axis_size("leaf")
    parts = jnp.broadcast_to(x[None], (count,) + x.shape)
    return lax.all_to_all(parts, "leaf", 0, 0).reshape(count * x.shape[0], x.shape[1])


def per_device(q_two, q_one, sources, coupling_two, coupling_one):
    index = lax.axis_index(AXES)
    terms = gram_terms(q_two, q_one, sources)
    terms = reduce_scatter(terms, index, [0])
    terms = gather_leaf(scatter_leaf(terms))
    terms = all_gather(terms, index, [0])
    x, y, top = level_solve(terms, coupling_two)
    mine = index & 1
    parts = top.reshape(2, TOP // 2, LANES)
    part = lax.dynamic_index_in_dim(parts, mine, 0, keepdims=False)
    part = part + exchange(part, 2)
    top = all_gather(part, index, [0])
    panel_one = update(panel_kernel, [q_two, q_one], [x], "panel")
    w, z = root_solve(top, coupling_one, x, y)
    solution = update(field_kernel, [q_two, q_one, sources], [w, z], "field")
    return (panel_one, solution)


def solution(mesh):
    placed = P(("group", "leaf"), None)
    return jax.shard_map(
        per_device,
        mesh=mesh,
        in_specs=(placed, placed, placed, P(), P()),
        out_specs=(placed, placed),
        check_vma=False,
    )
```

```python
import functools

import jax
import jax.numpy as jnp
from jax import lax
from jax.experimental import pallas as pl
from jax.experimental.pallas import tpu as pltpu
from jax.sharding import PartitionSpec as P

HIGH = lax.Precision.HIGHEST
AXES = ("leaf", "group")
F32 = jnp.float32
BF16 = jnp.bfloat16
R = 256
LANES = 128
PANEL = 32
TILE = 512
VMEM_LIMIT = 40 * 1024 * 1024


def split2(x):
    high = x.astype(BF16)
    return high, (x - high.astype(F32)).astype(BF16)


def split3(x):
    high = x.astype(BF16)
    rest = x - high.astype(F32)
    mid = rest.astype(BF16)
    return high, mid, (rest - mid.astype(F32)).astype(BF16)


def dot(left, right):
    return jnp.dot(left, right, preferred_element_type=F32)


def dot_t(left, right):
    return lax.dot_general(left, right, (((0,), (0,)), ((), ())), preferred_element_type=F32)


def dot_full(left, right):
    return jnp.dot(left, right, precision=HIGH, preferred_element_type=F32)


def dot_t_full(left, right):
    return lax.dot_general(
        left, right, (((0,), (0,)), ((), ())), precision=HIGH, preferred_element_type=F32
    )


def store_symmetric(ref, row, block):
    ref[row : row + 128, :] = block[:128, :128]
    ref[row + 128 : row + 256, :] = block[128:, :128]
    ref[row + 256 : row + 384, :] = block[128:, 128:]


def store_square(ref, row, block):
    ref[row : row + 256, :] = block[:, :128]
    ref[row + 256 : row + 512, :] = block[:, 128:]


def load_symmetric(ref, row):
    lower = ref[row + 128 : row + 256, :]
    top = jnp.concatenate([ref[row : row + 128, :], lower.T], axis=1)
    bottom = jnp.concatenate([lower, ref[row + 256 : row + 384, :]], axis=1)
    return jnp.concatenate([top, bottom], axis=0)


def load_square(ref, row):
    return jnp.concatenate([ref[row : row + 256, :], ref[row + 256 : row + 512, :]], axis=1)


def zero_first(acc):
    @pl.when(pl.program_id(0) == 0)
    def _():
        acc[...] = jnp.zeros_like(acc)


def at_last(body):
    pl.when(pl.program_id(0) == pl.num_programs(0) - 1)(body)


def own_gram_kernel(q_two, out, acc):
    zero_first(acc)
    h2, l2 = split2(q_two[...])
    acc[0] += dot_t(h2, h2)
    acc[1] += dot_t(h2, l2)

    @at_last
    def _():
        low = acc[1]
        store_symmetric(out, 0, acc[0] + low + low.T)


def cross_gram_kernel(q_two, q_one, out, acc):
    zero_first(acc)
    h2, l2 = split2(q_two[...])
    h1, l1 = split2(q_one[...])
    acc[0] += dot_t(h2, h1) + dot_t(h2, l1) + dot_t(l2, h1)
    acc[1] += dot_t(h1, h1)
    acc[2] += dot_t(h1, l1)

    @at_last
    def _():
        store_square(out, 0, acc[0])
        low = acc[2]
        store_symmetric(out, 512, acc[1] + low + low.T)


def source_gram_kernel(q_two, q_one, sources, out, acc):
    zero_first(acc)
    h2, l2 = split2(q_two[...])
    h1, l1 = split2(q_one[...])
    hs, ls = split2(sources[...])
    acc[0] += dot_t(h2, hs) + dot_t(h2, ls) + dot_t(l2, hs)
    acc[1] += dot_t(h1, hs) + dot_t(h1, ls) + dot_t(l1, hs)

    @at_last
    def _():
        store_square(out, 0, acc[0])
        store_square(out, 512, acc[1])


def estimate(passes, rows, arrays):
    return pl.CostEstimate(
        flops=2 * passes * rows * R * R, bytes_accessed=4 * arrays * rows * R, transcendentals=0
    )


def gram(kernel, tall, blocks, passes, packed, name):
    rows = tall[0].shape[0]
    spec = pl.BlockSpec((TILE, R), lambda i: (i, 0))
    return pl.pallas_call(
        kernel,
        grid=(rows // TILE,),
        in_specs=[spec] * len(tall),
        out_specs=pl.BlockSpec((packed, LANES), lambda i: (0, 0)),
        out_shape=jax.ShapeDtypeStruct((packed, LANES), F32),
        scratch_shapes=[pltpu.VMEM((blocks, R, R), F32)],
        compiler_params=pltpu.CompilerParams(vmem_limit_bytes=VMEM_LIMIT),
        cost_estimate=estimate(passes, rows, len(tall)),
        name=name,
    )(*tall)


def spread_lane(x, lane):
    return jnp.broadcast_to(x[:, lane : lane + 1], (8, LANES))


def eliminate(block, cols, rows):
    lane = lax.broadcasted_iota(jnp.int32, (8, LANES), 1)
    sub = lax.broadcasted_iota(jnp.int32, (8, LANES), 0)
    count = len(block)
    for t in range(count):
        own = [spread_lane(block[t], 8 * t + j) for j in range(8)]
        for j in range(8):
            cols[64 * t + 8 * j : 64 * t + 8 * j + 8, :] = own[j]
        rows[8 * t : 8 * t + 8, :] = block[t]
        entry = {}
        for i in range(8):
            for j in range(i + 1):
                at = 64 * t + 8 * j + i
                entry[i, j] = jnp.broadcast_to(cols[at : at + 1, :], (8, LANES))
        entry = sweep_small(entry)
        inverse = lambda i, j: entry[max(i, j), min(i, j)]
        inside = (lane >= 8 * t) & (lane < 8 * t + 8)
        old = []
        for j in range(8):
            row = jnp.broadcast_to(rows[8 * t + j : 8 * t + j + 1, :], (8, LANES))
            old.append(jnp.where(inside, jnp.where(lane == 8 * t + j, 1.0, 0.0), row))
        new = [tree_sum([inverse(i, j) * old[j] for j in range(8)]) for i in range(8)]
        for g in range(count):
            if g == t:
                continue
            base = jnp.where(inside, 0.0, block[g])
            terms = [spread_lane(block[g], 8 * t + j) * new[j] for j in range(8)]
            block[g] = base - tree_sum(terms)
        merged = new[0]
        for j in range(1, 8):
            merged = jnp.where(sub == j, new[j], merged)
        block[t] = merged
    return block


def tree_sum(terms):
    while len(terms) > 1:
        terms = [
            terms[i] + terms[i + 1] if i + 1 < len(terms) else terms[i]
            for i in range(0, len(terms), 2)
        ]
    return terms[0]


def sweep_small(entry):
    entry = dict(entry)
    get = lambda i, j: entry[max(i, j), min(i, j)]
    for k in range(0, 8, 2):
        a, b, c = get(k, k), get(k + 1, k), get(k + 1, k + 1)
        inv = pl.reciprocal(a * c - b * b, approx=True)
        e, f, g = c * inv, b * inv, a * inv
        others = [i for i in range(8) if i not in (k, k + 1)]
        left = {i: (get(i, k), get(i, k + 1)) for i in others}
        swept = {i: (e * u - f * v, g * v - f * u) for i, (u, v) in left.items()}
        for i in others:
            for j in others:
                if j <= i:
                    u, v = left[i]
                    m, n = swept[j]
                    entry[i, j] = entry[i, j] - (u * m + v * n)
        for i in others:
            entry[max(i, k), min(i, k)] = swept[i][0]
            entry[max(i, k + 1), min(i, k + 1)] = swept[i][1]
        entry[k, k], entry[k + 1, k], entry[k + 1, k + 1] = -e, f, -g
    return {key: -value for key, value in entry.items()}


def invert_half(matrix, cols, rows):
    block = eliminate([matrix[8 * i : 8 * i + 8, :] for i in range(LANES // 8)], cols, rows)
    return jnp.concatenate(block, axis=0)


SQUARE = jax.ShapeDtypeStruct((R, R), F32)
CORNER = jax.ShapeDtypeStruct((LANES, LANES), F32)


def call(kernel, out_shape, args, name, scratch=(), flops=0):
    return pl.pallas_call(
        kernel,
        out_shape=out_shape,
        scratch_shapes=list(scratch),
        compiler_params=pltpu.CompilerParams(vmem_limit_bytes=VMEM_LIMIT),
        cost_estimate=pl.CostEstimate(flops=flops, bytes_accessed=R * R * 4, transcendentals=0),
        name=name,
    )(*args)


def first_kernel(which, gram_ref, coupling, first_out, across_out, rest_out, row_out, col_out, cols, rows):
    matrix = coupling[which()] + load_symmetric(gram_ref, 0)
    eye = lax.broadcasted_iota(jnp.int32, (R, R), 0) == lax.broadcasted_iota(jnp.int32, (R, R), 1)
    diagonal = jnp.where(eye, matrix, 0.0)
    scale_row = lax.rsqrt(jnp.sum(diagonal, axis=0, keepdims=True))
    scale_col = lax.rsqrt(jnp.sum(diagonal, axis=1, keepdims=True))
    matrix = matrix * scale_col * scale_row
    side = matrix[:LANES, LANES:]
    first = invert_half(matrix[:LANES, :LANES], cols, rows)
    across = dot_full(first, side)
    first_out[...] = first
    across_out[...] = across
    rest_out[...] = matrix[LANES:, LANES:] - dot_t_full(side, across)
    row_out[...] = jnp.broadcast_to(scale_row, (8, R))
    col_out[...] = jnp.broadcast_to(scale_col, (R, LANES))


def second_kernel(first, across, rest, row, col, out, cols, rows):
    second = invert_half(rest[...], cols, rows)
    corner = -dot_full(across[...], second)
    top = first[...] - dot_full(corner, across[...].T)
    out[:LANES, :LANES] = top * col[:LANES, :] * row[:1, :LANES]
    out[:LANES, LANES:] = corner * col[:LANES, :] * row[:1, LANES:]
    out[LANES:, :LANES] = corner.T * col[LANES:, :] * row[:1, :LANES]
    out[LANES:, LANES:] = second * col[LANES:, :] * row[:1, LANES:]


SCRATCH = [pltpu.VMEM((1024, LANES), F32), pltpu.VMEM((LANES, LANES), F32)]
HALF_FLOPS = 5_000_000_000


def invert_first(which, packed, coupling, name):
    shapes = (
        CORNER,
        CORNER,
        CORNER,
        jax.ShapeDtypeStruct((8, R), F32),
        jax.ShapeDtypeStruct((R, LANES), F32),
    )
    kernel = functools.partial(first_kernel, which)
    return call(kernel, shapes, (packed, coupling), name, SCRATCH, HALF_FLOPS)


def invert_second(parts, name):
    return call(second_kernel, SQUARE, parts, name, SCRATCH, HALF_FLOPS)


def half_index():
    return lax.axis_index("group") // 2


def no_index():
    return 0


def panel_solve_kernel(inverse, terms, x_out, root_out):
    cross = load_square(terms, 0)
    x = dot_full(inverse[...], cross)
    x_out[...] = x
    store_symmetric(root_out, 0, load_symmetric(terms, 512) - dot_t_full(cross, x))


def source_solve_kernel(inverse, x, terms, y_out, side_out):
    projected = load_square(terms, 0)
    y_out[...] = dot_full(inverse[...], projected)
    store_square(side_out, 0, load_square(terms, 512) - dot_t_full(x[...], projected))


def dot_three(lh, ll, rh, rl):
    return dot(lh, rh) + (dot(lh, rl) + dot(ll, rh))


def panel_kernel(q_two, q_one, x, out):
    out[...] = q_one[...] - dot_three(*split2(q_two[...]), *split2(x[...]))


def field_kernel(q_two, q_one, sources, inverse, side, x, y, out, w_ref, z_ref):
    @pl.when(pl.program_id(0) == 0)
    def _():
        w = dot_full(inverse[...], load_square(side, 0))
        w_ref[...] = w
        z_ref[...] = y[...] - dot_full(x[...], w)

    change = dot_three(*split2(q_one[...]), *split2(w_ref[...]))
    change += dot_three(*split2(q_two[...]), *split2(z_ref[...]))
    out[...] = sources[...] - change


def update(kernel, tall, small, passes, name, scratch=()):
    rows = tall[0].shape[0]
    spec = pl.BlockSpec((TILE, R), lambda i: (i, 0))
    return pl.pallas_call(
        kernel,
        grid=(rows // TILE,),
        in_specs=[spec] * len(tall) + [pl.BlockSpec(x.shape, lambda i: (0, 0)) for x in small],
        out_specs=spec,
        out_shape=jax.ShapeDtypeStruct((rows, R), F32),
        scratch_shapes=list(scratch),
        compiler_params=pltpu.CompilerParams(vmem_limit_bytes=VMEM_LIMIT),
        cost_estimate=estimate(passes, rows, len(tall) + 1),
        name=name,
    )(*tall, *small)


def exchange(x, mask):
    count = lax.axis_size(AXES)
    return lax.ppermute(x, AXES, [(i, i ^ mask) for i in range(count)])


def code_of(index, bits):
    code = 0
    for place, bit in enumerate(bits):
        code = code | ((index >> bit) & 1) << place
    return code


def mask_of(code, bits):
    return sum(1 << bit for place, bit in enumerate(bits) if code >> place & 1)


def reduce_scatter(x, index, bits):
    count = 1 << len(bits)
    mine = code_of(index, bits)
    parts = x.reshape(count, x.shape[0] // count, x.shape[1])
    got = lax.dynamic_index_in_dim(parts, mine, 0, keepdims=False)
    arrived = []
    for other in range(1, count):
        part = lax.dynamic_index_in_dim(parts, mine ^ other, 0, keepdims=False)
        arrived.append(exchange(part, mask_of(other, bits)))
    for part in arrived:
        got = got + part
    return got


def all_gather(x, index, bits):
    count = 1 << len(bits)
    mine = code_of(index, bits)
    pieces = [x] + [exchange(x, mask_of(other, bits)) for other in range(1, count)]
    if count == 2:
        low = jnp.where(mine == 0, pieces[0], pieces[1])
        high = jnp.where(mine == 0, pieces[1], pieces[0])
        return jnp.concatenate([low, high], axis=0)
    out = jnp.zeros((count,) + x.shape, x.dtype)
    for other, piece in enumerate(pieces):
        out = lax.dynamic_update_index_in_dim(out, piece, mine ^ other, 0)
    return out.reshape(count * x.shape[0], x.shape[1])


def all_sum(x, bits):
    count = 1 << len(bits)
    arrived = [exchange(x, mask_of(other, bits)) for other in range(1, count)]
    for part in arrived:
        x = x + part
    return x


def per_device(q_two, q_one, sources, coupling_two, coupling_one):
    index = lax.axis_index(AXES)
    leaf_end = lax.axis_size("leaf").bit_length() + 1
    outer = [list(range(low, min(low + 2, leaf_end))) for low in range(3, leaf_end, 2)]
    own = gram(own_gram_kernel, [q_two], 2, 2, 384, "own_gram")
    crossing = gram(cross_gram_kernel, [q_two, q_one], 3, 5, 896, "cross_gram")
    source = gram(source_gram_kernel, [q_two, q_one, sources], 2, 6, 1024, "source_gram")

    own = reduce_scatter(reduce_scatter(own, index, [0]), index, [2])
    for bits in outer:
        own = all_sum(own, bits)
    own = all_gather(all_gather(own, index, [2]), index, [0])

    stages = [[0], [2]] + outer

    def whole_sum(terms):
        for bits in stages:
            terms = reduce_scatter(terms, index, bits)
        for bits in reversed(stages):
            terms = all_gather(terms, index, bits)
        return terms

    crossing = whole_sum(crossing)
    source = whole_sum(source)

    def across_halves(terms):
        mine = index & 1
        parts = terms.reshape(2, terms.shape[0] // 2, LANES)
        part = lax.dynamic_index_in_dim(parts, mine, 0, keepdims=False)
        return all_gather(part + exchange(part, 2), index, [0])

    parts = invert_first(half_index, own, coupling_two, "level_first")
    inverse = invert_second(parts, "level_second")
    x, root = call(
        panel_solve_kernel, (SQUARE, jax.ShapeDtypeStruct((384, LANES), F32)), (inverse, crossing), "panel_solve"
    )
    root = across_halves(root)
    panel_one = update(panel_kernel, [q_two, q_one], [x], 3, "panel")
    y, side = call(
        source_solve_kernel, (SQUARE, jax.ShapeDtypeStruct((512, LANES), F32)), (inverse, x, source), "source_solve"
    )
    side = across_halves(side)
    parts = invert_first(no_index, root, coupling_one[None], "root_first")
    inverse = invert_second(parts, "root_second")
    solution = update(
        field_kernel,
        [q_two, q_one, sources],
        [inverse, side, x, y],
        6,
        "field",
        [pltpu.VMEM((R, R), F32), pltpu.VMEM((R, R), F32)],
    )
    return (panel_one, solution)


def solution(mesh):
    placed = P(("group", "leaf"), None)
    return jax.shard_map(
        per_device,
        mesh=mesh,
        in_specs=(placed, placed, placed, P(), P()),
        out_specs=(placed, placed),
        check_vma=False,
    )
```

```python
import functools

import jax
import jax.numpy as jnp
from jax import lax
from jax.experimental import pallas as pl
from jax.experimental.pallas import tpu as pltpu
from jax.sharding import PartitionSpec as P

HIGH = lax.Precision.HIGHEST
AXES = ("leaf", "group")
F32 = jnp.float32
BF16 = jnp.bfloat16
R = 256
LANES = 128
TILE = 512
VMEM_LIMIT = 40 * 1024 * 1024
OWN, CROSS, PROJECTED, ROOT, SIDE, TERMS = 0, 384, 896, 1408, 1792, 2304


def split2(x):
    high = x.astype(BF16)
    return high, (x - high.astype(F32)).astype(BF16)


def split3(x):
    high = x.astype(BF16)
    rest = x - high.astype(F32)
    mid = rest.astype(BF16)
    return high, mid, (rest - mid.astype(F32)).astype(BF16)


def dot(left, right):
    return jnp.dot(left, right, preferred_element_type=F32)


def dot_t(left, right):
    return lax.dot_general(left, right, (((0,), (0,)), ((), ())), preferred_element_type=F32)


def dot_full(left, right):
    return jnp.dot(left, right, precision=HIGH, preferred_element_type=F32)


def dot_t_full(left, right):
    return lax.dot_general(
        left, right, (((0,), (0,)), ((), ())), precision=HIGH, preferred_element_type=F32
    )


def store_symmetric(ref, row, block):
    ref[row : row + 128, :] = block[:128, :128]
    ref[row + 128 : row + 256, :] = block[128:, :128]
    ref[row + 256 : row + 384, :] = block[128:, 128:]


def store_square(ref, row, block):
    ref[row : row + 256, :] = block[:, :128]
    ref[row + 256 : row + 512, :] = block[:, 128:]


def load_symmetric(ref, row):
    lower = ref[row + 128 : row + 256, :]
    top = jnp.concatenate([ref[row : row + 128, :], lower.T], axis=1)
    bottom = jnp.concatenate([lower, ref[row + 256 : row + 384, :]], axis=1)
    return jnp.concatenate([top, bottom], axis=0)


def load_square(ref, row):
    return jnp.concatenate([ref[row : row + 256, :], ref[row + 256 : row + 512, :]], axis=1)


def gram_kernel(q_two, q_one, sources, keep, send, b2, b1, bs, acc, packed, sems):
    tiles = b2.shape[0] // TILE
    pairs = ((q_two, b2), (q_one, b1), (sources, bs))

    def copy(tile, which):
        here = pl.ds(tile * TILE, TILE)
        source, target = pairs[which]
        return pltpu.make_async_copy(source.at[here], target.at[here], sems.at[which, tile])

    for tile in range(tiles):
        for which in range(3):
            copy(tile, which).start()
    acc[...] = jnp.zeros_like(acc)

    def step(tile, carry):
        for which in range(3):
            copy(tile, which).wait()
        here = pl.ds(pl.multiple_of(tile * TILE, TILE), TILE)
        h2, l2 = split2(b2[here, :])
        h1, l1 = split2(b1[here, :])
        hs, ls = split2(bs[here, :])
        acc[0] += dot_t(h2, h2)
        acc[1] += dot_t(h2, l2)
        acc[2] += dot_t(h2, h1) + dot_t(h2, l1) + dot_t(l2, h1)
        acc[3] += dot_t(h2, hs) + dot_t(h2, ls) + dot_t(l2, hs)
        acc[4] += dot_t(h1, h1)
        acc[5] += dot_t(h1, l1)
        acc[6] += dot_t(h1, hs) + dot_t(h1, ls) + dot_t(l1, hs)
        return carry

    lax.fori_loop(0, tiles, step, 0)
    low = acc[1]
    store_symmetric(packed, OWN, acc[0] + low + low.T)
    store_square(packed, CROSS, acc[2])
    store_square(packed, PROJECTED, acc[3])
    low = acc[5]
    store_symmetric(packed, ROOT, acc[4] + low + low.T)
    store_square(packed, SIDE, acc[6])
    mine = lax.rem(lax.axis_index("group"), 2)
    half = TERMS // 2
    keep[...] = packed[pl.ds(pl.multiple_of(mine * half, 8), half), :]
    send[...] = packed[pl.ds(pl.multiple_of((1 - mine) * half, 8), half), :]


def gram(q_two, q_one, sources):
    rows = q_two.shape[0]
    part = jax.ShapeDtypeStruct((TERMS // 2, LANES), F32)
    return pl.pallas_call(
        gram_kernel,
        in_specs=[pl.BlockSpec(memory_space=pl.ANY)] * 3,
        out_shape=(part, part),
        scratch_shapes=[
            pltpu.VMEM((rows, R), F32),
            pltpu.VMEM((rows, R), F32),
            pltpu.VMEM((rows, R), F32),
            pltpu.VMEM((7, R, R), F32),
            pltpu.VMEM((TERMS, LANES), F32),
            pltpu.SemaphoreType.DMA((3, rows // TILE)),
        ],
        compiler_params=pltpu.CompilerParams(vmem_limit_bytes=60 * 1024 * 1024),
        cost_estimate=estimate(13, rows, 3),
        name="gram",
    )(q_two, q_one, sources)


def estimate(passes, rows, arrays):
    return pl.CostEstimate(
        flops=2 * passes * rows * R * R, bytes_accessed=4 * arrays * rows * R, transcendentals=0
    )


def spread_lane(x, lane):
    return jnp.broadcast_to(x[:, lane : lane + 1], (8, LANES))


def eliminate(block, cols, rows):
    lane = lax.broadcasted_iota(jnp.int32, (8, LANES), 1)
    sub = lax.broadcasted_iota(jnp.int32, (8, LANES), 0)
    count = len(block)
    for t in range(count):
        own = [spread_lane(block[t], 8 * t + j) for j in range(8)]
        for j in range(8):
            cols[64 * t + 8 * j : 64 * t + 8 * j + 8, :] = own[j]
        rows[8 * t : 8 * t + 8, :] = block[t]
        entry = {}
        for i in range(8):
            for j in range(i + 1):
                at = 64 * t + 8 * j + i
                entry[i, j] = jnp.broadcast_to(cols[at : at + 1, :], (8, LANES))
        entry = sweep_small(entry)
        inverse = lambda i, j: entry[max(i, j), min(i, j)]
        inside = (lane >= 8 * t) & (lane < 8 * t + 8)
        old = []
        for j in range(8):
            row = jnp.broadcast_to(rows[8 * t + j : 8 * t + j + 1, :], (8, LANES))
            old.append(jnp.where(inside, jnp.where(lane == 8 * t + j, 1.0, 0.0), row))
        new = [tree_sum([inverse(i, j) * old[j] for j in range(8)]) for i in range(8)]
        for g in range(count):
            if g == t:
                continue
            base = jnp.where(inside, 0.0, block[g])
            terms = [spread_lane(block[g], 8 * t + j) * new[j] for j in range(8)]
            block[g] = base - tree_sum(terms)
        merged = new[0]
        for j in range(1, 8):
            merged = jnp.where(sub == j, new[j], merged)
        block[t] = merged
    return block


def tree_sum(terms):
    while len(terms) > 1:
        terms = [
            terms[i] + terms[i + 1] if i + 1 < len(terms) else terms[i]
            for i in range(0, len(terms), 2)
        ]
    return terms[0]


def sweep_small(entry):
    entry = dict(entry)
    get = lambda i, j: entry[max(i, j), min(i, j)]
    for k in range(0, 8, 2):
        a, b, c = get(k, k), get(k + 1, k), get(k + 1, k + 1)
        inv = pl.reciprocal(a * c - b * b, approx=True)
        e, f, g = c * inv, b * inv, a * inv
        others = [i for i in range(8) if i not in (k, k + 1)]
        left = {i: (get(i, k), get(i, k + 1)) for i in others}
        swept = {i: (e * u - f * v, g * v - f * u) for i, (u, v) in left.items()}
        for i in others:
            for j in others:
                if j <= i:
                    u, v = left[i]
                    m, n = swept[j]
                    entry[i, j] = entry[i, j] - (u * m + v * n)
        for i in others:
            entry[max(i, k), min(i, k)] = swept[i][0]
            entry[max(i, k + 1), min(i, k + 1)] = swept[i][1]
        entry[k, k], entry[k + 1, k], entry[k + 1, k + 1] = -e, f, -g
    return {key: -value for key, value in entry.items()}


def invert_half(matrix, cols, rows):
    block = eliminate([matrix[8 * i : 8 * i + 8, :] for i in range(LANES // 8)], cols, rows)
    return jnp.concatenate(block, axis=0)


SQUARE = jax.ShapeDtypeStruct((R, R), F32)
CORNER = jax.ShapeDtypeStruct((LANES, LANES), F32)


def call(kernel, out_shape, args, name, scratch=(), flops=0):
    return pl.pallas_call(
        kernel,
        out_shape=out_shape,
        scratch_shapes=list(scratch),
        compiler_params=pltpu.CompilerParams(vmem_limit_bytes=VMEM_LIMIT),
        cost_estimate=pl.CostEstimate(flops=flops, bytes_accessed=R * R * 4, transcendentals=0),
        name=name,
    )(*args)


def first_kernel(which, gram_ref, coupling, first_out, across_out, rest_out, row_out, col_out, cols, rows):
    matrix = coupling[which()] + load_symmetric(gram_ref, OWN)
    eye = lax.broadcasted_iota(jnp.int32, (R, R), 0) == lax.broadcasted_iota(jnp.int32, (R, R), 1)
    diagonal = jnp.where(eye, matrix, 0.0)
    scale_row = lax.rsqrt(jnp.sum(diagonal, axis=0, keepdims=True))
    scale_col = lax.rsqrt(jnp.sum(diagonal, axis=1, keepdims=True))
    matrix = matrix * scale_col * scale_row
    side = matrix[:LANES, LANES:]
    first = invert_half(matrix[:LANES, :LANES], cols, rows)
    across = dot_full(first, side)
    first_out[...] = first
    across_out[...] = across
    rest_out[...] = matrix[LANES:, LANES:] - dot_t_full(side, across)
    row_out[...] = jnp.broadcast_to(scale_row, (8, R))
    col_out[...] = jnp.broadcast_to(scale_col, (R, LANES))


def second_kernel(first, across, rest, row, col, out, cols, rows):
    second = invert_half(rest[...], cols, rows)
    corner = -dot_full(across[...], second)
    top = first[...] - dot_full(corner, across[...].T)
    out[:LANES, :LANES] = top * col[:LANES, :] * row[:1, :LANES]
    out[:LANES, LANES:] = corner * col[:LANES, :] * row[:1, LANES:]
    out[LANES:, :LANES] = corner.T * col[LANES:, :] * row[:1, :LANES]
    out[LANES:, LANES:] = second * col[LANES:, :] * row[:1, LANES:]


SCRATCH = [pltpu.VMEM((1024, LANES), F32), pltpu.VMEM((LANES, LANES), F32)]
HALF_FLOPS = 5_000_000_000


def invert_first(which, packed, coupling, name):
    shapes = (
        CORNER,
        CORNER,
        CORNER,
        jax.ShapeDtypeStruct((8, R), F32),
        jax.ShapeDtypeStruct((R, LANES), F32),
    )
    kernel = functools.partial(first_kernel, which)
    return call(kernel, shapes, (packed, coupling), name, SCRATCH, HALF_FLOPS)


def invert_second(parts, name):
    return call(second_kernel, SQUARE, parts, name, SCRATCH, HALF_FLOPS)


def half_index():
    return lax.axis_index("group") // 2


def no_index():
    return 0


def panel_solve_kernel(inverse, terms, x_out, root_out):
    cross = load_square(terms, CROSS)
    x = dot_full(inverse[...], cross)
    x_out[...] = x
    store_symmetric(root_out, 0, load_symmetric(terms, ROOT) - dot_t_full(cross, x))


def source_solve_kernel(inverse, x, terms, y_out, side_out):
    projected = load_square(terms, PROJECTED)
    y_out[...] = dot_full(inverse[...], projected)
    store_square(side_out, 0, load_square(terms, SIDE) - dot_t_full(x[...], projected))


def dot_three(lh, ll, rh, rl):
    return dot(lh, rh) + (dot(lh, rl) + dot(ll, rh))


def panel_kernel(q_two, q_one, x, out):
    out[...] = q_one[...] - dot_three(*split2(q_two[...]), *split2(x[...]))


def field_kernel(q_two, q_one, sources, inverse, side, x, y, out, w_ref, z_ref):
    @pl.when(pl.program_id(0) == 0)
    def _():
        w = dot_full(inverse[...], load_square(side, 0))
        w_ref[...] = w
        z_ref[...] = y[...] - dot_full(x[...], w)

    change = dot_three(*split2(q_one[...]), *split2(w_ref[...]))
    change += dot_three(*split2(q_two[...]), *split2(z_ref[...]))
    out[...] = sources[...] - change


def update(kernel, tall, small, passes, name, scratch=()):
    rows = tall[0].shape[0]
    spec = pl.BlockSpec((TILE, R), lambda i: (i, 0))
    return pl.pallas_call(
        kernel,
        grid=(rows // TILE,),
        in_specs=[spec] * len(tall) + [pl.BlockSpec(x.shape, lambda i: (0, 0)) for x in small],
        out_specs=spec,
        out_shape=jax.ShapeDtypeStruct((rows, R), F32),
        scratch_shapes=list(scratch),
        compiler_params=pltpu.CompilerParams(vmem_limit_bytes=VMEM_LIMIT),
        cost_estimate=estimate(passes, rows, len(tall) + 1),
        name=name,
    )(*tall, *small)


def exchange(x, mask):
    count = lax.axis_size(AXES)
    return lax.ppermute(x, AXES, [(i, i ^ mask) for i in range(count)])


def scatter_sum(x, index, bit):
    mine = (index >> bit) & 1
    parts = x.reshape(2, x.shape[0] // 2, x.shape[1])
    sent = lax.dynamic_index_in_dim(parts, 1 - mine, 0, keepdims=False)
    kept = lax.dynamic_index_in_dim(parts, mine, 0, keepdims=False)
    return kept + exchange(sent, 1 << bit)


def gather(x, index, bit):
    mine = (index >> bit) & 1
    other = exchange(x, 1 << bit)
    low = jnp.where(mine == 0, x, other)
    high = jnp.where(mine == 0, other, x)
    return jnp.concatenate([low, high], axis=0)


def per_device(q_two, q_one, sources, coupling_two, coupling_one):
    index = lax.axis_index(AXES)
    leaf_bits = list(range(2, lax.axis_size("leaf").bit_length() + 1))
    orders = (leaf_bits, leaf_bits[1:] + leaf_bits[:1])
    keep, send = gram(q_two, q_one, sources)
    terms = keep + exchange(send, 1)
    parts = [terms[: TERMS // 4], terms[TERMS // 4 :]]
    for step in range(len(leaf_bits)):
        parts = [scatter_sum(x, index, order[step]) for x, order in zip(parts, orders)]
    for step in reversed(range(len(leaf_bits))):
        parts = [gather(x, index, order[step]) for x, order in zip(parts, orders)]
    terms = gather(jnp.concatenate(parts, axis=0), index, 0)

    def across_halves(terms):
        mine = index & 1
        parts = terms.reshape(2, terms.shape[0] // 2, LANES)
        part = lax.dynamic_index_in_dim(parts, mine, 0, keepdims=False)
        return gather(part + exchange(part, 2), index, 0)

    parts = invert_first(half_index, terms, coupling_two, "level_first")
    inverse = invert_second(parts, "level_second")
    x, root = call(
        panel_solve_kernel, (SQUARE, jax.ShapeDtypeStruct((384, LANES), F32)), (inverse, terms), "panel_solve"
    )
    root = across_halves(root)
    panel_one = update(panel_kernel, [q_two, q_one], [x], 3, "panel")
    y, side = call(
        source_solve_kernel, (SQUARE, jax.ShapeDtypeStruct((512, LANES), F32)), (inverse, x, terms), "source_solve"
    )
    side = across_halves(side)
    parts = invert_first(no_index, root, coupling_one[None], "root_first")
    inverse = invert_second(parts, "root_second")
    solution = update(
        field_kernel,
        [q_two, q_one, sources],
        [inverse, side, x, y],
        6,
        "field",
        [pltpu.VMEM((R, R), F32), pltpu.VMEM((R, R), F32)],
    )
    return (panel_one, solution)


def solution(mesh):
    placed = P(("group", "leaf"), None)
    return jax.shard_map(
        per_device,
        mesh=mesh,
        in_specs=(placed, placed, placed, P(), P()),
        out_specs=(placed, placed),
        check_vma=False,
    )
```

```python
import functools

import jax
import jax.numpy as jnp
from jax import lax
from jax.experimental import pallas as pl
from jax.experimental.pallas import tpu as pltpu
from jax.sharding import PartitionSpec as P

HIGH = lax.Precision.HIGHEST
AXES = ("leaf", "group")
F32 = jnp.float32
BF16 = jnp.bfloat16
R = 256
LANES = 128
TILE = 512
AHEAD = 2
VMEM_LIMIT = 40 * 1024 * 1024
OWN, CROSS, PROJECTED, ROOT, SIDE, TERMS = 0, 384, 896, 1408, 1792, 2304


def split2(x):
    high = x.astype(BF16)
    return high, (x - high.astype(F32)).astype(BF16)


def split3(x):
    high = x.astype(BF16)
    rest = x - high.astype(F32)
    mid = rest.astype(BF16)
    return high, mid, (rest - mid.astype(F32)).astype(BF16)


def dot(left, right):
    return jnp.dot(left, right, preferred_element_type=F32)


def dot_t(left, right):
    return lax.dot_general(left, right, (((0,), (0,)), ((), ())), preferred_element_type=F32)


def dot_full(left, right):
    return jnp.dot(left, right, precision=HIGH, preferred_element_type=F32)


def dot_t_full(left, right):
    return lax.dot_general(
        left, right, (((0,), (0,)), ((), ())), precision=HIGH, preferred_element_type=F32
    )


def store_symmetric(ref, row, block):
    ref[row : row + 128, :] = block[:128, :128]
    ref[row + 128 : row + 256, :] = block[128:, :128]
    ref[row + 256 : row + 384, :] = block[128:, 128:]


def store_square(ref, row, block):
    ref[row : row + 256, :] = block[:, :128]
    ref[row + 256 : row + 512, :] = block[:, 128:]


def load_symmetric(ref, row):
    lower = ref[row + 128 : row + 256, :]
    top = jnp.concatenate([ref[row : row + 128, :], lower.T], axis=1)
    bottom = jnp.concatenate([lower, ref[row + 256 : row + 384, :]], axis=1)
    return jnp.concatenate([top, bottom], axis=0)


def load_square(ref, row):
    return jnp.concatenate([ref[row : row + 256, :], ref[row + 256 : row + 512, :]], axis=1)


def gram_kernel(q_two, q_one, sources, keep, send, b2, b1, bs, acc, packed, sems):
    tiles = b2.shape[0] // TILE
    pairs = ((q_two, b2), (q_one, b1), (sources, bs))

    def copy(tile, which):
        here = pl.ds(pl.multiple_of(tile * TILE, TILE), TILE)
        source, target = pairs[which]
        return pltpu.make_async_copy(source.at[here], target.at[here], sems.at[which, tile])

    def start(tile):
        for which in range(3):
            copy(tile, which).start()

    for tile in range(AHEAD):
        start(tile)
    acc[...] = jnp.zeros_like(acc)

    def step(tile, carry):
        for which in range(3):
            copy(tile, which).wait()

        @pl.when(tile + AHEAD < tiles)
        def _():
            start(tile + AHEAD)

        here = pl.ds(pl.multiple_of(tile * TILE, TILE), TILE)
        h2, l2 = split2(b2[here, :])
        h1, l1 = split2(b1[here, :])
        hs, ls = split2(bs[here, :])
        h2t, l2t, h1t, l1t = h2.T, l2.T, h1.T, l1.T
        left2 = jnp.concatenate([h2t, h2t, l2t], axis=1)
        left1 = jnp.concatenate([h1t, h1t, l1t], axis=1)
        right1 = jnp.concatenate([h1, l1, h1], axis=0)
        rights = jnp.concatenate([hs, ls, hs], axis=0)
        acc[0] += dot(h2t, h2)
        acc[1] += dot(h2t, l2)
        acc[2] += dot(left2, right1)
        acc[3] += dot(left2, rights)
        acc[4] += dot(h1t, h1)
        acc[5] += dot(h1t, l1)
        acc[6] += dot(left1, rights)
        return carry

    lax.fori_loop(0, tiles, step, 0)
    low = acc[1]
    store_symmetric(packed, OWN, acc[0] + low + low.T)
    store_square(packed, CROSS, acc[2])
    store_square(packed, PROJECTED, acc[3])
    low = acc[5]
    store_symmetric(packed, ROOT, acc[4] + low + low.T)
    store_square(packed, SIDE, acc[6])
    mine = lax.rem(lax.axis_index("group"), 2)
    half = TERMS // 2
    keep[...] = packed[pl.ds(pl.multiple_of(mine * half, 8), half), :]
    send[...] = packed[pl.ds(pl.multiple_of((1 - mine) * half, 8), half), :]


def gram(q_two, q_one, sources):
    rows = q_two.shape[0]
    part = jax.ShapeDtypeStruct((TERMS // 2, LANES), F32)
    return pl.pallas_call(
        gram_kernel,
        in_specs=[pl.BlockSpec(memory_space=pl.ANY)] * 3,
        out_shape=(part, part),
        scratch_shapes=[
            pltpu.VMEM((rows, R), F32),
            pltpu.VMEM((rows, R), F32),
            pltpu.VMEM((rows, R), F32),
            pltpu.VMEM((7, R, R), F32),
            pltpu.VMEM((TERMS, LANES), F32),
            pltpu.SemaphoreType.DMA((3, rows // TILE)),
        ],
        compiler_params=pltpu.CompilerParams(vmem_limit_bytes=60 * 1024 * 1024),
        cost_estimate=estimate(13, rows, 3),
        name="gram",
    )(q_two, q_one, sources)


def estimate(passes, rows, arrays):
    return pl.CostEstimate(
        flops=2 * passes * rows * R * R, bytes_accessed=4 * arrays * rows * R, transcendentals=0
    )


def spread_lane(x, lane):
    return jnp.broadcast_to(x[:, lane : lane + 1], (8, LANES))


def eliminate(block, cols, rows):
    count = len(block)
    lane = lax.broadcasted_iota(jnp.int32, (8, LANES), 1)
    for start in range(0, count, 4):
        panel = block[start : start + 4]
        left = stack_left(jnp.concatenate(panel, axis=0))
        for t in range(4):
            panel = eliminate_group(panel, t, start + t, cols, rows)
        inside = (lane >= 8 * start) & (lane < 8 * start + 32)
        panel = [jnp.where(inside, -x, x) for x in panel]
        change = dot_t(left, stack_right(jnp.concatenate(panel, axis=0)))
        for g in range(count):
            if start <= g < start + 4:
                block[g] = panel[g - start]
            else:
                block[g] = jnp.where(inside, 0.0, block[g]) - change[8 * g : 8 * g + 8, :]
    return [-x for x in block]


def eliminate_group(panel, t, at, cols, rows):
    lane = lax.broadcasted_iota(jnp.int32, (8, LANES), 1)
    sub = lax.broadcasted_iota(jnp.int32, (8, LANES), 0)
    for j in range(8):
        cols[64 * at + 8 * j : 64 * at + 8 * j + 8, :] = spread_lane(panel[t], 8 * at + j)
    rows[8 * at : 8 * at + 8, :] = panel[t]
    entry = {}
    for i in range(8):
        for j in range(i + 1):
            row = 64 * at + 8 * j + i
            entry[i, j] = jnp.broadcast_to(cols[row : row + 1, :], (8, LANES))
    inside = (lane >= 8 * at) & (lane < 8 * at + 8)
    line = []
    for j in range(8):
        row = jnp.broadcast_to(rows[8 * at + j : 8 * at + j + 1, :], (8, LANES))
        line.append(jnp.where(inside, jnp.where(lane == 8 * at + j, 1.0, 0.0), row))
    line = solve_small(entry, line)
    for g in range(4):
        if g != t:
            terms = [spread_lane(panel[g], 8 * at + j) * line[j] for j in range(8)]
            panel[g] = jnp.where(inside, 0.0, panel[g]) - tree_sum(terms)
    merged = line[0]
    for j in range(1, 8):
        merged = jnp.where(sub == j, line[j], merged)
    panel[t] = merged
    return panel


def tree_sum(terms):
    while len(terms) > 1:
        terms = [
            terms[i] + terms[i + 1] if i + 1 < len(terms) else terms[i]
            for i in range(0, len(terms), 2)
        ]
    return terms[0]


def solve_small(entry, line):
    factors, pivots = {}, {}
    for k in range(0, 8, 2):
        a, b, c = entry[k, k], entry[k + 1, k], entry[k + 1, k + 1]
        inv = pl.reciprocal(a * c - b * b, approx=True)
        e, f, g = c * inv, b * inv, a * inv
        pivots[k] = (e, f, g)
        for i in range(k + 2, 8):
            u, v = entry[i, k], entry[i, k + 1]
            factors[i, k] = (e * u - f * v, g * v - f * u)
        for i in range(k + 2, 8):
            u, v = entry[i, k], entry[i, k + 1]
            for j in range(k + 2, i + 1):
                m, n = factors[j, k]
                entry[i, j] = entry[i, j] - (u * m + v * n)
        for i in range(k + 2, 8):
            m, n = factors[i, k]
            line[i] = line[i] - (m * line[k] + n * line[k + 1])
    for k in range(6, -1, -2):
        e, f, g = pivots[k]
        x, y = e * line[k] - f * line[k + 1], g * line[k + 1] - f * line[k]
        if k < 6:
            x = x - tree_sum([factors[i, k][0] * line[i] for i in range(k + 2, 8)])
            y = y - tree_sum([factors[i, k][1] * line[i] for i in range(k + 2, 8)])
        line[k], line[k + 1] = x, y
    return line


def stack_left(x):
    h, m, l = split3(x)
    return jnp.concatenate([h, h, m, h, l, m], axis=0)


def stack_right(x):
    h, m, l = split3(x)
    return jnp.concatenate([h, m, h, l, h, m], axis=0)


def invert_half(matrix, cols, rows):
    block = eliminate([matrix[8 * i : 8 * i + 8, :] for i in range(LANES // 8)], cols, rows)
    return jnp.concatenate(block, axis=0)


SQUARE = jax.ShapeDtypeStruct((R, R), F32)
CORNER = jax.ShapeDtypeStruct((LANES, LANES), F32)


def call(kernel, out_shape, args, name, scratch=(), flops=0):
    return pl.pallas_call(
        kernel,
        out_shape=out_shape,
        scratch_shapes=list(scratch),
        compiler_params=pltpu.CompilerParams(vmem_limit_bytes=VMEM_LIMIT),
        cost_estimate=pl.CostEstimate(flops=flops, bytes_accessed=R * R * 4, transcendentals=0),
        name=name,
    )(*args)


def first_kernel(which, gram_ref, coupling, first_out, across_out, rest_out, row_out, col_out, cols, rows):
    matrix = coupling[which()] + load_symmetric(gram_ref, OWN)
    eye = lax.broadcasted_iota(jnp.int32, (R, R), 0) == lax.broadcasted_iota(jnp.int32, (R, R), 1)
    diagonal = jnp.where(eye, matrix, 0.0)
    scale_row = lax.rsqrt(jnp.sum(diagonal, axis=0, keepdims=True))
    scale_col = lax.rsqrt(jnp.sum(diagonal, axis=1, keepdims=True))
    matrix = matrix * scale_col * scale_row
    side = matrix[:LANES, LANES:]
    first = invert_half(matrix[:LANES, :LANES], cols, rows)
    across = dot_full(first, side)
    first_out[...] = first
    across_out[...] = across
    rest_out[...] = matrix[LANES:, LANES:] - dot_t_full(side, across)
    row_out[...] = jnp.broadcast_to(scale_row, (8, R))
    col_out[...] = jnp.broadcast_to(scale_col, (R, LANES))


def second_kernel(first, across, rest, row, col, out, cols, rows):
    second = invert_half(rest[...], cols, rows)
    corner = -dot_full(across[...], second)
    top = first[...] - dot_full(corner, across[...].T)
    out[:LANES, :LANES] = top * col[:LANES, :] * row[:1, :LANES]
    out[:LANES, LANES:] = corner * col[:LANES, :] * row[:1, LANES:]
    out[LANES:, :LANES] = corner.T * col[LANES:, :] * row[:1, :LANES]
    out[LANES:, LANES:] = second * col[LANES:, :] * row[:1, LANES:]


SCRATCH = [pltpu.VMEM((1024, LANES), F32), pltpu.VMEM((LANES, LANES), F32)]
HALF_FLOPS = 5_000_000_000


def invert_first(which, packed, coupling, name):
    shapes = (
        CORNER,
        CORNER,
        CORNER,
        jax.ShapeDtypeStruct((8, R), F32),
        jax.ShapeDtypeStruct((R, LANES), F32),
    )
    kernel = functools.partial(first_kernel, which)
    return call(kernel, shapes, (packed, coupling), name, SCRATCH, HALF_FLOPS)


def invert_second(parts, name):
    return call(second_kernel, SQUARE, parts, name, SCRATCH, HALF_FLOPS)


def half_index():
    return lax.axis_index("group") // 2


def no_index():
    return 0


def panel_solve_kernel(inverse, terms, x_out, root_out):
    cross = load_square(terms, CROSS)
    x = dot_full(inverse[...], cross)
    x_out[...] = x
    store_symmetric(root_out, 0, load_symmetric(terms, ROOT) - dot_t_full(cross, x))


def source_solve_kernel(inverse, x, terms, y_out, side_out):
    projected = load_square(terms, PROJECTED)
    y_out[...] = dot_full(inverse[...], projected)
    store_square(side_out, 0, load_square(terms, SIDE) - dot_t_full(x[...], projected))


def dot_three(lh, ll, rh, rl):
    return dot(lh, rh) + (dot(lh, rl) + dot(ll, rh))


def panel_kernel(q_two, q_one, x, out):
    out[...] = q_one[...] - dot_three(*split2(q_two[...]), *split2(x[...]))


def field_kernel(q_two, q_one, sources, inverse, side, x, y, out, w_ref, z_ref):
    @pl.when(pl.program_id(0) == 0)
    def _():
        w = dot_full(inverse[...], load_square(side, 0))
        w_ref[...] = w
        z_ref[...] = y[...] - dot_full(x[...], w)

    change = dot_three(*split2(q_one[...]), *split2(w_ref[...]))
    change += dot_three(*split2(q_two[...]), *split2(z_ref[...]))
    out[...] = sources[...] - change


def update(kernel, tall, small, passes, name, scratch=()):
    rows = tall[0].shape[0]
    spec = pl.BlockSpec((TILE, R), lambda i: (i, 0))
    return pl.pallas_call(
        kernel,
        grid=(rows // TILE,),
        in_specs=[spec] * len(tall) + [pl.BlockSpec(x.shape, lambda i: (0, 0)) for x in small],
        out_specs=spec,
        out_shape=jax.ShapeDtypeStruct((rows, R), F32),
        scratch_shapes=list(scratch),
        compiler_params=pltpu.CompilerParams(vmem_limit_bytes=VMEM_LIMIT),
        cost_estimate=estimate(passes, rows, len(tall) + 1),
        name=name,
    )(*tall, *small)


def exchange(x, mask):
    count = lax.axis_size(AXES)
    return lax.ppermute(x, AXES, [(i, i ^ mask) for i in range(count)])


def scatter_sum(x, index, bit):
    mine = (index >> bit) & 1
    parts = x.reshape(2, x.shape[0] // 2, x.shape[1])
    sent = lax.dynamic_index_in_dim(parts, 1 - mine, 0, keepdims=False)
    kept = lax.dynamic_index_in_dim(parts, mine, 0, keepdims=False)
    return kept + exchange(sent, 1 << bit)


def gather(x, index, bit):
    mine = (index >> bit) & 1
    other = exchange(x, 1 << bit)
    low = jnp.where(mine == 0, x, other)
    high = jnp.where(mine == 0, other, x)
    return jnp.concatenate([low, high], axis=0)


def per_device(q_two, q_one, sources, coupling_two, coupling_one):
    index = lax.axis_index(AXES)
    leaf_bits = list(range(2, lax.axis_size("leaf").bit_length() + 1))
    orders = (leaf_bits, leaf_bits[1:] + leaf_bits[:1])
    keep, send = gram(q_two, q_one, sources)
    terms = keep + exchange(send, 1)
    parts = [terms[: TERMS // 4], terms[TERMS // 4 :]]
    for step in range(len(leaf_bits)):
        parts = [scatter_sum(x, index, order[step]) for x, order in zip(parts, orders)]
    for step in reversed(range(len(leaf_bits))):
        parts = [gather(x, index, order[step]) for x, order in zip(parts, orders)]
    terms = gather(jnp.concatenate(parts, axis=0), index, 0)

    def half_rows(terms):
        parts = terms.reshape(2, terms.shape[0] // 2, LANES)
        return lax.dynamic_index_in_dim(parts, index & 1, 0, keepdims=False)

    parts = invert_first(half_index, terms, coupling_two, "level_first")
    inverse = invert_second(parts, "level_second")
    x, root = call(
        panel_solve_kernel, (SQUARE, jax.ShapeDtypeStruct((384, LANES), F32)), (inverse, terms), "panel_solve"
    )
    root = half_rows(root)
    arriving = exchange(root, 2)
    panel_one = update(panel_kernel, [q_two, q_one], [x], 3, "panel")
    arriving, panel_one = lax.optimization_barrier((arriving, panel_one))
    root = gather(root + arriving, index, 0)
    terms, panel_one = lax.optimization_barrier((terms, panel_one))
    y, side = call(
        source_solve_kernel, (SQUARE, jax.ShapeDtypeStruct((512, LANES), F32)), (inverse, x, terms), "source_solve"
    )
    side = half_rows(side)
    arriving = exchange(side, 2)
    parts = invert_first(no_index, root, coupling_one[None], "root_first")
    arriving, parts = lax.optimization_barrier((arriving, parts))
    side = gather(side + arriving, index, 0)
    inverse = invert_second(parts, "root_second")
    solution = update(
        field_kernel,
        [q_two, q_one, sources],
        [inverse, side, x, y],
        6,
        "field",
        [pltpu.VMEM((R, R), F32), pltpu.VMEM((R, R), F32)],
    )
    return (panel_one, solution)


def solution(mesh):
    placed = P(("group", "leaf"), None)
    return jax.shard_map(
        per_device,
        mesh=mesh,
        in_specs=(placed, placed, placed, P(), P()),
        out_specs=(placed, placed),
        check_vma=False,
    )
```

```python
import functools

import jax
import jax.numpy as jnp
from jax import lax
from jax.experimental import pallas as pl
from jax.experimental.pallas import tpu as pltpu
from jax.sharding import PartitionSpec as P

HIGH = lax.Precision.HIGHEST
AXES = ("leaf", "group")
F32 = jnp.float32
BF16 = jnp.bfloat16
R = 256
LANES = 128
TILE = 512
VMEM_LIMIT = 40 * 1024 * 1024
SYMMETRIC, FULL = 264, 512
OWN, ROOT, CROSS, PANEL_TERMS = 0, 264, 528, 1040
PROJECTED, SIDE, SOURCE_TERMS = 0, 512, 1024


def split2(x):
    high = x.astype(BF16)
    return high, (x - high.astype(F32)).astype(BF16)


def split3(x):
    high = x.astype(BF16)
    rest = x - high.astype(F32)
    mid = rest.astype(BF16)
    return high, mid, (rest - mid.astype(F32)).astype(BF16)


def dot(left, right):
    return jnp.dot(left, right, preferred_element_type=F32)


def dot_t(left, right):
    return lax.dot_general(left, right, (((0,), (0,)), ((), ())), preferred_element_type=F32)


def dot_full(left, right):
    return jnp.dot(left, right, precision=HIGH, preferred_element_type=F32)


def dot_t_full(left, right):
    return lax.dot_general(
        left, right, (((0,), (0,)), ((), ())), precision=HIGH, preferred_element_type=F32
    )


def square_index():
    row = lax.broadcasted_iota(jnp.int32, (LANES, LANES), 0)
    return row, lax.broadcasted_iota(jnp.int32, (LANES, LANES), 1)


def store_symmetric(ref, at, block):
    row, col = square_index()
    last = block[128:, 128:]
    ref[at : at + 128, :] = block[128:, :128]
    ref[at + 128 : at + 256, :] = jnp.where(row >= col, block[:128, :128], last)
    diagonal = jnp.sum(jnp.where(row == col, last, 0.0), axis=0, keepdims=True)
    ref[at + 256 : at + 264, :] = jnp.broadcast_to(diagonal, (8, LANES))


def store_square(ref, row, block):
    ref[row : row + 256, :] = block[:, :128]
    ref[row + 256 : row + 512, :] = block[:, 128:]


def load_symmetric(ref, at):
    row, col = square_index()
    lower = ref[at : at + 128, :]
    mixed = ref[at + 128 : at + 256, :]
    turned = mixed.T
    first = jnp.where(row >= col, mixed, turned)
    last = jnp.where(row < col, mixed, turned)
    last = jnp.where(row == col, ref[at + 256 : at + 257, :], last)
    top = jnp.concatenate([first, lower.T], axis=1)
    return jnp.concatenate([top, jnp.concatenate([lower, last], axis=1)], axis=0)


def load_square(ref, row):
    return jnp.concatenate([ref[row : row + 256, :], ref[row + 256 : row + 512, :]], axis=1)


def half_of(rows):
    return (rows + 15) // 16 * 8


def store_halves(packed, keep, send):
    half = half_of(packed.shape[0])
    far = packed.shape[0] - half
    mine = lax.rem(lax.axis_index("group"), 2)
    keep[...] = packed[pl.ds(pl.multiple_of(mine * far, 8), half), :]
    send[...] = packed[pl.ds(pl.multiple_of((1 - mine) * far, 8), half), :]


def tile_at(tile):
    return pl.ds(pl.multiple_of(tile * TILE, TILE), TILE)


def panel_gram_kernel(q_two, q_one, keep, send, b2, b1, acc, packed, sems):
    tiles = b2.shape[0] // TILE
    pairs = ((q_two, b2), (q_one, b1))

    def copy(tile, which):
        source, target = pairs[which]
        here = tile_at(tile)
        return pltpu.make_async_copy(source.at[here], target.at[here], sems.at[which, tile])

    for tile in range(tiles):
        for which in range(2):
            copy(tile, which).start()
    acc[...] = jnp.zeros_like(acc)

    def step(tile, carry):
        for which in range(2):
            copy(tile, which).wait()
        h2, l2 = split2(b2[tile_at(tile), :])
        h1, l1 = split2(b1[tile_at(tile), :])
        h2t, l2t, h1t = h2.T, l2.T, h1.T
        acc[0] += dot(h2t, h2)
        acc[1] += dot(h2t, l2)
        left = jnp.concatenate([h2t, h2t, l2t], axis=1)
        acc[2] += dot(left, jnp.concatenate([h1, l1, h1], axis=0))
        acc[3] += dot(h1t, h1)
        acc[4] += dot(h1t, l1)
        return carry

    lax.fori_loop(0, tiles, step, 0)
    low = acc[1]
    store_symmetric(packed, OWN, acc[0] + low + low.T)
    low = acc[4]
    store_symmetric(packed, ROOT, acc[3] + low + low.T)
    store_square(packed, CROSS, acc[2])
    store_halves(packed, keep, send)


def source_gram_kernel(b2, b1, sources, keep, send, acc, packed):
    acc[...] = jnp.zeros_like(acc)

    def step(tile, carry):
        hs, ls = split2(sources[tile_at(tile), :])
        right = jnp.concatenate([hs, ls, hs], axis=0)
        for which, panel in enumerate((b2, b1)):
            high, low = split2(panel[tile_at(tile), :])
            turned = high.T
            acc[which] += dot(jnp.concatenate([turned, turned, low.T], axis=1), right)
        return carry

    lax.fori_loop(0, b2.shape[0] // TILE, step, 0)
    store_square(packed, PROJECTED, acc[0])
    store_square(packed, SIDE, acc[1])
    store_halves(packed, keep, send)


def cost(passes, rows, arrays):
    return pl.CostEstimate(
        flops=2 * passes * rows * R * R, bytes_accessed=4 * arrays * rows * R, transcendentals=0
    )


def panel_gram(q_two, q_one):
    rows = q_two.shape[0]
    part = jax.ShapeDtypeStruct((half_of(PANEL_TERMS), LANES), F32)
    tall = jax.ShapeDtypeStruct((rows, R), F32)
    return pl.pallas_call(
        panel_gram_kernel,
        in_specs=[pl.BlockSpec(memory_space=pl.ANY)] * 2,
        out_shape=(part, part, tall, tall),
        scratch_shapes=[
            pltpu.VMEM((5, R, R), F32),
            pltpu.VMEM((PANEL_TERMS, LANES), F32),
            pltpu.SemaphoreType.DMA((2, rows // TILE)),
        ],
        compiler_params=pltpu.CompilerParams(vmem_limit_bytes=VMEM_LIMIT),
        cost_estimate=cost(7, rows, 2),
        name="panel_gram",
    )(pltpu.with_memory_space_constraint(q_two, pltpu.HBM), pltpu.with_memory_space_constraint(q_one, pltpu.HBM))


def source_gram(b2, b1, sources):
    part = jax.ShapeDtypeStruct((half_of(SOURCE_TERMS), LANES), F32)
    return pl.pallas_call(
        source_gram_kernel,
        out_shape=(part, part),
        scratch_shapes=[pltpu.VMEM((2, R, R), F32), pltpu.VMEM((SOURCE_TERMS, LANES), F32)],
        compiler_params=pltpu.CompilerParams(vmem_limit_bytes=VMEM_LIMIT),
        cost_estimate=cost(6, b2.shape[0], 3),
        name="source_gram",
    )(b2, b1, sources)


def spread_lane(x, lane):
    return jnp.broadcast_to(x[:, lane : lane + 1], (8, LANES))


def eliminate(block, cols, rows):
    count = len(block)
    lane = lax.broadcasted_iota(jnp.int32, (8, LANES), 1)
    for start in range(0, count, 4):
        panel = block[start : start + 4]
        left = stack_left(jnp.concatenate(panel, axis=0))
        for t in range(4):
            panel = eliminate_group(panel, t, start + t, cols, rows)
        inside = (lane >= 8 * start) & (lane < 8 * start + 32)
        panel = [jnp.where(inside, -x, x) for x in panel]
        change = dot_t(left, stack_right(jnp.concatenate(panel, axis=0)))
        for g in range(count):
            if start <= g < start + 4:
                block[g] = panel[g - start]
            else:
                block[g] = jnp.where(inside, 0.0, block[g]) - change[8 * g : 8 * g + 8, :]
    return [-x for x in block]


def eliminate_group(panel, t, at, cols, rows):
    lane = lax.broadcasted_iota(jnp.int32, (8, LANES), 1)
    sub = lax.broadcasted_iota(jnp.int32, (8, LANES), 0)
    for j in range(8):
        cols[64 * at + 8 * j : 64 * at + 8 * j + 8, :] = spread_lane(panel[t], 8 * at + j)
    rows[8 * at : 8 * at + 8, :] = panel[t]
    entry = {}
    for i in range(8):
        for j in range(i + 1):
            row = 64 * at + 8 * j + i
            entry[i, j] = jnp.broadcast_to(cols[row : row + 1, :], (8, LANES))
    inside = (lane >= 8 * at) & (lane < 8 * at + 8)
    line = []
    for j in range(8):
        row = jnp.broadcast_to(rows[8 * at + j : 8 * at + j + 1, :], (8, LANES))
        line.append(jnp.where(inside, jnp.where(lane == 8 * at + j, 1.0, 0.0), row))
    line = solve_small(entry, line)
    for g in range(4):
        if g != t:
            terms = [spread_lane(panel[g], 8 * at + j) * line[j] for j in range(8)]
            panel[g] = jnp.where(inside, 0.0, panel[g]) - tree_sum(terms)
    merged = line[0]
    for j in range(1, 8):
        merged = jnp.where(sub == j, line[j], merged)
    panel[t] = merged
    return panel


def tree_sum(terms):
    while len(terms) > 1:
        terms = [
            terms[i] + terms[i + 1] if i + 1 < len(terms) else terms[i]
            for i in range(0, len(terms), 2)
        ]
    return terms[0]


def solve_small(entry, line):
    factors, pivots = {}, {}
    for k in range(0, 8, 2):
        a, b, c = entry[k, k], entry[k + 1, k], entry[k + 1, k + 1]
        inv = pl.reciprocal(a * c - b * b, approx=True)
        e, f, g = c * inv, b * inv, a * inv
        pivots[k] = (e, f, g)
        for i in range(k + 2, 8):
            u, v = entry[i, k], entry[i, k + 1]
            factors[i, k] = (e * u - f * v, g * v - f * u)
        for i in range(k + 2, 8):
            u, v = entry[i, k], entry[i, k + 1]
            for j in range(k + 2, i + 1):
                m, n = factors[j, k]
                entry[i, j] = entry[i, j] - (u * m + v * n)
        for i in range(k + 2, 8):
            m, n = factors[i, k]
            line[i] = line[i] - (m * line[k] + n * line[k + 1])
    for k in range(6, -1, -2):
        e, f, g = pivots[k]
        x, y = e * line[k] - f * line[k + 1], g * line[k + 1] - f * line[k]
        if k < 6:
            x = x - tree_sum([factors[i, k][0] * line[i] for i in range(k + 2, 8)])
            y = y - tree_sum([factors[i, k][1] * line[i] for i in range(k + 2, 8)])
        line[k], line[k + 1] = x, y
    return line


def stack_left(x):
    h, m, l = split3(x)
    return jnp.concatenate([h, h, m, h, l, m], axis=0)


def stack_right(x):
    h, m, l = split3(x)
    return jnp.concatenate([h, m, h, l, h, m], axis=0)


def invert_half(matrix, cols, rows):
    block = eliminate([matrix[8 * i : 8 * i + 8, :] for i in range(LANES // 8)], cols, rows)
    return jnp.concatenate(block, axis=0)


SQUARE = jax.ShapeDtypeStruct((R, R), F32)
CORNER = jax.ShapeDtypeStruct((LANES, LANES), F32)


def call(kernel, out_shape, args, name, scratch=(), flops=0):
    return pl.pallas_call(
        kernel,
        out_shape=out_shape,
        scratch_shapes=list(scratch),
        compiler_params=pltpu.CompilerParams(vmem_limit_bytes=VMEM_LIMIT),
        cost_estimate=pl.CostEstimate(flops=flops, bytes_accessed=R * R * 4, transcendentals=0),
        name=name,
    )(*args)


def first_kernel(which, gram_ref, coupling, first_out, across_out, rest_out, row_out, col_out, cols, rows):
    matrix = coupling[which()] + load_symmetric(gram_ref, OWN)
    eye = lax.broadcasted_iota(jnp.int32, (R, R), 0) == lax.broadcasted_iota(jnp.int32, (R, R), 1)
    diagonal = jnp.where(eye, matrix, 0.0)
    scale_row = lax.rsqrt(jnp.sum(diagonal, axis=0, keepdims=True))
    scale_col = lax.rsqrt(jnp.sum(diagonal, axis=1, keepdims=True))
    matrix = matrix * scale_col * scale_row
    side = matrix[:LANES, LANES:]
    first = invert_half(matrix[:LANES, :LANES], cols, rows)
    across = dot_full(first, side)
    first_out[...] = first
    across_out[...] = across
    rest_out[...] = matrix[LANES:, LANES:] - dot_t_full(side, across)
    row_out[...] = jnp.broadcast_to(scale_row, (8, R))
    col_out[...] = jnp.broadcast_to(scale_col, (R, LANES))


def second_kernel(first, across, rest, row, col, out, cols, rows):
    second = invert_half(rest[...], cols, rows)
    corner = -dot_full(across[...], second)
    top = first[...] - dot_full(corner, across[...].T)
    out[:LANES, :LANES] = top * col[:LANES, :] * row[:1, :LANES]
    out[:LANES, LANES:] = corner * col[:LANES, :] * row[:1, LANES:]
    out[LANES:, :LANES] = corner.T * col[LANES:, :] * row[:1, :LANES]
    out[LANES:, LANES:] = second * col[LANES:, :] * row[:1, LANES:]


SCRATCH = [pltpu.VMEM((1024, LANES), F32), pltpu.VMEM((LANES, LANES), F32)]
HALF_FLOPS = 5_000_000_000


def invert_first(which, packed, coupling, name):
    shapes = (
        CORNER,
        CORNER,
        CORNER,
        jax.ShapeDtypeStruct((8, R), F32),
        jax.ShapeDtypeStruct((R, LANES), F32),
    )
    kernel = functools.partial(first_kernel, which)
    return call(kernel, shapes, (packed, coupling), name, SCRATCH, HALF_FLOPS)


def invert_second(parts, name):
    return call(second_kernel, SQUARE, parts, name, SCRATCH, HALF_FLOPS)


def half_index():
    return lax.axis_index("group") // 2


def no_index():
    return 0


def panel_solve_kernel(inverse, terms, x_out, root_out):
    cross = load_square(terms, CROSS)
    x = dot_full(inverse[...], cross)
    x_out[...] = x
    store_symmetric(root_out, 0, load_symmetric(terms, ROOT) - dot_t_full(cross, x))


def source_solve_kernel(inverse, x, terms, y_out, side_out):
    projected = load_square(terms, PROJECTED)
    y_out[...] = dot_full(inverse[...], projected)
    store_square(side_out, 0, load_square(terms, SIDE) - dot_t_full(x[...], projected))


def wide(x):
    high, low = split2(x)
    return jnp.concatenate([high, high, low], axis=1)


def tall(x):
    high, low = split2(x)
    return jnp.concatenate([high, low, high], axis=0)


def by_tiles(rows, out, stage, sems, value):
    tiles = rows // TILE

    def copy(tile):
        return pltpu.make_async_copy(stage.at[tile_at(tile)], out.at[tile_at(tile)], sems.at[tile])

    def step(tile, carry):
        stage[tile_at(tile), :] = value(tile_at(tile))
        copy(tile).start()
        return carry

    lax.fori_loop(0, tiles, step, 0)
    for tile in range(tiles):
        copy(tile).wait()


def panel_kernel(b2, b1, x, out, stage, sems):
    right = tall(x[...])
    by_tiles(b2.shape[0], out, stage, sems, lambda at: b1[at, :] - dot(wide(b2[at, :]), right))


def field_kernel(b2, panel, sources, inverse, side, y, out, stage, sems):
    weights = dot(wide(inverse[...]), tall(load_square(side, 0)))
    right = jnp.concatenate([tall(y[...]), tall(weights)], axis=0)

    def value(at):
        left = jnp.concatenate([wide(b2[at, :]), wide(panel[at, :])], axis=1)
        return sources[at, :] - dot(left, right)

    by_tiles(b2.shape[0], out, stage, sems, value)


def update(kernel, args, passes, name):
    rows = args[0].shape[0]
    return pl.pallas_call(
        kernel,
        out_specs=pl.BlockSpec(memory_space=pl.ANY),
        out_shape=jax.ShapeDtypeStruct((rows, R), F32),
        scratch_shapes=[pltpu.VMEM((rows, R), F32), pltpu.SemaphoreType.DMA((rows // TILE,))],
        compiler_params=pltpu.CompilerParams(vmem_limit_bytes=VMEM_LIMIT),
        cost_estimate=cost(passes, rows, 3),
        name=name,
    )(*args)


def exchange(x, mask):
    count = lax.axis_size(AXES)
    return lax.ppermute(x, AXES, [(i, i ^ mask) for i in range(count)])


def rows_of(x, bit_value):
    half = half_of(x.shape[0])
    return lax.dynamic_slice_in_dim(x, bit_value * (x.shape[0] - half), half, 0)


def scatter_sum(x, index, bit):
    mine = (index >> bit) & 1
    return rows_of(x, mine) + exchange(rows_of(x, 1 - mine), 1 << bit)


def join(x, other, rows, index, bit):
    mine = (index >> bit) & 1
    low = jnp.where(mine == 0, x, other)
    high = jnp.where(mine == 0, other, x)
    return jnp.concatenate([low[: rows - x.shape[0]], high], axis=0)


def gather(x, rows, index, bit):
    return join(x, exchange(x, 1 << bit), rows, index, bit)


def per_device(q_two, q_one, sources, coupling_two, coupling_one):
    index = lax.axis_index(AXES)
    leaf_bits = list(range(2, lax.axis_size("leaf").bit_length() + 1))
    panel_order, source_order = leaf_bits, leaf_bits[1:] + leaf_bits[:1]

    def scatter(x, order):
        sizes = []
        for bit in order:
            sizes.append(x.shape[0])
            x = scatter_sum(x, index, bit)
        return x, sizes

    keep, send, b2, b1 = panel_gram(q_two, q_one)
    terms = keep + exchange(send, 1)
    keep, send = source_gram(b2, b1, sources)
    source = keep + exchange(send, 1)
    terms, panel_sizes = scatter(terms, panel_order)
    source, source_sizes = scatter(source, source_order)
    for bit, rows in zip(reversed(panel_order), reversed(panel_sizes)):
        terms = gather(terms, rows, index, bit)
    terms = gather(terms, PANEL_TERMS, index, 0)
    for bit, rows in zip(reversed(source_order[1:]), reversed(source_sizes[1:])):
        source = gather(source, rows, index, bit)
    source_arriving = exchange(source, 1 << source_order[0])

    def half_rows(terms):
        return rows_of(terms, index & 1)

    parts = invert_first(half_index, terms, coupling_two, "level_first")
    source_arriving, parts = lax.optimization_barrier((source_arriving, parts))
    source = join(source, source_arriving, source_sizes[0], index, source_order[0])
    source_arriving = exchange(source, 1)
    inverse = invert_second(parts, "level_second")
    source_arriving, inverse = lax.optimization_barrier((source_arriving, inverse))
    x, root = call(
        panel_solve_kernel, (SQUARE, jax.ShapeDtypeStruct((SYMMETRIC, LANES), F32)), (inverse, terms), "panel_solve"
    )
    root = half_rows(root)
    arriving = exchange(root, 2)
    panel_one = update(panel_kernel, [b2, b1, x], 3, "panel")
    arriving, panel_one, source_arriving = lax.optimization_barrier((arriving, panel_one, source_arriving))
    root = gather(root + arriving, SYMMETRIC, index, 0)
    source = join(source, source_arriving, SOURCE_TERMS, index, 0)
    y, side = call(
        source_solve_kernel, (SQUARE, jax.ShapeDtypeStruct((FULL, LANES), F32)), (inverse, x, source), "source_solve"
    )
    side = half_rows(side)
    arriving = exchange(side, 2)
    parts = invert_first(no_index, root, coupling_one[None], "root_first")
    arriving, parts = lax.optimization_barrier((arriving, parts))
    side = gather(side + arriving, FULL, index, 0)
    inverse = invert_second(parts, "root_second")
    solution = update(field_kernel, [b2, panel_one, sources, inverse, side, y], 6, "field")
    return (panel_one, solution)


def solution(mesh):
    placed = P(("group", "leaf"), None)
    return jax.shard_map(
        per_device,
        mesh=mesh,
        in_specs=(placed, placed, placed, P(), P()),
        out_specs=(placed, placed),
        check_vma=False,
    )
```

```python
import functools

import jax
import jax.numpy as jnp
from jax import lax
from jax.experimental import pallas as pl
from jax.experimental.pallas import tpu as pltpu
from jax.sharding import PartitionSpec as P

HIGH = lax.Precision.HIGHEST
AXES = ("leaf", "group")
F32 = jnp.float32
BF16 = jnp.bfloat16
R = 256
LANES = 128
TILE = 512
VMEM_LIMIT = 40 * 1024 * 1024
SYMMETRIC, FULL = 264, 512
OWN, ROOT, CROSS, PANEL_TERMS = 0, 264, 528, 1040


def split2(x):
    high = x.astype(BF16)
    return high, (x - high.astype(F32)).astype(BF16)


def split3(x):
    high = x.astype(BF16)
    rest = x - high.astype(F32)
    mid = rest.astype(BF16)
    return high, mid, (rest - mid.astype(F32)).astype(BF16)


def dot(left, right):
    return jnp.dot(left, right, preferred_element_type=F32)


def dot_t(left, right):
    return lax.dot_general(left, right, (((0,), (0,)), ((), ())), preferred_element_type=F32)


def dot_full(left, right):
    return jnp.dot(left, right, precision=HIGH, preferred_element_type=F32)


def dot_t_full(left, right):
    return lax.dot_general(
        left, right, (((0,), (0,)), ((), ())), precision=HIGH, preferred_element_type=F32
    )


def square_index():
    row = lax.broadcasted_iota(jnp.int32, (LANES, LANES), 0)
    return row, lax.broadcasted_iota(jnp.int32, (LANES, LANES), 1)


def store_symmetric(ref, at, block):
    row, col = square_index()
    last = block[128:, 128:]
    ref[at : at + 128, :] = block[128:, :128]
    ref[at + 128 : at + 256, :] = jnp.where(row >= col, block[:128, :128], last)
    diagonal = jnp.sum(jnp.where(row == col, last, 0.0), axis=0, keepdims=True)
    ref[at + 256 : at + 264, :] = jnp.broadcast_to(diagonal, (8, LANES))


def store_square(ref, row, block):
    ref[row : row + 256, :] = block[:, :128]
    ref[row + 256 : row + 512, :] = block[:, 128:]


def load_symmetric(ref, at):
    row, col = square_index()
    lower = ref[at : at + 128, :]
    mixed = ref[at + 128 : at + 256, :]
    turned = mixed.T
    first = jnp.where(row >= col, mixed, turned)
    last = jnp.where(row < col, mixed, turned)
    last = jnp.where(row == col, ref[at + 256 : at + 257, :], last)
    top = jnp.concatenate([first, lower.T], axis=1)
    return jnp.concatenate([top, jnp.concatenate([lower, last], axis=1)], axis=0)


def load_square(ref, row):
    return jnp.concatenate([ref[row : row + 256, :], ref[row + 256 : row + 512, :]], axis=1)


def half_of(rows):
    return (rows + 15) // 16 * 8


def store_halves(packed, keep, send):
    half = half_of(packed.shape[0])
    far = packed.shape[0] - half
    mine = lax.rem(lax.axis_index("group"), 2)
    keep[...] = packed[pl.ds(pl.multiple_of(mine * far, 8), half), :]
    send[...] = packed[pl.ds(pl.multiple_of((1 - mine) * far, 8), half), :]


def tile_at(tile):
    return pl.ds(pl.multiple_of(tile * TILE, TILE), TILE)


def panel_gram_kernel(q_two, q_one, keep, send, b2, b1, acc, packed, sems):
    tiles = b2.shape[0] // TILE
    pairs = ((q_two, b2), (q_one, b1))

    def copy(tile, which):
        source, target = pairs[which]
        here = tile_at(tile)
        return pltpu.make_async_copy(source.at[here], target.at[here], sems.at[which, tile])

    for tile in range(tiles):
        for which in range(2):
            copy(tile, which).start()
    acc[...] = jnp.zeros_like(acc)

    def step(tile, carry):
        for which in range(2):
            copy(tile, which).wait()
        h2, l2 = split2(b2[tile_at(tile), :])
        h1, l1 = split2(b1[tile_at(tile), :])
        h2t, l2t, h1t = h2.T, l2.T, h1.T
        acc[0] += dot(h2t, h2)
        acc[1] += dot(h2t, l2)
        left = jnp.concatenate([h2t, h2t, l2t], axis=1)
        acc[2] += dot(left, jnp.concatenate([h1, l1, h1], axis=0))
        acc[3] += dot(h1t, h1)
        acc[4] += dot(h1t, l1)
        return carry

    lax.fori_loop(0, tiles, step, 0)
    low = acc[1]
    store_symmetric(packed, OWN, acc[0] + low + low.T)
    low = acc[4]
    store_symmetric(packed, ROOT, acc[3] + low + low.T)
    store_square(packed, CROSS, acc[2])
    store_halves(packed, keep, send)


def source_gram_kernel(b2, b1, sources, keep, send, acc):
    acc[...] = jnp.zeros_like(acc)

    def step(tile, carry):
        high, low = split2(sources[tile_at(tile), :])
        turned = high.T
        left = jnp.concatenate([turned, turned, low.T], axis=1)
        acc[:, :R] += dot(left, tall(b2[tile_at(tile), :]))
        acc[:, R:] += dot(left, tall(b1[tile_at(tile), :]))
        return carry

    lax.fori_loop(0, b2.shape[0] // TILE, step, 0)
    store_halves(acc, keep, send)


def cost(passes, rows, arrays):
    return pl.CostEstimate(
        flops=2 * passes * rows * R * R, bytes_accessed=4 * arrays * rows * R, transcendentals=0
    )


def panel_gram(q_two, q_one):
    rows = q_two.shape[0]
    part = jax.ShapeDtypeStruct((half_of(PANEL_TERMS), LANES), F32)
    tall = jax.ShapeDtypeStruct((rows, R), F32)
    return pl.pallas_call(
        panel_gram_kernel,
        in_specs=[pl.BlockSpec(memory_space=pl.ANY)] * 2,
        out_shape=(part, part, tall, tall),
        scratch_shapes=[
            pltpu.VMEM((5, R, R), F32),
            pltpu.VMEM((PANEL_TERMS, LANES), F32),
            pltpu.SemaphoreType.DMA((2, rows // TILE)),
        ],
        compiler_params=pltpu.CompilerParams(vmem_limit_bytes=VMEM_LIMIT),
        cost_estimate=cost(7, rows, 2),
        name="panel_gram",
    )(pltpu.with_memory_space_constraint(q_two, pltpu.HBM), pltpu.with_memory_space_constraint(q_one, pltpu.HBM))


def source_gram(b2, b1, sources):
    part = jax.ShapeDtypeStruct((half_of(R), 2 * R), F32)
    return pl.pallas_call(
        source_gram_kernel,
        out_shape=(part, part),
        scratch_shapes=[pltpu.VMEM((R, 2 * R), F32)],
        compiler_params=pltpu.CompilerParams(vmem_limit_bytes=VMEM_LIMIT),
        cost_estimate=cost(6, b2.shape[0], 3),
        name="source_gram",
    )(b2, b1, sources)


def spread_lane(x, lane):
    return jnp.broadcast_to(x[:, lane : lane + 1], (8, LANES))


def eliminate(block, cols, rows):
    count = len(block)
    lane = lax.broadcasted_iota(jnp.int32, (8, LANES), 1)
    for start in range(0, count, 4):
        panel = block[start : start + 4]
        left = stack_left(jnp.concatenate(panel, axis=0))
        for t in range(4):
            panel = eliminate_group(panel, t, start + t, cols, rows)
        inside = (lane >= 8 * start) & (lane < 8 * start + 32)
        panel = [jnp.where(inside, -x, x) for x in panel]
        change = dot_t(left, stack_right(jnp.concatenate(panel, axis=0)))
        for g in range(count):
            if start <= g < start + 4:
                block[g] = panel[g - start]
            else:
                block[g] = jnp.where(inside, 0.0, block[g]) - change[8 * g : 8 * g + 8, :]
    return [-x for x in block]


def eliminate_group(panel, t, at, cols, rows):
    lane = lax.broadcasted_iota(jnp.int32, (8, LANES), 1)
    sub = lax.broadcasted_iota(jnp.int32, (8, LANES), 0)
    for j in range(8):
        cols[64 * at + 8 * j : 64 * at + 8 * j + 8, :] = spread_lane(panel[t], 8 * at + j)
    rows[8 * at : 8 * at + 8, :] = panel[t]
    entry = {}
    for i in range(8):
        for j in range(i + 1):
            row = 64 * at + 8 * j + i
            entry[i, j] = jnp.broadcast_to(cols[row : row + 1, :], (8, LANES))
    inside = (lane >= 8 * at) & (lane < 8 * at + 8)
    line = []
    for j in range(8):
        row = jnp.broadcast_to(rows[8 * at + j : 8 * at + j + 1, :], (8, LANES))
        line.append(jnp.where(inside, jnp.where(lane == 8 * at + j, 1.0, 0.0), row))
    line = solve_small(entry, line)
    for g in range(4):
        if g != t:
            terms = [spread_lane(panel[g], 8 * at + j) * line[j] for j in range(8)]
            panel[g] = jnp.where(inside, 0.0, panel[g]) - tree_sum(terms)
    merged = line[0]
    for j in range(1, 8):
        merged = jnp.where(sub == j, line[j], merged)
    panel[t] = merged
    return panel


def tree_sum(terms):
    while len(terms) > 1:
        terms = [
            terms[i] + terms[i + 1] if i + 1 < len(terms) else terms[i]
            for i in range(0, len(terms), 2)
        ]
    return terms[0]


def solve_small(entry, line):
    factors, pivots = {}, {}
    for k in range(0, 8, 2):
        a, b, c = entry[k, k], entry[k + 1, k], entry[k + 1, k + 1]
        inv = pl.reciprocal(a * c - b * b, approx=True)
        e, f, g = c * inv, b * inv, a * inv
        pivots[k] = (e, f, g)
        for i in range(k + 2, 8):
            u, v = entry[i, k], entry[i, k + 1]
            factors[i, k] = (e * u - f * v, g * v - f * u)
        for i in range(k + 2, 8):
            u, v = entry[i, k], entry[i, k + 1]
            for j in range(k + 2, i + 1):
                m, n = factors[j, k]
                entry[i, j] = entry[i, j] - (u * m + v * n)
        for i in range(k + 2, 8):
            m, n = factors[i, k]
            line[i] = line[i] - (m * line[k] + n * line[k + 1])
    for k in range(6, -1, -2):
        e, f, g = pivots[k]
        x, y = e * line[k] - f * line[k + 1], g * line[k + 1] - f * line[k]
        if k < 6:
            x = x - tree_sum([factors[i, k][0] * line[i] for i in range(k + 2, 8)])
            y = y - tree_sum([factors[i, k][1] * line[i] for i in range(k + 2, 8)])
        line[k], line[k + 1] = x, y
    return line


def stack_left(x):
    h, m, l = split3(x)
    return jnp.concatenate([h, h, m, h, l, m], axis=0)


def stack_right(x):
    h, m, l = split3(x)
    return jnp.concatenate([h, m, h, l, h, m], axis=0)


def invert_half(matrix, cols, rows):
    block = eliminate([matrix[8 * i : 8 * i + 8, :] for i in range(LANES // 8)], cols, rows)
    return jnp.concatenate(block, axis=0)


SQUARE = jax.ShapeDtypeStruct((R, R), F32)
CORNER = jax.ShapeDtypeStruct((LANES, LANES), F32)


def call(kernel, out_shape, args, name, scratch=(), flops=0):
    return pl.pallas_call(
        kernel,
        out_shape=out_shape,
        scratch_shapes=list(scratch),
        compiler_params=pltpu.CompilerParams(vmem_limit_bytes=VMEM_LIMIT),
        cost_estimate=pl.CostEstimate(flops=flops, bytes_accessed=R * R * 4, transcendentals=0),
        name=name,
    )(*args)


def first_kernel(which, gram_ref, coupling, first_out, across_out, rest_out, row_out, col_out, cols, rows):
    matrix = coupling[which()] + load_symmetric(gram_ref, OWN)
    eye = lax.broadcasted_iota(jnp.int32, (R, R), 0) == lax.broadcasted_iota(jnp.int32, (R, R), 1)
    diagonal = jnp.where(eye, matrix, 0.0)
    scale_row = lax.rsqrt(jnp.sum(diagonal, axis=0, keepdims=True))
    scale_col = lax.rsqrt(jnp.sum(diagonal, axis=1, keepdims=True))
    matrix = matrix * scale_col * scale_row
    side = matrix[:LANES, LANES:]
    first = invert_half(matrix[:LANES, :LANES], cols, rows)
    across = dot_full(first, side)
    first_out[...] = first
    across_out[...] = across
    rest_out[...] = matrix[LANES:, LANES:] - dot_t_full(side, across)
    row_out[...] = jnp.broadcast_to(scale_row, (8, R))
    col_out[...] = jnp.broadcast_to(scale_col, (R, LANES))


def second_kernel(first, across, rest, row, col, out, cols, rows):
    second = invert_half(rest[...], cols, rows)
    corner = -dot_full(across[...], second)
    top = first[...] - dot_full(corner, across[...].T)
    out[:LANES, :LANES] = top * col[:LANES, :] * row[:1, :LANES]
    out[:LANES, LANES:] = corner * col[:LANES, :] * row[:1, LANES:]
    out[LANES:, :LANES] = corner.T * col[LANES:, :] * row[:1, :LANES]
    out[LANES:, LANES:] = second * col[LANES:, :] * row[:1, LANES:]


SCRATCH = [pltpu.VMEM((1024, LANES), F32), pltpu.VMEM((LANES, LANES), F32)]
HALF_FLOPS = 5_000_000_000


def invert_first(which, packed, coupling, name):
    shapes = (
        CORNER,
        CORNER,
        CORNER,
        jax.ShapeDtypeStruct((8, R), F32),
        jax.ShapeDtypeStruct((R, LANES), F32),
    )
    kernel = functools.partial(first_kernel, which)
    return call(kernel, shapes, (packed, coupling), name, SCRATCH, HALF_FLOPS)


def invert_second(parts, name):
    return call(second_kernel, SQUARE, parts, name, SCRATCH, HALF_FLOPS)


def half_index():
    return lax.axis_index("group") // 2


def no_index():
    return 0


def level_solve_kernel(inverse, terms, source, x_out, root_out, y_out, side_out):
    cross = load_square(terms, CROSS)
    x = dot_full(inverse[...], cross)
    x_out[...] = x
    store_symmetric(root_out, 0, load_symmetric(terms, ROOT) - dot_t_full(cross, x))
    projected = source[:, :R]
    y_out[...] = dot_full(projected, inverse[...])
    side = source[:, R:] - dot_full(projected, x)
    count = side.shape[0]
    side_out[:count, :] = side[:, :LANES]
    side_out[count:, :] = side[:, LANES:]


def wide(x):
    high, low = split2(x)
    return jnp.concatenate([high, high, low], axis=1)


def tall(x):
    high, low = split2(x)
    return jnp.concatenate([high, low, high], axis=0)


def by_tiles(rows, out, stage, sems, value):
    tiles = rows // TILE

    def copy(tile):
        return pltpu.make_async_copy(stage.at[tile_at(tile)], out.at[tile_at(tile)], sems.at[tile])

    def step(tile, carry):
        stage[tile_at(tile), :] = value(tile_at(tile))
        copy(tile).start()
        return carry

    lax.fori_loop(0, tiles, step, 0)
    for tile in range(tiles):
        copy(tile).wait()


def panel_kernel(b2, b1, x, out, stage, sems):
    right = tall(x[...])
    by_tiles(b2.shape[0], out, stage, sems, lambda at: b1[at, :] - dot(wide(b2[at, :]), right))


def field_kernel(b2, panel, sources, inverse, solved, out, stage, sems):
    weights = dot(wide(solved[:, R:]), tall(inverse[...])).T
    right = jnp.concatenate([tall(solved[:, :R].T), tall(weights)], axis=0)

    def value(at):
        left = jnp.concatenate([wide(b2[at, :]), wide(panel[at, :])], axis=1)
        return sources[at, :] - dot(left, right)

    by_tiles(b2.shape[0], out, stage, sems, value)


def update(kernel, args, passes, name):
    rows = args[0].shape[0]
    return pl.pallas_call(
        kernel,
        out_specs=pl.BlockSpec(memory_space=pl.ANY),
        out_shape=jax.ShapeDtypeStruct((rows, R), F32),
        scratch_shapes=[pltpu.VMEM((rows, R), F32), pltpu.SemaphoreType.DMA((rows // TILE,))],
        compiler_params=pltpu.CompilerParams(vmem_limit_bytes=VMEM_LIMIT),
        cost_estimate=cost(passes, rows, 3),
        name=name,
    )(*args)


def exchange(x, mask):
    count = lax.axis_size(AXES)
    return lax.ppermute(x, AXES, [(i, i ^ mask) for i in range(count)])


def rows_of(x, bit_value):
    half = half_of(x.shape[0])
    return lax.dynamic_slice_in_dim(x, bit_value * (x.shape[0] - half), half, 0)


def scatter_sum(x, index, bit):
    mine = (index >> bit) & 1
    return rows_of(x, mine) + exchange(rows_of(x, 1 - mine), 1 << bit)


def join(x, other, rows, index, bit):
    mine = (index >> bit) & 1
    low = jnp.where(mine == 0, x, other)
    high = jnp.where(mine == 0, other, x)
    return jnp.concatenate([low[: rows - x.shape[0]], high], axis=0)


def gather(x, rows, index, bit):
    return join(x, exchange(x, 1 << bit), rows, index, bit)


def per_device(q_two, q_one, sources, coupling_two, coupling_one):
    index = lax.axis_index(AXES)
    leaf_bits = list(range(2, lax.axis_size("leaf").bit_length() + 1))
    panel_order = source_order = leaf_bits

    def after(x, *others):
        return lax.optimization_barrier((x,) + others)[0]

    def half_rows(terms):
        return rows_of(terms, index & 1)

    keep, send, b2, b1 = panel_gram(q_two, q_one)
    arriving = exchange(send, 1)
    source_keep, source_send = source_gram(b2, b1, sources)
    arriving, source_send = lax.optimization_barrier((arriving, source_send))
    terms = keep + arriving
    source = source_keep + exchange(source_send, 1)
    sizes, source_sizes = [], []
    source_left = list(source_order)

    def source_start(source):
        bit = source_left.pop(0)
        mine = (index >> bit) & 1
        source_sizes.append(source.shape[0])
        return rows_of(source, mine), exchange(rows_of(source, 1 - mine), 1 << bit)

    for step, bit in enumerate(panel_order):
        sizes.append(terms.shape[0])
        terms = scatter_sum(terms, index, bit)
        if step == 0:
            terms, source = lax.optimization_barrier((terms, source))
            kept, flying = source_start(source)
    terms, flying = lax.optimization_barrier((terms, flying))
    source = kept + flying
    for step, bit in reversed(list(enumerate(panel_order))):
        if step == 0:
            terms, source = lax.optimization_barrier((terms, source))
            kept, flying = source_start(source)
        terms = gather(terms, sizes[step], index, bit)
    terms, flying = lax.optimization_barrier((terms, flying))
    source = kept + flying
    terms = gather(terms, PANEL_TERMS, index, 0)
    kept, flying = source_start(after(source, terms))
    flying = (kept, flying)

    parts = invert_first(half_index, terms, coupling_two, "level_first")
    source = flying[0] + after(flying[1], *parts)
    while source_left:
        kept, flying = source_start(source)
        source = kept + flying
    inverse = invert_second(parts, "level_second")
    count = source.shape[0]
    shapes = (
        SQUARE,
        jax.ShapeDtypeStruct((SYMMETRIC, LANES), F32),
        jax.ShapeDtypeStruct((count, R), F32),
        jax.ShapeDtypeStruct((2 * count, LANES), F32),
    )
    x, root, y, side = call(level_solve_kernel, shapes, (inverse, terms, source), "level_solve")
    both = jnp.concatenate([half_rows(root), side], axis=0)
    arriving = exchange(both, 2)
    panel_one = update(panel_kernel, [b2, b1, x], 3, "panel")
    arriving, panel_one = lax.optimization_barrier((arriving, panel_one))
    both = both + arriving
    root, side = both[: -2 * count], both[-2 * count :]
    solved = jnp.concatenate([y, side[:count], side[count:]], axis=1)

    back = list(zip(reversed(source_order), reversed(source_sizes)))
    *early, (middle_bit, middle_size), (last_bit, last_size) = back
    for bit, rows in early:
        solved = gather(solved, rows, index, bit)
    root = gather(root, SYMMETRIC, index, 0)
    solved_arriving = exchange(solved, 1 << middle_bit)
    parts = invert_first(no_index, root, coupling_one[None], "root_first")
    solved = join(solved, after(solved_arriving, *parts), middle_size, index, middle_bit)
    solved_arriving = exchange(solved, 1 << last_bit)
    inverse = invert_second(parts, "root_second")
    solved = join(solved, after(solved_arriving, inverse), last_size, index, last_bit)
    solved = gather(solved, R, index, 0)
    solution = update(field_kernel, [b2, panel_one, sources, inverse, solved], 6, "field")
    return (panel_one, solution)


def solution(mesh):
    placed = P(("group", "leaf"), None)
    return jax.shard_map(
        per_device,
        mesh=mesh,
        in_specs=(placed, placed, placed, P(), P()),
        out_specs=(placed, placed),
        check_vma=False,
    )
```

```python
import functools

import jax
import jax.numpy as jnp
from jax import lax
from jax.experimental import pallas as pl
from jax.experimental.pallas import tpu as pltpu
from jax.sharding import PartitionSpec as P

HIGH = lax.Precision.HIGHEST
AXES = ("leaf", "group")
F32 = jnp.float32
BF16 = jnp.bfloat16
R = 256
LANES = 128
TILE = 512
VMEM_LIMIT = 16 * 1024 * 1024
SYMMETRIC, FULL = 264, 512
OWN, ROOT, CROSS, PANEL_TERMS = 0, 264, 528, 1040


def split2(x):
    high = x.astype(BF16)
    return high, (x - high.astype(F32)).astype(BF16)


def split3(x):
    high = x.astype(BF16)
    rest = x - high.astype(F32)
    mid = rest.astype(BF16)
    return high, mid, (rest - mid.astype(F32)).astype(BF16)


def dot(left, right):
    return jnp.dot(left, right, preferred_element_type=F32)


def dot_t(left, right):
    return lax.dot_general(left, right, (((0,), (0,)), ((), ())), preferred_element_type=F32)


def dot_full(left, right):
    return jnp.dot(left, right, precision=HIGH, preferred_element_type=F32)


def dot_t_full(left, right):
    return lax.dot_general(
        left, right, (((0,), (0,)), ((), ())), precision=HIGH, preferred_element_type=F32
    )


def square_index():
    row = lax.broadcasted_iota(jnp.int32, (LANES, LANES), 0)
    return row, lax.broadcasted_iota(jnp.int32, (LANES, LANES), 1)


def store_symmetric(ref, at, block):
    row, col = square_index()
    last = block[128:, 128:]
    ref[at : at + 128, :] = block[128:, :128]
    ref[at + 128 : at + 256, :] = jnp.where(row >= col, block[:128, :128], last)
    diagonal = jnp.sum(jnp.where(row == col, last, 0.0), axis=0, keepdims=True)
    ref[at + 256 : at + 264, :] = jnp.broadcast_to(diagonal, (8, LANES))


def store_square(ref, row, block):
    ref[row : row + 256, :] = block[:, :128]
    ref[row + 256 : row + 512, :] = block[:, 128:]


def load_symmetric(ref, at):
    row, col = square_index()
    lower = ref[at : at + 128, :]
    mixed = ref[at + 128 : at + 256, :]
    turned = mixed.T
    first = jnp.where(row >= col, mixed, turned)
    last = jnp.where(row < col, mixed, turned)
    last = jnp.where(row == col, ref[at + 256 : at + 257, :], last)
    top = jnp.concatenate([first, lower.T], axis=1)
    return jnp.concatenate([top, jnp.concatenate([lower, last], axis=1)], axis=0)


def load_square(ref, row):
    return jnp.concatenate([ref[row : row + 256, :], ref[row + 256 : row + 512, :]], axis=1)


def half_of(rows):
    return (rows + 15) // 16 * 8


def store_halves(packed, keep, send):
    half = half_of(packed.shape[0])
    far = packed.shape[0] - half
    mine = lax.rem(lax.axis_index("group"), 2)
    keep[...] = packed[pl.ds(pl.multiple_of(mine * far, 8), half), :]
    send[...] = packed[pl.ds(pl.multiple_of((1 - mine) * far, 8), half), :]


def tile_at(tile):
    return pl.ds(pl.multiple_of(tile * TILE, TILE), TILE)


def panel_gram_kernel(q_two, q_one, keep, send, b2, b1, acc, packed, sems):
    tiles = b2.shape[0] // TILE
    pairs = ((q_two, b2), (q_one, b1))

    def copy(tile, which):
        source, target = pairs[which]
        here = tile_at(tile)
        return pltpu.make_async_copy(source.at[here], target.at[here], sems.at[which, tile])

    for tile in range(tiles):
        for which in range(2):
            copy(tile, which).start()
    acc[...] = jnp.zeros_like(acc)

    def step(tile, carry):
        for which in range(2):
            copy(tile, which).wait()
        h2, l2 = split2(b2[tile_at(tile), :])
        h1, l1 = split2(b1[tile_at(tile), :])
        h2t, l2t, h1t = h2.T, l2.T, h1.T
        acc[0] += dot(h2t, h2)
        acc[1] += dot(h2t, l2)
        left = jnp.concatenate([h2t, h2t, l2t], axis=1)
        acc[2] += dot(left, jnp.concatenate([h1, l1, h1], axis=0))
        acc[3] += dot(h1t, h1)
        acc[4] += dot(h1t, l1)
        return carry

    lax.fori_loop(0, tiles, step, 0)
    low = acc[1]
    store_symmetric(packed, OWN, acc[0] + low + low.T)
    low = acc[4]
    store_symmetric(packed, ROOT, acc[3] + low + low.T)
    store_square(packed, CROSS, acc[2])
    packed[PANEL_TERMS:, :] = jnp.zeros((packed.shape[0] - PANEL_TERMS, LANES), F32)
    store_halves(packed, keep, send)


def source_gram_kernel(b2, b1, sources, keep, send, acc):
    acc[...] = jnp.zeros_like(acc)

    def step(tile, carry):
        high, low = split2(sources[tile_at(tile), :])
        turned = high.T
        left = jnp.concatenate([turned, turned, low.T], axis=1)
        acc[:, :R] += dot(left, tall(b2[tile_at(tile), :]))
        acc[:, R:] += dot(left, tall(b1[tile_at(tile), :]))
        return carry

    lax.fori_loop(0, b2.shape[0] // TILE, step, 0)
    store_halves(acc, keep, send)


def cost(passes, rows, arrays):
    return pl.CostEstimate(
        flops=2 * passes * rows * R * R, bytes_accessed=4 * arrays * rows * R, transcendentals=0
    )


def panel_gram(q_two, q_one, shares):
    rows = q_two.shape[0]
    half = (PANEL_TERMS + 16 * shares - 1) // (16 * shares) * 8 * shares
    part = jax.ShapeDtypeStruct((half, LANES), F32)
    tall = jax.ShapeDtypeStruct((rows, R), F32)
    return pl.pallas_call(
        panel_gram_kernel,
        in_specs=[pl.BlockSpec(memory_space=pl.ANY)] * 2,
        out_shape=(part, part, tall, tall),
        scratch_shapes=[
            pltpu.VMEM((5, R, R), F32),
            pltpu.VMEM((2 * half, LANES), F32),
            pltpu.SemaphoreType.DMA((2, rows // TILE)),
        ],
        compiler_params=pltpu.CompilerParams(vmem_limit_bytes=VMEM_LIMIT),
        cost_estimate=cost(7, rows, 2),
        name="panel_gram",
    )(pltpu.with_memory_space_constraint(q_two, pltpu.HBM), pltpu.with_memory_space_constraint(q_one, pltpu.HBM))


def source_gram(b2, b1, sources):
    part = jax.ShapeDtypeStruct((half_of(R), 2 * R), F32)
    return pl.pallas_call(
        source_gram_kernel,
        out_shape=(part, part),
        scratch_shapes=[pltpu.VMEM((R, 2 * R), F32)],
        compiler_params=pltpu.CompilerParams(vmem_limit_bytes=VMEM_LIMIT),
        cost_estimate=cost(6, b2.shape[0], 3),
        name="source_gram",
    )(b2, b1, sources)


def spread_lane(x, lane):
    return jnp.broadcast_to(x[:, lane : lane + 1], (8, LANES))


def eliminate(block, cols, rows):
    count = len(block)
    lane = lax.broadcasted_iota(jnp.int32, (8, LANES), 1)
    for start in range(0, count, 4):
        panel = block[start : start + 4]
        left = stack_left(jnp.concatenate(panel, axis=0))
        for t in range(4):
            panel = eliminate_group(panel, t, start + t, cols, rows)
        inside = (lane >= 8 * start) & (lane < 8 * start + 32)
        panel = [jnp.where(inside, -x, x) for x in panel]
        change = dot_t(left, stack_right(jnp.concatenate(panel, axis=0)))
        for g in range(count):
            if start <= g < start + 4:
                block[g] = panel[g - start]
            else:
                block[g] = jnp.where(inside, 0.0, block[g]) - change[8 * g : 8 * g + 8, :]
    return [-x for x in block]


def eliminate_group(panel, t, at, cols, rows):
    lane = lax.broadcasted_iota(jnp.int32, (8, LANES), 1)
    sub = lax.broadcasted_iota(jnp.int32, (8, LANES), 0)
    for j in range(8):
        cols[64 * at + 8 * j : 64 * at + 8 * j + 8, :] = spread_lane(panel[t], 8 * at + j)
    rows[8 * at : 8 * at + 8, :] = panel[t]
    entry = {}
    for i in range(8):
        for j in range(i + 1):
            row = 64 * at + 8 * j + i
            entry[i, j] = jnp.broadcast_to(cols[row : row + 1, :], (8, LANES))
    inside = (lane >= 8 * at) & (lane < 8 * at + 8)
    line = []
    for j in range(8):
        row = jnp.broadcast_to(rows[8 * at + j : 8 * at + j + 1, :], (8, LANES))
        line.append(jnp.where(inside, jnp.where(lane == 8 * at + j, 1.0, 0.0), row))
    line = solve_small(entry, line)
    for g in range(4):
        if g != t:
            terms = [spread_lane(panel[g], 8 * at + j) * line[j] for j in range(8)]
            panel[g] = jnp.where(inside, 0.0, panel[g]) - tree_sum(terms)
    merged = line[0]
    for j in range(1, 8):
        merged = jnp.where(sub == j, line[j], merged)
    panel[t] = merged
    return panel


def tree_sum(terms):
    while len(terms) > 1:
        terms = [
            terms[i] + terms[i + 1] if i + 1 < len(terms) else terms[i]
            for i in range(0, len(terms), 2)
        ]
    return terms[0]


def solve_small(entry, line):
    factors, pivots = {}, {}
    for k in range(0, 8, 2):
        a, b, c = entry[k, k], entry[k + 1, k], entry[k + 1, k + 1]
        inv = pl.reciprocal(a * c - b * b, approx=True)
        e, f, g = c * inv, b * inv, a * inv
        pivots[k] = (e, f, g)
        for i in range(k + 2, 8):
            u, v = entry[i, k], entry[i, k + 1]
            factors[i, k] = (e * u - f * v, g * v - f * u)
        for i in range(k + 2, 8):
            u, v = entry[i, k], entry[i, k + 1]
            for j in range(k + 2, i + 1):
                m, n = factors[j, k]
                entry[i, j] = entry[i, j] - (u * m + v * n)
        for i in range(k + 2, 8):
            m, n = factors[i, k]
            line[i] = line[i] - (m * line[k] + n * line[k + 1])
    for k in range(6, -1, -2):
        e, f, g = pivots[k]
        x, y = e * line[k] - f * line[k + 1], g * line[k + 1] - f * line[k]
        if k < 6:
            x = x - tree_sum([factors[i, k][0] * line[i] for i in range(k + 2, 8)])
            y = y - tree_sum([factors[i, k][1] * line[i] for i in range(k + 2, 8)])
        line[k], line[k + 1] = x, y
    return line


def stack_left(x):
    h, m, l = split3(x)
    return jnp.concatenate([h, h, m, h, l, m], axis=0)


def stack_right(x):
    h, m, l = split3(x)
    return jnp.concatenate([h, m, h, l, h, m], axis=0)


def invert_half(matrix, cols, rows):
    block = eliminate([matrix[8 * i : 8 * i + 8, :] for i in range(LANES // 8)], cols, rows)
    return jnp.concatenate(block, axis=0)


SQUARE = jax.ShapeDtypeStruct((R, R), F32)
CORNER = jax.ShapeDtypeStruct((LANES, LANES), F32)


def call(kernel, out_shape, args, name, scratch=(), flops=0):
    return pl.pallas_call(
        kernel,
        out_shape=out_shape,
        scratch_shapes=list(scratch),
        compiler_params=pltpu.CompilerParams(vmem_limit_bytes=VMEM_LIMIT),
        cost_estimate=pl.CostEstimate(flops=flops, bytes_accessed=R * R * 4, transcendentals=0),
        name=name,
    )(*args)


def first_kernel(which, gram_ref, coupling, first_out, across_out, rest_out, row_out, col_out, cols, rows):
    matrix = coupling[which()] + load_symmetric(gram_ref, OWN)
    eye = lax.broadcasted_iota(jnp.int32, (R, R), 0) == lax.broadcasted_iota(jnp.int32, (R, R), 1)
    diagonal = jnp.where(eye, matrix, 0.0)
    scale_row = lax.rsqrt(jnp.sum(diagonal, axis=0, keepdims=True))
    scale_col = lax.rsqrt(jnp.sum(diagonal, axis=1, keepdims=True))
    matrix = matrix * scale_col * scale_row
    side = matrix[:LANES, LANES:]
    first = invert_half(matrix[:LANES, :LANES], cols, rows)
    across = dot_full(first, side)
    first_out[...] = first
    across_out[...] = across
    rest_out[...] = matrix[LANES:, LANES:] - dot_t_full(side, across)
    row_out[...] = jnp.broadcast_to(scale_row, (8, R))
    col_out[...] = jnp.broadcast_to(scale_col, (R, LANES))


def second_kernel(first, across, rest, row, col, out, cols, rows):
    second = invert_half(rest[...], cols, rows)
    corner = -dot_full(across[...], second)
    top = first[...] - dot_full(corner, across[...].T)
    out[:LANES, :LANES] = top * col[:LANES, :] * row[:1, :LANES]
    out[:LANES, LANES:] = corner * col[:LANES, :] * row[:1, LANES:]
    out[LANES:, :LANES] = corner.T * col[LANES:, :] * row[:1, :LANES]
    out[LANES:, LANES:] = second * col[LANES:, :] * row[:1, LANES:]


SCRATCH = [pltpu.VMEM((1024, LANES), F32), pltpu.VMEM((LANES, LANES), F32)]
HALF_FLOPS = 5_000_000_000


def invert_first(which, packed, coupling, name):
    shapes = (
        CORNER,
        CORNER,
        CORNER,
        jax.ShapeDtypeStruct((8, R), F32),
        jax.ShapeDtypeStruct((R, LANES), F32),
    )
    kernel = functools.partial(first_kernel, which)
    return call(kernel, shapes, (packed, coupling), name, SCRATCH, HALF_FLOPS)


def invert_second(parts, name):
    return call(second_kernel, SQUARE, parts, name, SCRATCH, HALF_FLOPS)


def half_index():
    return lax.axis_index("group") // 2


def no_index():
    return 0


def level_solve_kernel(inverse, terms, source, x_out, root_out, y_out, side_out):
    cross = load_square(terms, CROSS)
    x = dot_full(inverse[...], cross)
    x_out[...] = x
    store_symmetric(root_out, 0, load_symmetric(terms, ROOT) - dot_t_full(cross, x))
    projected = source[:, :R]
    y_out[...] = dot_full(projected, inverse[...])
    side = source[:, R:] - dot_full(projected, x)
    count = side.shape[0]
    side_out[:count, :] = side[:, :LANES]
    side_out[count:, :] = side[:, LANES:]


def wide(x):
    high, low = split2(x)
    return jnp.concatenate([high, high, low], axis=1)


def tall(x):
    high, low = split2(x)
    return jnp.concatenate([high, low, high], axis=0)


def by_tiles(rows, out, stage, sems, value):
    tiles = rows // TILE

    def copy(tile):
        return pltpu.make_async_copy(stage.at[tile_at(tile)], out.at[tile_at(tile)], sems.at[tile])

    def step(tile, carry):
        stage[tile_at(tile), :] = value(tile_at(tile))
        copy(tile).start()
        return carry

    lax.fori_loop(0, tiles, step, 0)
    for tile in range(tiles):
        copy(tile).wait()


def panel_kernel(b2, b1, x, out, stage, sems):
    right = tall(x[...])
    by_tiles(b2.shape[0], out, stage, sems, lambda at: b1[at, :] - dot(wide(b2[at, :]), right))


def field_kernel(b2, panel, sources, inverse, solved, out, stage, sems):
    weights = dot(wide(solved[:, R:]), tall(inverse[...])).T
    right = jnp.concatenate([tall(solved[:, :R].T), tall(weights)], axis=0)

    def value(at):
        left = jnp.concatenate([wide(b2[at, :]), wide(panel[at, :])], axis=1)
        return sources[at, :] - dot(left, right)

    by_tiles(b2.shape[0], out, stage, sems, value)


def update(kernel, args, passes, name):
    rows = args[0].shape[0]
    return pl.pallas_call(
        kernel,
        out_specs=pl.BlockSpec(memory_space=pl.ANY),
        out_shape=jax.ShapeDtypeStruct((rows, R), F32),
        scratch_shapes=[pltpu.VMEM((rows, R), F32), pltpu.SemaphoreType.DMA((rows // TILE,))],
        compiler_params=pltpu.CompilerParams(vmem_limit_bytes=VMEM_LIMIT),
        cost_estimate=cost(passes, rows, 3),
        name=name,
    )(*args)


def exchange(x, mask):
    count = lax.axis_size(AXES)
    return lax.ppermute(x, AXES, [(i, i ^ mask) for i in range(count)])


def rows_of(x, bit_value):
    half = half_of(x.shape[0])
    return lax.dynamic_slice_in_dim(x, bit_value * (x.shape[0] - half), half, 0)


def scatter_sum(x, index, bit):
    mine = (index >> bit) & 1
    return rows_of(x, mine) + exchange(rows_of(x, 1 - mine), 1 << bit)


def join(x, other, rows, index, bit):
    mine = (index >> bit) & 1
    low = jnp.where(mine == 0, x, other)
    high = jnp.where(mine == 0, other, x)
    return jnp.concatenate([low[: rows - x.shape[0]], high], axis=0)


def gather(x, rows, index, bit):
    return join(x, exchange(x, 1 << bit), rows, index, bit)


def per_device(q_two, q_one, sources, coupling_two, coupling_one):
    index = lax.axis_index(AXES)
    leaf_bits = list(range(2, lax.axis_size("leaf").bit_length() + 1))
    source_order = leaf_bits

    def after(x, *others):
        return lax.optimization_barrier((x,) + others)[0]

    def half_rows(terms):
        return rows_of(terms, index & 1)

    leaves = lax.axis_size("leaf")
    keep, send, b2, b1 = panel_gram(q_two, q_one, leaves)
    arriving = exchange(send, 1)
    source_keep, source_send = source_gram(b2, b1, sources)
    arriving, source_send = lax.optimization_barrier((arriving, source_send))
    terms = keep + arriving
    flying = exchange(source_send, 1)
    shares = lax.all_to_all(terms.reshape(leaves, -1, LANES), "leaf", 0, 0)
    shares, flying = lax.optimization_barrier((shares, flying))
    source = source_keep + flying
    source_sizes = []
    source_left = list(source_order)

    def source_start(source):
        bit = source_left.pop(0)
        mine = (index >> bit) & 1
        source_sizes.append(source.shape[0])
        return rows_of(source, mine), exchange(rows_of(source, 1 - mine), 1 << bit)

    kept, flying = source_start(source)
    share = jnp.sum(shares, axis=0)
    shares = lax.all_to_all(jnp.broadcast_to(share[None], shares.shape), "leaf", 0, 0)
    shares, flying = lax.optimization_barrier((shares, flying))
    source = kept + flying
    kept, flying = source_start(source)
    terms = shares.reshape(-1, LANES)
    terms = gather(terms, 2 * terms.shape[0], index, 0)
    flying = (kept, flying)

    parts = invert_first(half_index, terms, coupling_two, "level_first")
    flying, parts = lax.optimization_barrier((flying, parts))
    source = flying[0] + flying[1]
    kept, flying = source_start(source)
    inverse = invert_second(parts, "level_second")
    flying, inverse = lax.optimization_barrier((flying, inverse))
    source = kept + flying
    while source_left:
        kept, flying = source_start(source)
        source = kept + flying
    count = source.shape[0]
    shapes = (
        SQUARE,
        jax.ShapeDtypeStruct((SYMMETRIC, LANES), F32),
        jax.ShapeDtypeStruct((count, R), F32),
        jax.ShapeDtypeStruct((2 * count, LANES), F32),
    )
    x, root, y, side = call(level_solve_kernel, shapes, (inverse, terms, source), "level_solve")
    both = jnp.concatenate([half_rows(root), side], axis=0)
    arriving = exchange(both, 2)
    panel_one = update(panel_kernel, [b2, b1, x], 3, "panel")
    arriving, panel_one = lax.optimization_barrier((arriving, panel_one))
    both = both + arriving
    root, side = both[: -2 * count], both[-2 * count :]
    solved = jnp.concatenate([y, side[:count], side[count:]], axis=1)

    back = list(zip(reversed(source_order), reversed(source_sizes)))
    *early, (middle_bit, middle_size), (last_bit, last_size) = back
    for bit, rows in early:
        solved = gather(solved, rows, index, bit)
    root = gather(root, SYMMETRIC, index, 0)
    solved_arriving = exchange(solved, 1 << middle_bit)
    parts = invert_first(no_index, root, coupling_one[None], "root_first")
    solved = join(solved, after(solved_arriving, *parts), middle_size, index, middle_bit)
    solved_arriving = exchange(solved, 1 << last_bit)
    inverse = invert_second(parts, "root_second")
    solved = join(solved, after(solved_arriving, inverse), last_size, index, last_bit)
    solved = gather(solved, R, index, 0)
    solution = update(field_kernel, [b2, panel_one, sources, inverse, solved], 6, "field")
    return (panel_one, solution)


def solution(mesh):
    placed = P(("group", "leaf"), None)
    return jax.shard_map(
        per_device,
        mesh=mesh,
        in_specs=(placed, placed, placed, P(), P()),
        out_specs=(placed, placed),
        check_vma=False,
    )
```

```python
import functools

import jax
import jax.numpy as jnp
from jax import lax
from jax.experimental import pallas as pl
from jax.experimental.pallas import tpu as pltpu
from jax.sharding import PartitionSpec as P

HIGH = lax.Precision.HIGHEST
AXES = ("leaf", "group")
F32 = jnp.float32
BF16 = jnp.bfloat16
R = 256
LANES = 128
TILE = 512
VMEM_LIMIT = 16 * 1024 * 1024
SYMMETRIC, FULL = 264, 512
OWN, ROOT, CROSS, PANEL_TERMS = 0, 264, 528, 1040
PROJECTED, SIDE, SOURCE_TERMS = 0, 512, 1024


def split2(x):
    high = x.astype(BF16)
    return high, (x - high.astype(F32)).astype(BF16)


def split3(x):
    high = x.astype(BF16)
    rest = x - high.astype(F32)
    mid = rest.astype(BF16)
    return high, mid, (rest - mid.astype(F32)).astype(BF16)


def dot(left, right):
    return jnp.dot(left, right, preferred_element_type=F32)


def dot_t(left, right):
    return lax.dot_general(left, right, (((0,), (0,)), ((), ())), preferred_element_type=F32)


def dot_full(left, right):
    return jnp.dot(left, right, precision=HIGH, preferred_element_type=F32)


def dot_t_full(left, right):
    return lax.dot_general(
        left, right, (((0,), (0,)), ((), ())), precision=HIGH, preferred_element_type=F32
    )


def square_index():
    row = lax.broadcasted_iota(jnp.int32, (LANES, LANES), 0)
    return row, lax.broadcasted_iota(jnp.int32, (LANES, LANES), 1)


def store_symmetric(ref, at, block):
    row, col = square_index()
    last = block[128:, 128:]
    ref[at : at + 128, :] = block[128:, :128]
    ref[at + 128 : at + 256, :] = jnp.where(row >= col, block[:128, :128], last)
    diagonal = jnp.sum(jnp.where(row == col, last, 0.0), axis=0, keepdims=True)
    ref[at + 256 : at + 264, :] = jnp.broadcast_to(diagonal, (8, LANES))


def store_square(ref, row, block):
    ref[row : row + 256, :] = block[:, :128]
    ref[row + 256 : row + 512, :] = block[:, 128:]


def load_symmetric(ref, at):
    row, col = square_index()
    lower = ref[at : at + 128, :]
    mixed = ref[at + 128 : at + 256, :]
    turned = mixed.T
    first = jnp.where(row >= col, mixed, turned)
    last = jnp.where(row < col, mixed, turned)
    last = jnp.where(row == col, ref[at + 256 : at + 257, :], last)
    top = jnp.concatenate([first, lower.T], axis=1)
    return jnp.concatenate([top, jnp.concatenate([lower, last], axis=1)], axis=0)


def load_square(ref, row):
    return jnp.concatenate([ref[row : row + 256, :], ref[row + 256 : row + 512, :]], axis=1)


def half_of(rows):
    return (rows + 15) // 16 * 8


def store_halves(packed, keep, send):
    half = half_of(packed.shape[0])
    far = packed.shape[0] - half
    mine = lax.rem(lax.axis_index("group"), 2)
    keep[...] = packed[pl.ds(pl.multiple_of(mine * far, 8), half), :]
    send[...] = packed[pl.ds(pl.multiple_of((1 - mine) * far, 8), half), :]


def tile_at(tile):
    return pl.ds(pl.multiple_of(tile * TILE, TILE), TILE)


def panel_gram_kernel(q_two, q_one, keep, send, b2, b1, acc, packed, sems):
    tiles = b2.shape[0] // TILE
    pairs = ((q_two, b2), (q_one, b1))

    def copy(tile, which):
        source, target = pairs[which]
        here = tile_at(tile)
        return pltpu.make_async_copy(source.at[here], target.at[here], sems.at[which, tile])

    for tile in range(tiles):
        for which in range(2):
            copy(tile, which).start()
    acc[...] = jnp.zeros_like(acc)

    def step(tile, carry):
        for which in range(2):
            copy(tile, which).wait()
        h2, l2 = split2(b2[tile_at(tile), :])
        h1, l1 = split2(b1[tile_at(tile), :])
        h2t, l2t, h1t = h2.T, l2.T, h1.T
        acc[0] += dot(h2t, h2)
        acc[1] += dot(h2t, l2)
        left = jnp.concatenate([h2t, h2t, l2t], axis=1)
        acc[2] += dot(left, jnp.concatenate([h1, l1, h1], axis=0))
        acc[3] += dot(h1t, h1)
        acc[4] += dot(h1t, l1)
        return carry

    lax.fori_loop(0, tiles, step, 0)
    low = acc[1]
    store_symmetric(packed, OWN, acc[0] + low + low.T)
    low = acc[4]
    store_symmetric(packed, ROOT, acc[3] + low + low.T)
    store_square(packed, CROSS, acc[2])
    store_halves(packed, keep, send)


def source_gram_kernel(b2, b1, sources, keep, send, acc, packed):
    acc[...] = jnp.zeros_like(acc)

    def step(tile, carry):
        hs, ls = split2(sources[tile_at(tile), :])
        right = jnp.concatenate([hs, ls, hs], axis=0)
        for which, panel in enumerate((b2, b1)):
            high, low = split2(panel[tile_at(tile), :])
            turned = high.T
            acc[which] += dot(jnp.concatenate([turned, turned, low.T], axis=1), right)
        return carry

    lax.fori_loop(0, b2.shape[0] // TILE, step, 0)
    store_square(packed, PROJECTED, acc[0])
    store_square(packed, SIDE, acc[1])
    store_halves(packed, keep, send)


def cost(passes, rows, arrays):
    return pl.CostEstimate(
        flops=2 * passes * rows * R * R, bytes_accessed=4 * arrays * rows * R, transcendentals=0
    )


def panel_gram(q_two, q_one):
    rows = q_two.shape[0]
    part = jax.ShapeDtypeStruct((half_of(PANEL_TERMS), LANES), F32)
    tall = jax.ShapeDtypeStruct((rows, R), F32)
    return pl.pallas_call(
        panel_gram_kernel,
        in_specs=[pl.BlockSpec(memory_space=pl.ANY)] * 2,
        out_shape=(part, part, tall, tall),
        scratch_shapes=[
            pltpu.VMEM((5, R, R), F32),
            pltpu.VMEM((PANEL_TERMS, LANES), F32),
            pltpu.SemaphoreType.DMA((2, rows // TILE)),
        ],
        compiler_params=pltpu.CompilerParams(vmem_limit_bytes=VMEM_LIMIT),
        cost_estimate=cost(7, rows, 2),
        name="panel_gram",
    )(pltpu.with_memory_space_constraint(q_two, pltpu.HBM), pltpu.with_memory_space_constraint(q_one, pltpu.HBM))


def source_gram(b2, b1, sources):
    part = jax.ShapeDtypeStruct((half_of(SOURCE_TERMS), LANES), F32)
    return pl.pallas_call(
        source_gram_kernel,
        out_shape=(part, part),
        scratch_shapes=[pltpu.VMEM((2, R, R), F32), pltpu.VMEM((SOURCE_TERMS, LANES), F32)],
        compiler_params=pltpu.CompilerParams(vmem_limit_bytes=VMEM_LIMIT),
        cost_estimate=cost(6, b2.shape[0], 3),
        name="source_gram",
    )(b2, b1, sources)


def spread_lane(x, lane):
    return jnp.broadcast_to(x[:, lane : lane + 1], (8, LANES))


def eliminate(block, cols, rows):
    count = len(block)
    lane = lax.broadcasted_iota(jnp.int32, (8, LANES), 1)
    for start in range(0, count, 4):
        panel = block[start : start + 4]
        left = stack_left(jnp.concatenate(panel, axis=0))
        for t in range(4):
            panel = eliminate_group(panel, t, start + t, cols, rows)
        inside = (lane >= 8 * start) & (lane < 8 * start + 32)
        panel = [jnp.where(inside, -x, x) for x in panel]
        change = dot_t(left, stack_right(jnp.concatenate(panel, axis=0)))
        for g in range(count):
            if start <= g < start + 4:
                block[g] = panel[g - start]
            else:
                block[g] = jnp.where(inside, 0.0, block[g]) - change[8 * g : 8 * g + 8, :]
    return [-x for x in block]


def eliminate_group(panel, t, at, cols, rows):
    lane = lax.broadcasted_iota(jnp.int32, (8, LANES), 1)
    sub = lax.broadcasted_iota(jnp.int32, (8, LANES), 0)
    for j in range(8):
        cols[64 * at + 8 * j : 64 * at + 8 * j + 8, :] = spread_lane(panel[t], 8 * at + j)
    rows[8 * at : 8 * at + 8, :] = panel[t]
    entry = {}
    for i in range(8):
        for j in range(i + 1):
            row = 64 * at + 8 * j + i
            entry[i, j] = jnp.broadcast_to(cols[row : row + 1, :], (8, LANES))
    inside = (lane >= 8 * at) & (lane < 8 * at + 8)
    line = []
    for j in range(8):
        row = jnp.broadcast_to(rows[8 * at + j : 8 * at + j + 1, :], (8, LANES))
        line.append(jnp.where(inside, jnp.where(lane == 8 * at + j, 1.0, 0.0), row))
    line = solve_small(entry, line)
    for g in range(4):
        if g != t:
            terms = [spread_lane(panel[g], 8 * at + j) * line[j] for j in range(8)]
            panel[g] = jnp.where(inside, 0.0, panel[g]) - tree_sum(terms)
    merged = line[0]
    for j in range(1, 8):
        merged = jnp.where(sub == j, line[j], merged)
    panel[t] = merged
    return panel


def tree_sum(terms):
    while len(terms) > 1:
        terms = [
            terms[i] + terms[i + 1] if i + 1 < len(terms) else terms[i]
            for i in range(0, len(terms), 2)
        ]
    return terms[0]


def solve_small(entry, line):
    factors, pivots = {}, {}
    for k in range(0, 8, 2):
        a, b, c = entry[k, k], entry[k + 1, k], entry[k + 1, k + 1]
        inv = pl.reciprocal(a * c - b * b, approx=True)
        e, f, g = c * inv, b * inv, a * inv
        pivots[k] = (e, f, g)
        for i in range(k + 2, 8):
            u, v = entry[i, k], entry[i, k + 1]
            factors[i, k] = (e * u - f * v, g * v - f * u)
        for i in range(k + 2, 8):
            u, v = entry[i, k], entry[i, k + 1]
            for j in range(k + 2, i + 1):
                m, n = factors[j, k]
                entry[i, j] = entry[i, j] - (u * m + v * n)
        for i in range(k + 2, 8):
            m, n = factors[i, k]
            line[i] = line[i] - (m * line[k] + n * line[k + 1])
    for k in range(6, -1, -2):
        e, f, g = pivots[k]
        x, y = e * line[k] - f * line[k + 1], g * line[k + 1] - f * line[k]
        if k < 6:
            x = x - tree_sum([factors[i, k][0] * line[i] for i in range(k + 2, 8)])
            y = y - tree_sum([factors[i, k][1] * line[i] for i in range(k + 2, 8)])
        line[k], line[k + 1] = x, y
    return line


def stack_left(x):
    h, m, l = split3(x)
    return jnp.concatenate([h, h, m, h, l, m], axis=0)


def stack_right(x):
    h, m, l = split3(x)
    return jnp.concatenate([h, m, h, l, h, m], axis=0)


def invert_half(matrix, cols, rows):
    block = eliminate([matrix[8 * i : 8 * i + 8, :] for i in range(LANES // 8)], cols, rows)
    return jnp.concatenate(block, axis=0)


SQUARE = jax.ShapeDtypeStruct((R, R), F32)
CORNER = jax.ShapeDtypeStruct((LANES, LANES), F32)


def call(kernel, out_shape, args, name, scratch=(), flops=0):
    return pl.pallas_call(
        kernel,
        out_shape=out_shape,
        scratch_shapes=list(scratch),
        compiler_params=pltpu.CompilerParams(vmem_limit_bytes=VMEM_LIMIT),
        cost_estimate=pl.CostEstimate(flops=flops, bytes_accessed=R * R * 4, transcendentals=0),
        name=name,
    )(*args)


def first_kernel(which, gram_ref, coupling, first_out, across_out, rest_out, row_out, col_out, cols, rows):
    matrix = coupling[which()] + load_symmetric(gram_ref, OWN)
    eye = lax.broadcasted_iota(jnp.int32, (R, R), 0) == lax.broadcasted_iota(jnp.int32, (R, R), 1)
    diagonal = jnp.where(eye, matrix, 0.0)
    scale_row = lax.rsqrt(jnp.sum(diagonal, axis=0, keepdims=True))
    scale_col = lax.rsqrt(jnp.sum(diagonal, axis=1, keepdims=True))
    matrix = matrix * scale_col * scale_row
    side = matrix[:LANES, LANES:]
    first = invert_half(matrix[:LANES, :LANES], cols, rows)
    across = dot_full(first, side)
    first_out[...] = first
    across_out[...] = across
    rest_out[...] = matrix[LANES:, LANES:] - dot_t_full(side, across)
    row_out[...] = jnp.broadcast_to(scale_row, (8, R))
    col_out[...] = jnp.broadcast_to(scale_col, (R, LANES))


def second_kernel(first, across, rest, row, col, out, cols, rows):
    second = invert_half(rest[...], cols, rows)
    corner = -dot_full(across[...], second)
    top = first[...] - dot_full(corner, across[...].T)
    out[:LANES, :LANES] = top * col[:LANES, :] * row[:1, :LANES]
    out[:LANES, LANES:] = corner * col[:LANES, :] * row[:1, LANES:]
    out[LANES:, :LANES] = corner.T * col[LANES:, :] * row[:1, :LANES]
    out[LANES:, LANES:] = second * col[LANES:, :] * row[:1, LANES:]


SCRATCH = [pltpu.VMEM((1024, LANES), F32), pltpu.VMEM((LANES, LANES), F32)]
HALF_FLOPS = 5_000_000_000


def invert_first(which, packed, coupling, name):
    shapes = (
        CORNER,
        CORNER,
        CORNER,
        jax.ShapeDtypeStruct((8, R), F32),
        jax.ShapeDtypeStruct((R, LANES), F32),
    )
    kernel = functools.partial(first_kernel, which)
    return call(kernel, shapes, (packed, coupling), name, SCRATCH, HALF_FLOPS)


def invert_second(parts, name):
    return call(second_kernel, SQUARE, parts, name, SCRATCH, HALF_FLOPS)


def half_index():
    return lax.axis_index("group") // 2


def no_index():
    return 0


def panel_solve_kernel(inverse, terms, x_out, root_out):
    cross = load_square(terms, CROSS)
    x = dot_full(inverse[...], cross)
    x_out[...] = x
    store_symmetric(root_out, 0, load_symmetric(terms, ROOT) - dot_t_full(cross, x))


def wide(x):
    high, low = split2(x)
    return jnp.concatenate([high, high, low], axis=1)


def tall(x):
    high, low = split2(x)
    return jnp.concatenate([high, low, high], axis=0)


def by_tiles(rows, out, stage, sems, value, beside=None):
    tiles = rows // TILE

    def copy(tile):
        return pltpu.make_async_copy(stage.at[tile_at(tile)], out.at[tile_at(tile)], sems.at[tile])

    def step(tile, carry):
        stage[tile_at(tile), :] = value(tile_at(tile))
        copy(tile).start()
        return carry

    lax.fori_loop(0, tiles, step, 0)
    if beside is not None:
        beside()
    for tile in range(tiles):
        copy(tile).wait()


def panel_kernel(b2, b1, x, inverse, terms, out, y_out, side_out, stage, sems):
    def sources_part():
        projected = load_square(terms, PROJECTED)
        y_out[...] = dot_full(inverse[...], projected)
        store_square(side_out, 0, load_square(terms, SIDE) - dot_t_full(x[...], projected))

    right = tall(x[...])
    by_tiles(b2.shape[0], out, stage, sems, lambda at: b1[at, :] - dot(wide(b2[at, :]), right), sources_part)


def field_kernel(b2, panel, sources, inverse, side, y, out, stage, sems):
    weights = dot(wide(inverse[...]), tall(load_square(side, 0)))
    right = jnp.concatenate([tall(y[...]), tall(weights)], axis=0)

    def value(at):
        left = jnp.concatenate([wide(b2[at, :]), wide(panel[at, :])], axis=1)
        return sources[at, :] - dot(left, right)

    by_tiles(b2.shape[0], out, stage, sems, value)


def update(kernel, args, passes, name, more=()):
    rows = args[0].shape[0]
    return pl.pallas_call(
        kernel,
        out_specs=[pl.BlockSpec(memory_space=pl.ANY)] + [pl.BlockSpec(memory_space=pltpu.VMEM)] * len(more),
        out_shape=[jax.ShapeDtypeStruct((rows, R), F32), *more],
        scratch_shapes=[pltpu.VMEM((rows, R), F32), pltpu.SemaphoreType.DMA((rows // TILE,))],
        compiler_params=pltpu.CompilerParams(vmem_limit_bytes=VMEM_LIMIT),
        cost_estimate=cost(passes, rows, 3),
        name=name,
    )(*args)


def exchange(x, mask):
    count = lax.axis_size(AXES)
    return lax.ppermute(x, AXES, [(i, i ^ mask) for i in range(count)])


def choose(x, upper):
    half = half_of(x.shape[0])
    low, high = x[:half], x[x.shape[0] - half :]
    return jnp.where(upper, high, low), jnp.where(upper, low, high)


def join(x, other, rows, upper):
    low, high = jnp.where(upper, other, x), jnp.where(upper, x, other)
    return jnp.concatenate([low[: rows - x.shape[0]], high], axis=0)


def summing_stages(bits):
    down = [("scatter", bit) for bit in bits[:-1]]
    return down + [("sum", bits[-1])] + [("gather", bit) for bit in reversed(bits[:-1])]


class Chain:
    def __init__(self, value, upper):
        self.value, self.upper, self.sizes = value, upper, {}

    def start(self, kind, bit):
        self.kind, self.bit = kind, bit
        sent = self.value
        if kind == "scatter":
            self.sizes[bit] = self.value.shape[0]
            self.value, sent = choose(self.value, self.upper[bit])
        self.flying = exchange(sent, 1 << bit)

    def finish(self):
        if self.kind == "gather":
            self.value = join(self.value, self.flying, self.sizes[self.bit], self.upper[self.bit])
        else:
            self.value = self.value + self.flying


def per_device(q_two, q_one, sources, coupling_two, coupling_one):
    index = lax.axis_index(AXES)
    places = lax.axis_size(AXES).bit_length() - 1
    flags = [(index >> bit) & 1 == 1 for bit in range(places)]
    q_two, *upper = lax.optimization_barrier((q_two, *flags))
    stages = summing_stages(list(range(2, places)))

    keep, send, b2, b1 = panel_gram(q_two, q_one)
    arriving = exchange(send, 1)
    source_keep, source_send = source_gram(b2, b1, sources)
    arriving, source_send = lax.optimization_barrier((arriving, source_send))

    panels = Chain(keep + arriving, upper)
    source = Chain(source_keep, upper)
    panels.sizes[0], source.sizes[0] = PANEL_TERMS, SOURCE_TERMS
    source_left = [("gather", 0)] + stages[::-1]
    for step, stage in enumerate(stages):
        panels.start(*stage)
        if step == 0:
            source.kind, source.bit, source.flying = "sum", 0, exchange(source_send, 1)
        else:
            source.start(*source_left.pop())
        panels.flying, source.flying = lax.optimization_barrier((panels.flying, source.flying))
        panels.finish()
        source.finish()
    panels.start("gather", 0)
    source.start(*source_left.pop())
    panels.finish()
    terms = panels.value
    parts = invert_first(half_index, terms, coupling_two, "level_first")
    source.flying, parts = lax.optimization_barrier((source.flying, parts))
    source.finish()
    source.start(*source_left.pop())
    inverse = invert_second(parts, "level_second")
    source.flying, inverse = lax.optimization_barrier((source.flying, inverse))
    source.finish()

    x, root = call(
        panel_solve_kernel, (SQUARE, jax.ShapeDtypeStruct((SYMMETRIC, LANES), F32)), (inverse, terms), "panel_solve"
    )
    arriving = exchange(root, 2)
    full = jax.ShapeDtypeStruct((FULL, LANES), F32)
    panel_one, y, side = update(panel_kernel, [b2, b1, x, inverse, source.value], 5, "panel", [SQUARE, full])
    side = Chain(choose(side, upper[0])[0], upper)
    side.sizes[0] = FULL
    side_flying = exchange(side.value, 2)
    arriving, side.value = lax.optimization_barrier((arriving, side.value))
    root = root + arriving
    parts = invert_first(no_index, root, coupling_one[None], "root_first")
    side_flying, parts = lax.optimization_barrier((side_flying, parts))
    side.value = side.value + side_flying
    side.start("gather", 0)
    inverse = invert_second(parts, "root_second")
    side.finish()
    (solution,) = update(field_kernel, [b2, panel_one, sources, inverse, side.value, y], 6, "field")
    return (panel_one, solution)


def solution(mesh):
    placed = P(("group", "leaf"), None)
    return jax.shard_map(
        per_device,
        mesh=mesh,
        in_specs=(placed, placed, placed, P(), P()),
        out_specs=(placed, placed),
        check_vma=False,
    )
```

```python
import functools

import jax
import jax.numpy as jnp
from jax import lax
from jax.experimental import pallas as pl
from jax.experimental.pallas import tpu as pltpu
from jax.sharding import PartitionSpec as P

HIGH = lax.Precision.HIGHEST
AXES = ("leaf", "group")
F32 = jnp.float32
BF16 = jnp.bfloat16
R = 256
LANES = 128
TILE = 512
VMEM_LIMIT = 16 * 1024 * 1024
SYMMETRIC, FULL = 264, 512
OWN, ROOT, CROSS, PANEL_TERMS = 0, 264, 528, 1040
PROJECTED, SIDE, SOURCE_TERMS = 0, 512, 1024


def split2(x):
    high = x.astype(BF16)
    return high, (x - high.astype(F32)).astype(BF16)


def split3(x):
    high = x.astype(BF16)
    rest = x - high.astype(F32)
    mid = rest.astype(BF16)
    return high, mid, (rest - mid.astype(F32)).astype(BF16)


def dot(left, right):
    return jnp.dot(left, right, preferred_element_type=F32)


def dot_t(left, right):
    return lax.dot_general(left, right, (((0,), (0,)), ((), ())), preferred_element_type=F32)


def dot_full(left, right):
    return jnp.dot(left, right, precision=HIGH, preferred_element_type=F32)


def dot_t_full(left, right):
    return lax.dot_general(
        left, right, (((0,), (0,)), ((), ())), precision=HIGH, preferred_element_type=F32
    )


def square_index():
    row = lax.broadcasted_iota(jnp.int32, (LANES, LANES), 0)
    return row, lax.broadcasted_iota(jnp.int32, (LANES, LANES), 1)


def store_symmetric(ref, at, block):
    row, col = square_index()
    last = block[128:, 128:]
    ref[at : at + 128, :] = block[128:, :128]
    ref[at + 128 : at + 256, :] = jnp.where(row >= col, block[:128, :128], last)
    diagonal = jnp.sum(jnp.where(row == col, last, 0.0), axis=0, keepdims=True)
    ref[at + 256 : at + 264, :] = jnp.broadcast_to(diagonal, (8, LANES))


def store_square(ref, row, block):
    ref[row : row + 256, :] = block[:, :128]
    ref[row + 256 : row + 512, :] = block[:, 128:]


def load_symmetric(ref, at):
    row, col = square_index()
    lower = ref[at : at + 128, :]
    mixed = ref[at + 128 : at + 256, :]
    turned = mixed.T
    first = jnp.where(row >= col, mixed, turned)
    last = jnp.where(row < col, mixed, turned)
    last = jnp.where(row == col, ref[at + 256 : at + 257, :], last)
    top = jnp.concatenate([first, lower.T], axis=1)
    return jnp.concatenate([top, jnp.concatenate([lower, last], axis=1)], axis=0)


def load_square(ref, row):
    return jnp.concatenate([ref[row : row + 256, :], ref[row + 256 : row + 512, :]], axis=1)


def half_of(rows):
    return (rows + 15) // 16 * 8


def store_halves(packed, keep, send):
    half = half_of(packed.shape[0])
    far = packed.shape[0] - half
    mine = lax.rem(lax.axis_index("group"), 2)
    keep[...] = packed[pl.ds(pl.multiple_of(mine * far, 8), half), :]
    send[...] = packed[pl.ds(pl.multiple_of((1 - mine) * far, 8), half), :]


def tile_at(tile):
    return pl.ds(pl.multiple_of(tile * TILE, TILE), TILE)


def panel_gram_kernel(q_two, q_one, keep, send, b2, b1, acc, packed, sems):
    tiles = b2.shape[0] // TILE
    pairs = ((q_two, b2), (q_one, b1))

    def copy(tile, which):
        source, target = pairs[which]
        here = tile_at(tile)
        return pltpu.make_async_copy(source.at[here], target.at[here], sems.at[which, tile])

    for tile in range(tiles):
        for which in range(2):
            copy(tile, which).start()
    acc[...] = jnp.zeros_like(acc)

    def step(tile, carry):
        for which in range(2):
            copy(tile, which).wait()
        h2, l2 = split2(b2[tile_at(tile), :])
        h1, l1 = split2(b1[tile_at(tile), :])
        h2t, l2t, h1t = h2.T, l2.T, h1.T
        acc[0] += dot(h2t, h2)
        acc[1] += dot(h2t, l2)
        left = jnp.concatenate([h2t, h2t, l2t], axis=1)
        acc[2] += dot(left, jnp.concatenate([h1, l1, h1], axis=0))
        acc[3] += dot(h1t, h1)
        acc[4] += dot(h1t, l1)
        return carry

    lax.fori_loop(0, tiles, step, 0)
    low = acc[1]
    store_symmetric(packed, OWN, acc[0] + low + low.T)
    low = acc[4]
    store_symmetric(packed, ROOT, acc[3] + low + low.T)
    store_square(packed, CROSS, acc[2])
    store_halves(packed, keep, send)


def source_gram_kernel(b2, b1, sources, keep, send, acc, packed):
    acc[...] = jnp.zeros_like(acc)

    def step(tile, carry):
        hs, ls = split2(sources[tile_at(tile), :])
        right = jnp.concatenate([hs, ls, hs], axis=0)
        for which, panel in enumerate((b2, b1)):
            high, low = split2(panel[tile_at(tile), :])
            turned = high.T
            acc[which] += dot(jnp.concatenate([turned, turned, low.T], axis=1), right)
        return carry

    lax.fori_loop(0, b2.shape[0] // TILE, step, 0)
    store_square(packed, PROJECTED, acc[0])
    store_square(packed, SIDE, acc[1])
    store_halves(packed, keep, send)


def cost(passes, rows, arrays):
    return pl.CostEstimate(
        flops=2 * passes * rows * R * R, bytes_accessed=4 * arrays * rows * R, transcendentals=0
    )


def panel_gram(q_two, q_one):
    rows = q_two.shape[0]
    part = jax.ShapeDtypeStruct((half_of(PANEL_TERMS), LANES), F32)
    tall = jax.ShapeDtypeStruct((rows, R), F32)
    return pl.pallas_call(
        panel_gram_kernel,
        in_specs=[pl.BlockSpec(memory_space=pl.ANY)] * 2,
        out_shape=(part, part, tall, tall),
        scratch_shapes=[
            pltpu.VMEM((5, R, R), F32),
            pltpu.VMEM((PANEL_TERMS, LANES), F32),
            pltpu.SemaphoreType.DMA((2, rows // TILE)),
        ],
        compiler_params=pltpu.CompilerParams(vmem_limit_bytes=VMEM_LIMIT),
        cost_estimate=cost(7, rows, 2),
        name="panel_gram",
    )(pltpu.with_memory_space_constraint(q_two, pltpu.HBM), pltpu.with_memory_space_constraint(q_one, pltpu.HBM))


def source_gram(b2, b1, sources):
    part = jax.ShapeDtypeStruct((half_of(SOURCE_TERMS), LANES), F32)
    return pl.pallas_call(
        source_gram_kernel,
        out_shape=(part, part),
        scratch_shapes=[pltpu.VMEM((2, R, R), F32), pltpu.VMEM((SOURCE_TERMS, LANES), F32)],
        compiler_params=pltpu.CompilerParams(vmem_limit_bytes=VMEM_LIMIT),
        cost_estimate=cost(6, b2.shape[0], 3),
        name="source_gram",
    )(b2, b1, sources)


def spread_lane(x, lane):
    return jnp.broadcast_to(x[:, lane : lane + 1], (8, LANES))


def eliminate(block, cols, rows):
    count = len(block)
    lane = lax.broadcasted_iota(jnp.int32, (8, LANES), 1)
    for start in range(0, count, 4):
        panel = block[start : start + 4]
        left = stack_left(jnp.concatenate(panel, axis=0))
        for t in range(4):
            panel = eliminate_group(panel, t, start + t, cols, rows)
        inside = (lane >= 8 * start) & (lane < 8 * start + 32)
        panel = [jnp.where(inside, -x, x) for x in panel]
        change = dot_t(left, stack_right(jnp.concatenate(panel, axis=0)))
        for g in range(count):
            if start <= g < start + 4:
                block[g] = panel[g - start]
            else:
                block[g] = jnp.where(inside, 0.0, block[g]) - change[8 * g : 8 * g + 8, :]
    return [-x for x in block]


def eliminate_group(panel, t, at, cols, rows):
    lane = lax.broadcasted_iota(jnp.int32, (8, LANES), 1)
    sub = lax.broadcasted_iota(jnp.int32, (8, LANES), 0)
    for j in range(8):
        cols[64 * at + 8 * j : 64 * at + 8 * j + 8, :] = spread_lane(panel[t], 8 * at + j)
    rows[8 * at : 8 * at + 8, :] = panel[t]
    entry = {}
    for i in range(8):
        for j in range(i + 1):
            row = 64 * at + 8 * j + i
            entry[i, j] = jnp.broadcast_to(cols[row : row + 1, :], (8, LANES))
    inside = (lane >= 8 * at) & (lane < 8 * at + 8)
    line = []
    for j in range(8):
        row = jnp.broadcast_to(rows[8 * at + j : 8 * at + j + 1, :], (8, LANES))
        line.append(jnp.where(inside, jnp.where(lane == 8 * at + j, 1.0, 0.0), row))
    after = None
    if t < 3:
        columns = [spread_lane(panel[t + 1], 8 * at + j) for j in range(8)]
        after = [columns, jnp.where(inside, 0.0, panel[t + 1])]
    line, after = solve_small(entry, line, after)
    for g in range(4):
        if g == t + 1:
            panel[g] = after
        elif g != t:
            terms = [spread_lane(panel[g], 8 * at + j) * line[j] for j in range(8)]
            panel[g] = jnp.where(inside, 0.0, panel[g]) - tree_sum(terms)
    merged = line[0]
    for j in range(1, 8):
        merged = jnp.where(sub == j, line[j], merged)
    panel[t] = merged
    return panel


def tree_sum(terms):
    while len(terms) > 1:
        terms = [
            terms[i] + terms[i + 1] if i + 1 < len(terms) else terms[i]
            for i in range(0, len(terms), 2)
        ]
    return terms[0]


def solve_small(entry, line, after):
    columns, block = after or (None, None)
    factors, scaled = {}, {}
    for k in range(0, 8, 2):
        a, b, c = entry[k, k], entry[k + 1, k], entry[k + 1, k + 1]
        inv = pl.reciprocal(a * c - b * b, approx=True)
        below = range(k + 2, 8)
        first = {i: c * entry[i, k] - b * entry[i, k + 1] for i in below}
        second = {i: a * entry[i, k + 1] - b * entry[i, k] for i in below}
        for i in below:
            for j in range(k + 2, i + 1):
                entry[i, j] = entry[i, j] - inv * (first[i] * entry[j, k] + second[i] * entry[j, k + 1])
        top = c * line[k] - b * line[k + 1]
        bottom = a * line[k + 1] - b * line[k]
        if columns is not None:
            block = block - inv * (columns[k] * top + columns[k + 1] * bottom)
        scaled[k], scaled[k + 1] = inv * top, inv * bottom
        for i in below:
            m, n = inv * first[i], inv * second[i]
            factors[i, k] = m, n
            line[i] = line[i] - (m * line[k] + n * line[k + 1])
            if columns is not None:
                columns[i] = columns[i] - (m * columns[k] + n * columns[k + 1])
    for k in range(6, -1, -2):
        x, y = scaled[k], scaled[k + 1]
        if k < 6:
            x = x - tree_sum([factors[i, k][0] * line[i] for i in range(k + 2, 8)])
            y = y - tree_sum([factors[i, k][1] * line[i] for i in range(k + 2, 8)])
        line[k], line[k + 1] = x, y
    return line, block


def stack_left(x):
    h, m, l = split3(x)
    return jnp.concatenate([h, h, m, h, l, m], axis=0)


def stack_right(x):
    h, m, l = split3(x)
    return jnp.concatenate([h, m, h, l, h, m], axis=0)


def invert_half(matrix, cols, rows):
    block = eliminate([matrix[8 * i : 8 * i + 8, :] for i in range(LANES // 8)], cols, rows)
    return jnp.concatenate(block, axis=0)


SQUARE = jax.ShapeDtypeStruct((R, R), F32)
CORNER = jax.ShapeDtypeStruct((LANES, LANES), F32)


def call(kernel, out_shape, args, name, scratch=(), flops=0):
    return pl.pallas_call(
        kernel,
        out_shape=out_shape,
        scratch_shapes=list(scratch),
        compiler_params=pltpu.CompilerParams(vmem_limit_bytes=VMEM_LIMIT),
        cost_estimate=pl.CostEstimate(flops=flops, bytes_accessed=R * R * 4, transcendentals=0),
        name=name,
    )(*args)


def first_kernel(which, gram_ref, coupling, first_out, across_out, rest_out, row_out, col_out, cols, rows):
    matrix = coupling[which()] + load_symmetric(gram_ref, OWN)
    eye = lax.broadcasted_iota(jnp.int32, (R, R), 0) == lax.broadcasted_iota(jnp.int32, (R, R), 1)
    diagonal = jnp.where(eye, matrix, 0.0)
    scale_row = lax.rsqrt(jnp.sum(diagonal, axis=0, keepdims=True))
    scale_col = lax.rsqrt(jnp.sum(diagonal, axis=1, keepdims=True))
    matrix = matrix * scale_col * scale_row
    side = matrix[:LANES, LANES:]
    first = invert_half(matrix[:LANES, :LANES], cols, rows)
    across = dot_full(first, side)
    first_out[...] = first
    across_out[...] = across
    rest_out[...] = matrix[LANES:, LANES:] - dot_t_full(side, across)
    row_out[...] = jnp.broadcast_to(scale_row, (8, R))
    col_out[...] = jnp.broadcast_to(scale_col, (R, LANES))


def second_kernel(first, across, rest, row, col, out, cols, rows):
    second = invert_half(rest[...], cols, rows)
    corner = -dot_full(across[...], second)
    top = first[...] - dot_full(corner, across[...].T)
    out[:LANES, :LANES] = top * col[:LANES, :] * row[:1, :LANES]
    out[:LANES, LANES:] = corner * col[:LANES, :] * row[:1, LANES:]
    out[LANES:, :LANES] = corner.T * col[LANES:, :] * row[:1, :LANES]
    out[LANES:, LANES:] = second * col[LANES:, :] * row[:1, LANES:]


SCRATCH = [pltpu.VMEM((1024, LANES), F32), pltpu.VMEM((LANES, LANES), F32)]
HALF_FLOPS = 5_000_000_000


def invert_first(which, packed, coupling, name):
    shapes = (
        CORNER,
        CORNER,
        CORNER,
        jax.ShapeDtypeStruct((8, R), F32),
        jax.ShapeDtypeStruct((R, LANES), F32),
    )
    kernel = functools.partial(first_kernel, which)
    return call(kernel, shapes, (packed, coupling), name, SCRATCH, HALF_FLOPS)


def invert_second(parts, name):
    return call(second_kernel, SQUARE, parts, name, SCRATCH, HALF_FLOPS)


def half_index():
    return lax.axis_index("group") // 2


def no_index():
    return 0


def panel_solve_kernel(inverse, terms, x_out, root_out):
    cross = load_square(terms, CROSS)
    x = dot_full(inverse[...], cross)
    x_out[...] = x
    store_symmetric(root_out, 0, load_symmetric(terms, ROOT) - dot_t_full(cross, x))


def wide(x):
    high, low = split2(x)
    return jnp.concatenate([high, high, low], axis=1)


def tall(x):
    high, low = split2(x)
    return jnp.concatenate([high, low, high], axis=0)


def by_tiles(rows, out, stage, sems, value, beside=None):
    tiles = rows // TILE

    def copy(tile):
        return pltpu.make_async_copy(stage.at[tile_at(tile)], out.at[tile_at(tile)], sems.at[tile])

    def step(tile, carry):
        stage[tile_at(tile), :] = value(tile_at(tile))
        copy(tile).start()
        return carry

    lax.fori_loop(0, tiles, step, 0)
    if beside is not None:
        beside()
    for tile in range(tiles):
        copy(tile).wait()


def panel_kernel(b2, b1, x, inverse, terms, out, y_out, side_out, stage, sems):
    def sources_part():
        projected = load_square(terms, PROJECTED)
        y_out[...] = dot_full(inverse[...], projected)
        store_square(side_out, 0, load_square(terms, SIDE) - dot_t_full(x[...], projected))

    right = tall(x[...])
    by_tiles(b2.shape[0], out, stage, sems, lambda at: b1[at, :] - dot(wide(b2[at, :]), right), sources_part)


def field_kernel(b2, panel, sources, inverse, side, y, out, stage, sems):
    weights = dot(wide(inverse[...]), tall(load_square(side, 0)))
    right = jnp.concatenate([tall(y[...]), tall(weights)], axis=0)

    def value(at):
        left = jnp.concatenate([wide(b2[at, :]), wide(panel[at, :])], axis=1)
        return sources[at, :] - dot(left, right)

    by_tiles(b2.shape[0], out, stage, sems, value)


def update(kernel, args, passes, name, more=()):
    rows = args[0].shape[0]
    return pl.pallas_call(
        kernel,
        out_specs=[pl.BlockSpec(memory_space=pl.ANY)] + [pl.BlockSpec(memory_space=pltpu.VMEM)] * len(more),
        out_shape=[jax.ShapeDtypeStruct((rows, R), F32), *more],
        scratch_shapes=[pltpu.VMEM((rows, R), F32), pltpu.SemaphoreType.DMA((rows // TILE,))],
        compiler_params=pltpu.CompilerParams(vmem_limit_bytes=VMEM_LIMIT),
        cost_estimate=cost(passes, rows, 3),
        name=name,
    )(*args)


def exchange(x, mask):
    count = lax.axis_size(AXES)
    return lax.ppermute(x, AXES, [(i, i ^ mask) for i in range(count)])


def choose(x, upper):
    half = half_of(x.shape[0])
    low, high = x[:half], x[x.shape[0] - half :]
    return jnp.where(upper, high, low), jnp.where(upper, low, high)


def join(x, other, rows, upper):
    low, high = jnp.where(upper, other, x), jnp.where(upper, x, other)
    return jnp.concatenate([low[: rows - x.shape[0]], high], axis=0)


def summing_stages(bits):
    down = [("scatter", bit) for bit in bits[:-1]]
    return down + [("sum", bits[-1])] + [("gather", bit) for bit in reversed(bits[:-1])]


class Chain:
    def __init__(self, value, upper):
        self.value, self.upper, self.sizes = value, upper, {}

    def start(self, kind, bit):
        self.kind, self.bit = kind, bit
        sent = self.value
        if kind == "scatter":
            self.sizes[bit] = self.value.shape[0]
            self.value, sent = choose(self.value, self.upper[bit])
        self.flying = exchange(sent, 1 << bit)

    def finish(self):
        if self.kind == "gather":
            self.value = join(self.value, self.flying, self.sizes[self.bit], self.upper[self.bit])
        else:
            self.value = self.value + self.flying


def per_device(q_two, q_one, sources, coupling_two, coupling_one):
    index = lax.axis_index(AXES)
    places = lax.axis_size(AXES).bit_length() - 1
    flags = [(index >> bit) & 1 == 1 for bit in range(places)]
    q_two, *upper = lax.optimization_barrier((q_two, *flags))
    stages = summing_stages(list(range(2, places)))

    keep, send, b2, b1 = panel_gram(q_two, q_one)
    arriving = exchange(send, 1)
    source_keep, source_send = source_gram(b2, b1, sources)
    arriving, source_send = lax.optimization_barrier((arriving, source_send))

    panels = Chain(keep + arriving, upper)
    source = Chain(source_keep, upper)
    panels.sizes[0], source.sizes[0] = PANEL_TERMS, SOURCE_TERMS
    source_left = [("gather", 0)] + stages[::-1]
    for step, stage in enumerate(stages):
        panels.start(*stage)
        if step == 0:
            source.kind, source.bit, source.flying = "sum", 0, exchange(source_send, 1)
        else:
            source.start(*source_left.pop())
        panels.flying, source.flying = lax.optimization_barrier((panels.flying, source.flying))
        panels.finish()
        source.finish()
    panels.start("gather", 0)
    source.start(*source_left.pop())
    panels.finish()
    terms = panels.value
    parts = invert_first(half_index, terms, coupling_two, "level_first")
    source.flying, parts = lax.optimization_barrier((source.flying, parts))
    source.finish()
    source.start(*source_left.pop())
    inverse = invert_second(parts, "level_second")
    source.flying, inverse = lax.optimization_barrier((source.flying, inverse))
    source.finish()

    x, root = call(
        panel_solve_kernel, (SQUARE, jax.ShapeDtypeStruct((SYMMETRIC, LANES), F32)), (inverse, terms), "panel_solve"
    )
    arriving = exchange(root, 2)
    full = jax.ShapeDtypeStruct((FULL, LANES), F32)
    panel_one, y, side = update(panel_kernel, [b2, b1, x, inverse, source.value], 5, "panel", [SQUARE, full])
    side = Chain(choose(side, upper[0])[0], upper)
    side.sizes[0] = FULL
    side_flying = exchange(side.value, 2)
    arriving, side.value = lax.optimization_barrier((arriving, side.value))
    root = root + arriving
    parts = invert_first(no_index, root, coupling_one[None], "root_first")
    side_flying, parts = lax.optimization_barrier((side_flying, parts))
    side.value = side.value + side_flying
    side.start("gather", 0)
    inverse = invert_second(parts, "root_second")
    side.finish()
    (solution,) = update(field_kernel, [b2, panel_one, sources, inverse, side.value, y], 6, "field")
    return (panel_one, solution)


def solution(mesh):
    placed = P(("group", "leaf"), None)
    return jax.shard_map(
        per_device,
        mesh=mesh,
        in_specs=(placed, placed, placed, P(), P()),
        out_specs=(placed, placed),
        check_vma=False,
    )
```

```python
import functools

import jax
import jax.numpy as jnp
from jax import lax
from jax.experimental import pallas as pl
from jax.experimental.pallas import tpu as pltpu
from jax.sharding import PartitionSpec as P

HIGH = lax.Precision.HIGHEST
AXES = ("leaf", "group")
F32 = jnp.float32
BF16 = jnp.bfloat16
R = 256
LANES = 128
TILE = 512
VMEM_LIMIT = 16 * 1024 * 1024
SYMMETRIC, FULL = 264, 512
OWN, ROOT, CROSS, PANEL_TERMS = 0, 264, 528, 1040
PROJECTED, SIDE, SOURCE_TERMS = 0, 512, 1024


def split2(x):
    high = x.astype(BF16)
    return high, (x - high.astype(F32)).astype(BF16)


def split3(x):
    high = x.astype(BF16)
    rest = x - high.astype(F32)
    mid = rest.astype(BF16)
    return high, mid, (rest - mid.astype(F32)).astype(BF16)


def dot(left, right):
    return jnp.dot(left, right, preferred_element_type=F32)


def dot_t(left, right):
    return lax.dot_general(left, right, (((0,), (0,)), ((), ())), preferred_element_type=F32)


def dot_full(left, right):
    return jnp.dot(left, right, precision=HIGH, preferred_element_type=F32)


def dot_t_full(left, right):
    return lax.dot_general(
        left, right, (((0,), (0,)), ((), ())), precision=HIGH, preferred_element_type=F32
    )


def square_index():
    row = lax.broadcasted_iota(jnp.int32, (LANES, LANES), 0)
    return row, lax.broadcasted_iota(jnp.int32, (LANES, LANES), 1)


def store_symmetric(ref, at, block):
    row, col = square_index()
    last = block[128:, 128:]
    ref[at : at + 128, :] = block[128:, :128]
    ref[at + 128 : at + 256, :] = jnp.where(row >= col, block[:128, :128], last)
    diagonal = jnp.sum(jnp.where(row == col, last, 0.0), axis=0, keepdims=True)
    ref[at + 256 : at + 264, :] = jnp.broadcast_to(diagonal, (8, LANES))


def store_square(ref, row, block):
    ref[row : row + 256, :] = block[:, :128]
    ref[row + 256 : row + 512, :] = block[:, 128:]


def load_symmetric(ref, at):
    row, col = square_index()
    lower = ref[at : at + 128, :]
    mixed = ref[at + 128 : at + 256, :]
    turned = mixed.T
    first = jnp.where(row >= col, mixed, turned)
    last = jnp.where(row < col, mixed, turned)
    last = jnp.where(row == col, ref[at + 256 : at + 257, :], last)
    top = jnp.concatenate([first, lower.T], axis=1)
    return jnp.concatenate([top, jnp.concatenate([lower, last], axis=1)], axis=0)


def load_square(ref, row):
    return jnp.concatenate([ref[row : row + 256, :], ref[row + 256 : row + 512, :]], axis=1)


def half_of(rows):
    return (rows + 15) // 16 * 8


def store_halves(packed, keep, send):
    half = half_of(packed.shape[0])
    far = packed.shape[0] - half
    mine = lax.rem(lax.axis_index("group"), 2)
    keep[...] = packed[pl.ds(pl.multiple_of(mine * far, 8), half), :]
    send[...] = packed[pl.ds(pl.multiple_of((1 - mine) * far, 8), half), :]


def tile_at(tile):
    return pl.ds(pl.multiple_of(tile * TILE, TILE), TILE)


def panel_gram_kernel(q_two, q_one, keep, send, b2, b1, acc, packed, sems):
    tiles = b2.shape[0] // TILE
    pairs = ((q_two, b2), (q_one, b1))

    def copy(tile, which):
        source, target = pairs[which]
        here = tile_at(tile)
        return pltpu.make_async_copy(source.at[here], target.at[here], sems.at[which, tile])

    for tile in range(tiles):
        for which in range(2):
            copy(tile, which).start()
    acc[...] = jnp.zeros_like(acc)

    def step(tile, carry):
        for which in range(2):
            copy(tile, which).wait()
        h2, l2 = split2(b2[tile_at(tile), :])
        h1, l1 = split2(b1[tile_at(tile), :])
        h2t, l2t, h1t = h2.T, l2.T, h1.T
        acc[0] += dot(h2t, h2)
        acc[1] += dot(h2t, l2)
        left = jnp.concatenate([h2t, h2t, l2t], axis=1)
        acc[2] += dot(left, jnp.concatenate([h1, l1, h1], axis=0))
        acc[3] += dot(h1t, h1)
        acc[4] += dot(h1t, l1)
        return carry

    lax.fori_loop(0, tiles, step, 0)
    low = acc[1]
    store_symmetric(packed, OWN, acc[0] + low + low.T)
    low = acc[4]
    store_symmetric(packed, ROOT, acc[3] + low + low.T)
    store_square(packed, CROSS, acc[2])
    store_halves(packed, keep, send)


def source_gram_kernel(b2, b1, sources, keep, send, acc, packed):
    acc[...] = jnp.zeros_like(acc)

    def step(tile, carry):
        hs, ls = split2(sources[tile_at(tile), :])
        right = jnp.concatenate([hs, ls, hs], axis=0)
        for which, panel in enumerate((b2, b1)):
            high, low = split2(panel[tile_at(tile), :])
            turned = high.T
            acc[which] += dot(jnp.concatenate([turned, turned, low.T], axis=1), right)
        return carry

    lax.fori_loop(0, b2.shape[0] // TILE, step, 0)
    store_square(packed, PROJECTED, acc[0])
    store_square(packed, SIDE, acc[1])
    store_halves(packed, keep, send)


def cost(passes, rows, arrays):
    return pl.CostEstimate(
        flops=2 * passes * rows * R * R, bytes_accessed=4 * arrays * rows * R, transcendentals=0
    )


def panel_gram(q_two, q_one):
    rows = q_two.shape[0]
    part = jax.ShapeDtypeStruct((half_of(PANEL_TERMS), LANES), F32)
    tall = jax.ShapeDtypeStruct((rows, R), F32)
    return pl.pallas_call(
        panel_gram_kernel,
        in_specs=[pl.BlockSpec(memory_space=pl.ANY)] * 2,
        out_shape=(part, part, tall, tall),
        scratch_shapes=[
            pltpu.VMEM((5, R, R), F32),
            pltpu.VMEM((PANEL_TERMS, LANES), F32),
            pltpu.SemaphoreType.DMA((2, rows // TILE)),
        ],
        compiler_params=pltpu.CompilerParams(vmem_limit_bytes=VMEM_LIMIT),
        cost_estimate=cost(7, rows, 2),
        name="panel_gram",
    )(pltpu.with_memory_space_constraint(q_two, pltpu.HBM), pltpu.with_memory_space_constraint(q_one, pltpu.HBM))


def source_gram(b2, b1, sources):
    part = jax.ShapeDtypeStruct((half_of(SOURCE_TERMS), LANES), F32)
    return pl.pallas_call(
        source_gram_kernel,
        out_shape=(part, part),
        scratch_shapes=[pltpu.VMEM((2, R, R), F32), pltpu.VMEM((SOURCE_TERMS, LANES), F32)],
        compiler_params=pltpu.CompilerParams(vmem_limit_bytes=VMEM_LIMIT),
        cost_estimate=cost(6, b2.shape[0], 3),
        name="source_gram",
    )(b2, b1, sources)


def spread_lane(x, lane):
    return jnp.broadcast_to(x[:, lane : lane + 1], (8, LANES))


def eliminate(block, cols, rows):
    count = len(block)
    lane = lax.broadcasted_iota(jnp.int32, (8, LANES), 1)
    for start in range(0, count, 4):
        panel = block[start : start + 4]
        left = stack_left(jnp.concatenate(panel, axis=0))
        for t in range(4):
            panel = eliminate_group(panel, t, start + t, cols, rows)
        inside = (lane >= 8 * start) & (lane < 8 * start + 32)
        panel = [jnp.where(inside, -x, x) for x in panel]
        change = dot_t(left, stack_right(jnp.concatenate(panel, axis=0)))
        for g in range(count):
            if start <= g < start + 4:
                block[g] = panel[g - start]
            else:
                block[g] = jnp.where(inside, 0.0, block[g]) - change[8 * g : 8 * g + 8, :]
    return [-x for x in block]


def eliminate_group(panel, t, at, cols, rows):
    lane = lax.broadcasted_iota(jnp.int32, (8, LANES), 1)
    sub = lax.broadcasted_iota(jnp.int32, (8, LANES), 0)
    for j in range(8):
        cols[64 * at + 8 * j : 64 * at + 8 * j + 8, :] = spread_lane(panel[t], 8 * at + j)
    rows[8 * at : 8 * at + 8, :] = panel[t]
    entry = {}
    for i in range(8):
        for j in range(i + 1):
            row = 64 * at + 8 * j + i
            entry[i, j] = jnp.broadcast_to(cols[row : row + 1, :], (8, LANES))
    inside = (lane >= 8 * at) & (lane < 8 * at + 8)
    line = []
    for j in range(8):
        row = jnp.broadcast_to(rows[8 * at + j : 8 * at + j + 1, :], (8, LANES))
        line.append(jnp.where(inside, jnp.where(lane == 8 * at + j, 1.0, 0.0), row))
    after = None
    if t < 3:
        columns = [spread_lane(panel[t + 1], 8 * at + j) for j in range(8)]
        after = [columns, jnp.where(inside, 0.0, panel[t + 1])]
    line, after = solve_small(entry, line, after)
    for g in range(4):
        if g == t + 1:
            panel[g] = after
        elif g != t:
            terms = [spread_lane(panel[g], 8 * at + j) * line[j] for j in range(8)]
            panel[g] = jnp.where(inside, 0.0, panel[g]) - tree_sum(terms)
    merged = line[0]
    for j in range(1, 8):
        merged = jnp.where(sub == j, line[j], merged)
    panel[t] = merged
    return panel


def tree_sum(terms):
    while len(terms) > 1:
        terms = [
            terms[i] + terms[i + 1] if i + 1 < len(terms) else terms[i]
            for i in range(0, len(terms), 2)
        ]
    return terms[0]


def solve_small(entry, line, after):
    columns, block = after or (None, None)
    factors, scaled = {}, {}
    for k in range(0, 8, 2):
        a, b, c = entry[k, k], entry[k + 1, k], entry[k + 1, k + 1]
        inv = pl.reciprocal(a * c - b * b, approx=True)
        below = range(k + 2, 8)
        first = {i: c * entry[i, k] - b * entry[i, k + 1] for i in below}
        second = {i: a * entry[i, k + 1] - b * entry[i, k] for i in below}
        for i in below:
            for j in range(k + 2, i + 1):
                entry[i, j] = entry[i, j] - inv * (first[i] * entry[j, k] + second[i] * entry[j, k + 1])
        top = c * line[k] - b * line[k + 1]
        bottom = a * line[k + 1] - b * line[k]
        if columns is not None:
            block = block - inv * (columns[k] * top + columns[k + 1] * bottom)
        scaled[k], scaled[k + 1] = inv * top, inv * bottom
        for i in below:
            m, n = inv * first[i], inv * second[i]
            factors[i, k] = m, n
            line[i] = line[i] - (m * line[k] + n * line[k + 1])
            if columns is not None:
                columns[i] = columns[i] - (m * columns[k] + n * columns[k + 1])
    for k in range(6, -1, -2):
        x, y = scaled[k], scaled[k + 1]
        if k < 6:
            x = x - tree_sum([factors[i, k][0] * line[i] for i in range(k + 2, 8)])
            y = y - tree_sum([factors[i, k][1] * line[i] for i in range(k + 2, 8)])
        line[k], line[k + 1] = x, y
    return line, block


def stack_left(x):
    h, m, l = split3(x)
    return jnp.concatenate([h, h, m, h, l, m], axis=0)


def stack_right(x):
    h, m, l = split3(x)
    return jnp.concatenate([h, m, h, l, h, m], axis=0)


def invert_half(matrix, cols, rows):
    block = eliminate([matrix[8 * i : 8 * i + 8, :] for i in range(LANES // 8)], cols, rows)
    return jnp.concatenate(block, axis=0)


SQUARE = jax.ShapeDtypeStruct((R, R), F32)
CORNER = jax.ShapeDtypeStruct((LANES, LANES), F32)


def call(kernel, out_shape, args, name, scratch=(), flops=0):
    return pl.pallas_call(
        kernel,
        out_shape=out_shape,
        scratch_shapes=list(scratch),
        compiler_params=pltpu.CompilerParams(vmem_limit_bytes=VMEM_LIMIT),
        cost_estimate=pl.CostEstimate(flops=flops, bytes_accessed=R * R * 4, transcendentals=0),
        name=name,
    )(*args)


def first_kernel(which, gram_ref, coupling, first_out, across_out, rest_out, row_out, col_out, cols, rows):
    matrix = coupling[which()] + load_symmetric(gram_ref, OWN)
    eye = lax.broadcasted_iota(jnp.int32, (R, R), 0) == lax.broadcasted_iota(jnp.int32, (R, R), 1)
    diagonal = jnp.where(eye, matrix, 0.0)
    scale_row = lax.rsqrt(jnp.sum(diagonal, axis=0, keepdims=True))
    scale_col = lax.rsqrt(jnp.sum(diagonal, axis=1, keepdims=True))
    matrix = matrix * scale_col * scale_row
    side = matrix[:LANES, LANES:]
    first = invert_half(matrix[:LANES, :LANES], cols, rows)
    across = dot_full(first, side)
    first_out[...] = first
    across_out[...] = across
    rest_out[...] = matrix[LANES:, LANES:] - dot_t_full(side, across)
    row_out[...] = jnp.broadcast_to(scale_row, (8, R))
    col_out[...] = jnp.broadcast_to(scale_col, (R, LANES))


def second_kernel(first, across, rest, row, col, out, cols, rows):
    second = invert_half(rest[...], cols, rows)
    corner = -dot_full(across[...], second)
    top = first[...] - dot_full(corner, across[...].T)
    out[:LANES, :LANES] = top * col[:LANES, :] * row[:1, :LANES]
    out[:LANES, LANES:] = corner * col[:LANES, :] * row[:1, LANES:]
    out[LANES:, :LANES] = corner.T * col[LANES:, :] * row[:1, :LANES]
    out[LANES:, LANES:] = second * col[LANES:, :] * row[:1, LANES:]


SCRATCH = [pltpu.VMEM((1024, LANES), F32), pltpu.VMEM((LANES, LANES), F32)]
HALF_FLOPS = 5_000_000_000


def invert_first(which, packed, coupling, name):
    shapes = (
        CORNER,
        CORNER,
        CORNER,
        jax.ShapeDtypeStruct((8, R), F32),
        jax.ShapeDtypeStruct((R, LANES), F32),
    )
    kernel = functools.partial(first_kernel, which)
    return call(kernel, shapes, (packed, coupling), name, SCRATCH, HALF_FLOPS)


def invert_second(parts, name):
    return call(second_kernel, SQUARE, parts, name, SCRATCH, HALF_FLOPS)


def half_index():
    return lax.axis_index("group") // 2


def no_index():
    return 0


def panel_solve_kernel(inverse, terms, x_out, root_out):
    cross = load_square(terms, CROSS)
    x = dot_full(inverse[...], cross)
    x_out[...] = x
    store_symmetric(root_out, 0, load_symmetric(terms, ROOT) - dot_t_full(cross, x))


def wide(x):
    high, low = split2(x)
    return jnp.concatenate([high, high, low], axis=1)


def tall(x):
    high, low = split2(x)
    return jnp.concatenate([high, low, high], axis=0)


def by_tiles(rows, out, stage, sems, value):
    tiles = rows // TILE

    def copy(tile):
        return pltpu.make_async_copy(stage.at[tile_at(tile)], out.at[tile_at(tile)], sems.at[tile])

    def step(tile, carry):
        stage[tile_at(tile), :] = value(tile_at(tile))
        copy(tile).start()
        return carry

    lax.fori_loop(0, tiles, step, 0)
    for tile in range(tiles):
        copy(tile).wait()


def panel_kernel(b2, b1, x, out, stage, sems):
    right = tall(x[...])
    by_tiles(b2.shape[0], out, stage, sems, lambda at: b1[at, :] - dot(wide(b2[at, :]), right))


def source_solve_kernel(inverse, x, terms, y_out, side_out):
    projected = load_square(terms, PROJECTED)
    y_out[...] = dot_full(inverse[...], projected)
    store_square(side_out, 0, load_square(terms, SIDE) - dot_t_full(x[...], projected))


def field_kernel(b2, panel, sources, inverse, side, y, out, stage, sems):
    weights = dot(wide(inverse[...]), tall(load_square(side, 0)))
    right = jnp.concatenate([tall(y[...]), tall(weights)], axis=0)

    def value(at):
        left = jnp.concatenate([wide(b2[at, :]), wide(panel[at, :])], axis=1)
        return sources[at, :] - dot(left, right)

    by_tiles(b2.shape[0], out, stage, sems, value)


def update(kernel, args, passes, name):
    rows = args[0].shape[0]
    return pl.pallas_call(
        kernel,
        out_specs=pl.BlockSpec(memory_space=pl.ANY),
        out_shape=jax.ShapeDtypeStruct((rows, R), F32),
        scratch_shapes=[pltpu.VMEM((rows, R), F32), pltpu.SemaphoreType.DMA((rows // TILE,))],
        compiler_params=pltpu.CompilerParams(vmem_limit_bytes=VMEM_LIMIT),
        cost_estimate=cost(passes, rows, 3),
        name=name,
    )(*args)


def exchange(x, mask):
    count = lax.axis_size(AXES)
    return lax.ppermute(x, AXES, [(i, i ^ mask) for i in range(count)])


def choose(x, upper):
    half = half_of(x.shape[0])
    low, high = x[:half], x[x.shape[0] - half :]
    return jnp.where(upper, high, low), jnp.where(upper, low, high)


def join(x, other, rows, upper):
    low, high = jnp.where(upper, other, x), jnp.where(upper, x, other)
    return jnp.concatenate([low[: rows - x.shape[0]], high], axis=0)


def summing_stages(bits):
    down = [("scatter", bit) for bit in bits[:-1]]
    return down + [("sum", bits[-1])] + [("gather", bit) for bit in reversed(bits[:-1])]


class Chain:
    def __init__(self, value, upper):
        self.value, self.upper, self.sizes = value, upper, {}

    def start(self, kind, bit):
        self.kind, self.bit = kind, bit
        sent = self.value
        if kind == "scatter":
            self.sizes[bit] = self.value.shape[0]
            self.value, sent = choose(self.value, self.upper[bit])
        self.flying = exchange(sent, 1 << bit)

    def finish(self):
        if self.kind == "gather":
            self.value = join(self.value, self.flying, self.sizes[self.bit], self.upper[self.bit])
        else:
            self.value = self.value + self.flying


def per_device(q_two, q_one, sources, coupling_two, coupling_one):
    index = lax.axis_index(AXES)
    places = lax.axis_size(AXES).bit_length() - 1
    flags = [(index >> bit) & 1 == 1 for bit in range(places)]
    q_two, *upper = lax.optimization_barrier((q_two, *flags))
    bits = list(range(2, places))
    stages = summing_stages(bits)
    source_left = [("gather", 0)] + summing_stages([bits[1], bits[0], *bits[2:]])[::-1]

    keep, send, b2, b1 = panel_gram(q_two, q_one)
    arriving = exchange(send, 1)
    source_keep, source_send = source_gram(b2, b1, sources)
    arriving, source_send = lax.optimization_barrier((arriving, source_send))

    panels = Chain(keep + arriving, upper)
    source = Chain(source_keep, upper)
    panels.sizes[0], source.sizes[0] = PANEL_TERMS, SOURCE_TERMS
    source.kind, source.bit, source.flying = "sum", 0, exchange(source_send, 1)
    down = len(bits) - 1
    for step, stage in enumerate(stages):
        panels.start(*stage)
        if step == 0:
            source.finish()
        if step < down or step >= down + 2:
            source.start(*source_left.pop())
            panels.flying, source.flying = lax.optimization_barrier((panels.flying, source.flying))
            source.finish()
        panels.finish()
    panels.start("gather", 0)
    source.start(*source_left.pop())
    panels.finish()
    terms = panels.value
    parts = invert_first(half_index, terms, coupling_two, "level_first")
    source.flying, parts = lax.optimization_barrier((source.flying, parts))
    source.finish()
    source.start(*source_left.pop())
    inverse = invert_second(parts, "level_second")
    x, root = call(
        panel_solve_kernel, (SQUARE, jax.ShapeDtypeStruct((SYMMETRIC, LANES), F32)), (inverse, terms), "panel_solve"
    )
    source.flying, x = lax.optimization_barrier((source.flying, x))
    source.finish()
    source.start(*source_left.pop())
    arriving = exchange(root, 2)
    panel_one = update(panel_kernel, [b2, b1, x], 3, "panel")
    arriving, source.flying, panel_one = lax.optimization_barrier((arriving, source.flying, panel_one))
    source.finish()
    full = jax.ShapeDtypeStruct((FULL, LANES), F32)
    y, side = call(source_solve_kernel, (SQUARE, full), (inverse, x, source.value), "source_solve")
    side = Chain(choose(side, upper[0])[0], upper)
    side.sizes[0] = FULL
    side_flying = exchange(side.value, 2)
    root = root + arriving
    parts = invert_first(no_index, root, coupling_one[None], "root_first")
    side_flying, parts = lax.optimization_barrier((side_flying, parts))
    side.value = side.value + side_flying
    side.start("gather", 0)
    inverse = invert_second(parts, "root_second")
    side.finish()
    solution = update(field_kernel, [b2, panel_one, sources, inverse, side.value, y], 6, "field")
    return (panel_one, solution)


def solution(mesh):
    placed = P(("group", "leaf"), None)
    return jax.shard_map(
        per_device,
        mesh=mesh,
        in_specs=(placed, placed, placed, P(), P()),
        out_specs=(placed, placed),
        check_vma=False,
    )
```

```python
import functools

import jax
import jax.numpy as jnp
from jax import lax
from jax.experimental import pallas as pl
from jax.experimental.pallas import tpu as pltpu
from jax.sharding import PartitionSpec as P

HIGH = lax.Precision.HIGHEST
AXES = ("leaf", "group")
F32 = jnp.float32
BF16 = jnp.bfloat16
R = 256
LANES = 128
TILE = 512
GROUPS = 8
VMEM_LIMIT = 16 * 1024 * 1024
SYMMETRIC, FULL = 264, 512
OWN, ROOT, CROSS, PANEL_TERMS = 0, 264, 528, 1040
PROJECTED, SIDE, SOURCE_TERMS = 0, 512, 1024


def split2(x):
    high = x.astype(BF16)
    return high, (x - high.astype(F32)).astype(BF16)


def split3(x):
    high = x.astype(BF16)
    rest = x - high.astype(F32)
    mid = rest.astype(BF16)
    return high, mid, (rest - mid.astype(F32)).astype(BF16)


def dot(left, right):
    return jnp.dot(left, right, preferred_element_type=F32)


def dot_t(left, right):
    return lax.dot_general(left, right, (((0,), (0,)), ((), ())), preferred_element_type=F32)


def dot_full(left, right):
    return jnp.dot(left, right, precision=HIGH, preferred_element_type=F32)


def dot_t_full(left, right):
    return lax.dot_general(
        left, right, (((0,), (0,)), ((), ())), precision=HIGH, preferred_element_type=F32
    )


def square_index():
    row = lax.broadcasted_iota(jnp.int32, (LANES, LANES), 0)
    return row, lax.broadcasted_iota(jnp.int32, (LANES, LANES), 1)


def store_symmetric(ref, at, block):
    row, col = square_index()
    last = block[128:, 128:]
    ref[at : at + 128, :] = block[128:, :128]
    ref[at + 128 : at + 256, :] = jnp.where(row >= col, block[:128, :128], last)
    diagonal = jnp.sum(jnp.where(row == col, last, 0.0), axis=0, keepdims=True)
    ref[at + 256 : at + 264, :] = jnp.broadcast_to(diagonal, (8, LANES))


def store_square(ref, row, block):
    ref[row : row + 256, :] = block[:, :128]
    ref[row + 256 : row + 512, :] = block[:, 128:]


def load_symmetric(ref, at):
    row, col = square_index()
    lower = ref[at : at + 128, :]
    mixed = ref[at + 128 : at + 256, :]
    turned = mixed.T
    first = jnp.where(row >= col, mixed, turned)
    last = jnp.where(row < col, mixed, turned)
    last = jnp.where(row == col, ref[at + 256 : at + 257, :], last)
    top = jnp.concatenate([first, lower.T], axis=1)
    return jnp.concatenate([top, jnp.concatenate([lower, last], axis=1)], axis=0)


def load_square(ref, row):
    return jnp.concatenate([ref[row : row + 256, :], ref[row + 256 : row + 512, :]], axis=1)


def half_of(rows):
    return (rows + 15) // 16 * 8


def store_halves(packed, keep, send):
    half = half_of(packed.shape[0])
    far = packed.shape[0] - half
    mine = lax.rem(lax.axis_index("group"), 2)
    keep[...] = packed[pl.ds(pl.multiple_of(mine * far, 8), half), :]
    send[...] = packed[pl.ds(pl.multiple_of((1 - mine) * far, 8), half), :]


def tile_at(tile):
    return pl.ds(pl.multiple_of(tile * TILE, TILE), TILE)


def panel_gram_kernel(q_two, q_one, keep, send, b2, b1, acc, packed, sems):
    tiles = b2.shape[0] // TILE
    pairs = ((q_two, b2), (q_one, b1))

    def copies(at, sem):
        return [
            pltpu.make_async_copy(source.at[at], target.at[at], sems.at[which, sem])
            for which, (source, target) in enumerate(pairs)
        ]

    small = TILE // 2
    parts = (pl.ds(0, small), pl.ds(small, small))
    for sem, at in enumerate(parts):
        for copy in copies(at, sem):
            copy.start()
    for tile in range(1, tiles):
        for copy in copies(tile_at(tile), tile + 1):
            copy.start()
    acc[...] = jnp.zeros_like(acc)

    def add_rows(at, sem):
        for copy in copies(at, sem):
            copy.wait()
        h2, l2 = split2(b2[at, :])
        h1, l1 = split2(b1[at, :])
        h2t, l2t, h1t = h2.T, l2.T, h1.T
        acc[0] += dot(h2t, h2)
        acc[1] += dot(h2t, l2)
        left = jnp.concatenate([h2t, h2t, l2t], axis=1)
        acc[2] += dot(left, jnp.concatenate([h1, l1, h1], axis=0))
        acc[3] += dot(h1t, h1)
        acc[4] += dot(h1t, l1)

    def step(tile, carry):
        add_rows(tile_at(tile), tile + 1)
        return carry

    for sem, at in enumerate(parts):
        add_rows(at, sem)
    lax.fori_loop(1, tiles, step, 0)
    low = acc[1]
    store_symmetric(packed, OWN, acc[0] + low + low.T)
    low = acc[4]
    store_symmetric(packed, ROOT, acc[3] + low + low.T)
    store_square(packed, CROSS, acc[2])
    store_halves(packed, keep, send)


def source_gram_kernel(b2, b1, sources, keep, send, acc, packed):
    acc[...] = jnp.zeros_like(acc)

    def step(tile, carry):
        hs, ls = split2(sources[tile_at(tile), :])
        right = jnp.concatenate([hs, ls, hs], axis=0)
        for which, panel in enumerate((b2, b1)):
            high, low = split2(panel[tile_at(tile), :])
            turned = high.T
            acc[which] += dot(jnp.concatenate([turned, turned, low.T], axis=1), right)
        return carry

    lax.fori_loop(0, b2.shape[0] // TILE, step, 0)
    store_square(packed, PROJECTED, acc[0])
    store_square(packed, SIDE, acc[1])
    store_halves(packed, keep, send)


def cost(passes, rows, arrays):
    return pl.CostEstimate(
        flops=2 * passes * rows * R * R, bytes_accessed=4 * arrays * rows * R, transcendentals=0
    )


def panel_gram(q_two, q_one):
    rows = q_two.shape[0]
    part = jax.ShapeDtypeStruct((half_of(PANEL_TERMS), LANES), F32)
    tall = jax.ShapeDtypeStruct((rows, R), F32)
    return pl.pallas_call(
        panel_gram_kernel,
        in_specs=[pl.BlockSpec(memory_space=pl.ANY)] * 2,
        out_shape=(part, part, tall, tall),
        scratch_shapes=[
            pltpu.VMEM((5, R, R), F32),
            pltpu.VMEM((PANEL_TERMS, LANES), F32),
            pltpu.SemaphoreType.DMA((2, rows // TILE + 1)),
        ],
        compiler_params=pltpu.CompilerParams(vmem_limit_bytes=VMEM_LIMIT),
        cost_estimate=cost(7, rows, 2),
        name="panel_gram",
    )(pltpu.with_memory_space_constraint(q_two, pltpu.HBM), pltpu.with_memory_space_constraint(q_one, pltpu.HBM))


def source_gram(b2, b1, sources):
    part = jax.ShapeDtypeStruct((half_of(SOURCE_TERMS), LANES), F32)
    return pl.pallas_call(
        source_gram_kernel,
        out_shape=(part, part),
        scratch_shapes=[pltpu.VMEM((2, R, R), F32), pltpu.VMEM((SOURCE_TERMS, LANES), F32)],
        compiler_params=pltpu.CompilerParams(vmem_limit_bytes=VMEM_LIMIT),
        cost_estimate=cost(6, b2.shape[0], 3),
        name="source_gram",
    )(b2, b1, sources)


def spread_lane(x, lane):
    return jnp.broadcast_to(x[:, lane : lane + 1], (8, LANES))


def eliminate(block, cols, rows):
    count = len(block)
    lane = lax.broadcasted_iota(jnp.int32, (8, LANES), 1)
    for start in range(0, count, GROUPS):
        panel = block[start : start + GROUPS]
        left = stack_left(jnp.concatenate(panel, axis=0))
        for t in range(GROUPS):
            panel = eliminate_group(panel, t, start + t, cols, rows)
        inside = (lane >= 8 * start) & (lane < 8 * (start + GROUPS))
        panel = [jnp.where(inside, -x, x) for x in panel]
        change = dot_t(left, stack_right(jnp.concatenate(panel, axis=0)))
        for g in range(count):
            if start <= g < start + GROUPS:
                block[g] = panel[g - start]
            else:
                block[g] = jnp.where(inside, 0.0, block[g]) - change[8 * g : 8 * g + 8, :]
    return [-x for x in block]


def eliminate_group(panel, t, at, cols, rows):
    lane = lax.broadcasted_iota(jnp.int32, (8, LANES), 1)
    sub = lax.broadcasted_iota(jnp.int32, (8, LANES), 0)
    for j in range(8):
        cols[64 * at + 8 * j : 64 * at + 8 * j + 8, :] = spread_lane(panel[t], 8 * at + j)
    rows[8 * at : 8 * at + 8, :] = panel[t]
    entry = {}
    for i in range(8):
        for j in range(i + 1):
            row = 64 * at + 8 * j + i
            entry[i, j] = jnp.broadcast_to(cols[row : row + 1, :], (8, LANES))
    inside = (lane >= 8 * at) & (lane < 8 * at + 8)
    line = []
    for j in range(8):
        row = jnp.broadcast_to(rows[8 * at + j : 8 * at + j + 1, :], (8, LANES))
        line.append(jnp.where(inside, jnp.where(lane == 8 * at + j, 1.0, 0.0), row))
    after = None
    if t < GROUPS - 1:
        columns = [spread_lane(panel[t + 1], 8 * at + j) for j in range(8)]
        after = [columns, jnp.where(inside, 0.0, panel[t + 1])]
    line, after = solve_small(entry, line, after)
    for g in range(GROUPS):
        if g == t + 1:
            panel[g] = after
        elif g != t:
            terms = [spread_lane(panel[g], 8 * at + j) * line[j] for j in range(8)]
            panel[g] = jnp.where(inside, 0.0, panel[g]) - tree_sum(terms)
    merged = line[0]
    for j in range(1, 8):
        merged = jnp.where(sub == j, line[j], merged)
    panel[t] = merged
    return panel


def tree_sum(terms):
    while len(terms) > 1:
        terms = [
            terms[i] + terms[i + 1] if i + 1 < len(terms) else terms[i]
            for i in range(0, len(terms), 2)
        ]
    return terms[0]


def solve_small(entry, line, after):
    columns, block = after or (None, None)
    factors, scaled = {}, {}
    for k in range(0, 8, 2):
        a, b, c = entry[k, k], entry[k + 1, k], entry[k + 1, k + 1]
        inv = pl.reciprocal(a * c - b * b, approx=True)
        below = range(k + 2, 8)
        first = {i: c * entry[i, k] - b * entry[i, k + 1] for i in below}
        second = {i: a * entry[i, k + 1] - b * entry[i, k] for i in below}
        for i in below:
            for j in range(k + 2, i + 1):
                entry[i, j] = entry[i, j] - inv * (first[i] * entry[j, k] + second[i] * entry[j, k + 1])
        top = c * line[k] - b * line[k + 1]
        bottom = a * line[k + 1] - b * line[k]
        if columns is not None:
            block = block - inv * (columns[k] * top + columns[k + 1] * bottom)
        scaled[k], scaled[k + 1] = inv * top, inv * bottom
        for i in below:
            m, n = inv * first[i], inv * second[i]
            factors[i, k] = m, n
            line[i] = line[i] - (m * line[k] + n * line[k + 1])
            if columns is not None:
                columns[i] = columns[i] - (m * columns[k] + n * columns[k + 1])
    for k in range(6, -1, -2):
        x, y = scaled[k], scaled[k + 1]
        if k < 6:
            x = x - tree_sum([factors[i, k][0] * line[i] for i in range(k + 2, 8)])
            y = y - tree_sum([factors[i, k][1] * line[i] for i in range(k + 2, 8)])
        line[k], line[k + 1] = x, y
    return line, block


def stack_left(x):
    h, m, l = split3(x)
    return jnp.concatenate([h, h, m, h, l, m], axis=0)


def stack_right(x):
    h, m, l = split3(x)
    return jnp.concatenate([h, m, h, l, h, m], axis=0)


def invert_half(matrix, cols, rows):
    block = eliminate([matrix[8 * i : 8 * i + 8, :] for i in range(LANES // 8)], cols, rows)
    return jnp.concatenate(block, axis=0)


SQUARE = jax.ShapeDtypeStruct((R, R), F32)
CORNER = jax.ShapeDtypeStruct((LANES, LANES), F32)


def call(kernel, out_shape, args, name, scratch=(), flops=0):
    return pl.pallas_call(
        kernel,
        out_shape=out_shape,
        scratch_shapes=list(scratch),
        compiler_params=pltpu.CompilerParams(vmem_limit_bytes=VMEM_LIMIT),
        cost_estimate=pl.CostEstimate(flops=flops, bytes_accessed=R * R * 4, transcendentals=0),
        name=name,
    )(*args)


def first_kernel(which, gram_ref, coupling, first_out, across_out, rest_out, row_out, col_out, cols, rows):
    matrix = coupling[which()] + load_symmetric(gram_ref, OWN)
    eye = lax.broadcasted_iota(jnp.int32, (R, R), 0) == lax.broadcasted_iota(jnp.int32, (R, R), 1)
    diagonal = jnp.where(eye, matrix, 0.0)
    scale_row = lax.rsqrt(jnp.sum(diagonal, axis=0, keepdims=True))
    scale_col = lax.rsqrt(jnp.sum(diagonal, axis=1, keepdims=True))
    matrix = matrix * scale_col * scale_row
    side = matrix[:LANES, LANES:]
    first = invert_half(matrix[:LANES, :LANES], cols, rows)
    across = dot_full(first, side)
    first_out[...] = first
    across_out[...] = across
    rest_out[...] = matrix[LANES:, LANES:] - dot_t_full(side, across)
    row_out[...] = jnp.broadcast_to(scale_row, (8, R))
    col_out[...] = jnp.broadcast_to(scale_col, (R, LANES))


def second_kernel(first, across, rest, row, col, out, cols, rows):
    second = invert_half(rest[...], cols, rows)
    corner = -dot_full(across[...], second)
    top = first[...] - dot_full(corner, across[...].T)
    out[:LANES, :LANES] = top * col[:LANES, :] * row[:1, :LANES]
    out[:LANES, LANES:] = corner * col[:LANES, :] * row[:1, LANES:]
    out[LANES:, :LANES] = corner.T * col[LANES:, :] * row[:1, :LANES]
    out[LANES:, LANES:] = second * col[LANES:, :] * row[:1, LANES:]


SCRATCH = [pltpu.VMEM((1024, LANES), F32), pltpu.VMEM((LANES, LANES), F32)]
HALF_FLOPS = 5_000_000_000


def invert_first(which, packed, coupling, name):
    shapes = (
        CORNER,
        CORNER,
        CORNER,
        jax.ShapeDtypeStruct((8, R), F32),
        jax.ShapeDtypeStruct((R, LANES), F32),
    )
    kernel = functools.partial(first_kernel, which)
    return call(kernel, shapes, (packed, coupling), name, SCRATCH, HALF_FLOPS)


def invert_second(parts, name):
    return call(second_kernel, SQUARE, parts, name, SCRATCH, HALF_FLOPS)


def half_index():
    return lax.axis_index("group") // 2


def no_index():
    return 0


def panel_solve_kernel(inverse, terms, x_out, root_out):
    cross = load_square(terms, CROSS)
    x = dot_full(inverse[...], cross)
    x_out[...] = x
    store_symmetric(root_out, 0, load_symmetric(terms, ROOT) - dot_t_full(cross, x))


def wide(x):
    high, low = split2(x)
    return jnp.concatenate([high, high, low], axis=1)


def tall(x):
    high, low = split2(x)
    return jnp.concatenate([high, low, high], axis=0)


def by_tiles(rows, out, stage, sems, value, beside=None):
    tiles = rows // TILE

    def copy(tile):
        return pltpu.make_async_copy(stage.at[tile_at(tile)], out.at[tile_at(tile)], sems.at[tile])

    def step(tile, carry):
        stage[tile_at(tile), :] = value(tile_at(tile))
        copy(tile).start()
        return carry

    lax.fori_loop(0, tiles, step, 0)
    if beside is not None:
        beside()
    for tile in range(tiles):
        copy(tile).wait()


def panel_kernel(b2, b1, sources, x, inverse, terms, out, level, high, low, side_out, stage, sems):
    projected = load_square(terms, PROJECTED)
    y = dot_full(inverse[...], projected)
    store_square(side_out, 0, load_square(terms, SIDE) - dot_t_full(x[...], projected))
    right = jnp.concatenate([tall(x[...]), tall(y)], axis=1)

    def value(at):
        change = dot(wide(b2[at, :]), right)
        panel = b1[at, :] - change[:, :R]
        level[at, :] = sources[at, :] - change[:, R:]
        high[at, :], low[at, :] = split2(panel)
        return panel

    by_tiles(b2.shape[0], out, stage, sems, value)


def field_kernel(level, high, low, inverse, side, out, stage, sems):
    weights = tall(dot(wide(inverse[...]), tall(load_square(side, 0))))

    def value(at):
        left = jnp.concatenate([high[at, :], high[at, :], low[at, :]], axis=1)
        return level[at, :] - dot(left, weights)

    by_tiles(level.shape[0], out, stage, sems, value)


def update(kernel, args, passes, name, more=()):
    rows = args[0].shape[0]
    return pl.pallas_call(
        kernel,
        out_specs=[pl.BlockSpec(memory_space=pl.ANY)] + [pl.BlockSpec(memory_space=pltpu.VMEM)] * len(more),
        out_shape=[jax.ShapeDtypeStruct((rows, R), F32), *more],
        scratch_shapes=[pltpu.VMEM((rows, R), F32), pltpu.SemaphoreType.DMA((rows // TILE,))],
        compiler_params=pltpu.CompilerParams(vmem_limit_bytes=VMEM_LIMIT),
        cost_estimate=cost(passes, rows, 3),
        name=name,
    )(*args)


def exchange(x, mask):
    count = lax.axis_size(AXES)
    return lax.ppermute(x, AXES, [(i, i ^ mask) for i in range(count)])


def choose(x, upper):
    half = half_of(x.shape[0])
    low, high = x[:half], x[x.shape[0] - half :]
    return jnp.where(upper, high, low), jnp.where(upper, low, high)


def join(x, other, rows, upper):
    low, high = jnp.where(upper, other, x), jnp.where(upper, x, other)
    return jnp.concatenate([low[: rows - x.shape[0]], high], axis=0)


def summing_stages(bits):
    down = [("scatter", bit) for bit in bits[:-1]]
    return down + [("sum", bits[-1])] + [("gather", bit) for bit in reversed(bits[:-1])]


class Chain:
    def __init__(self, value, upper):
        self.value, self.upper, self.sizes = value, upper, {}

    def start(self, kind, bit):
        self.kind, self.bit = kind, bit
        sent = self.value
        if kind == "scatter":
            self.sizes[bit] = self.value.shape[0]
            self.value, sent = choose(self.value, self.upper[bit])
        self.flying = exchange(sent, 1 << bit)

    def finish(self):
        if self.kind == "gather":
            self.value = join(self.value, self.flying, self.sizes[self.bit], self.upper[self.bit])
        else:
            self.value = self.value + self.flying


def per_device(q_two, q_one, sources, coupling_two, coupling_one):
    index = lax.axis_index(AXES)
    places = lax.axis_size(AXES).bit_length() - 1
    flags = [(index >> bit) & 1 == 1 for bit in range(places)]
    q_two, *upper = lax.optimization_barrier((q_two, *flags))
    stages = summing_stages(list(range(2, places)))

    keep, send, b2, b1 = panel_gram(q_two, q_one)
    arriving = exchange(send, 1)
    source_keep, source_send = source_gram(b2, b1, sources)
    arriving, source_send = lax.optimization_barrier((arriving, source_send))

    panels = Chain(keep + arriving, upper)
    source = Chain(source_keep, upper)
    panels.sizes[0], source.sizes[0] = PANEL_TERMS, SOURCE_TERMS
    source_left = [("gather", 0)] + stages[::-1]
    for step, stage in enumerate(stages):
        panels.start(*stage)
        if step == 0:
            source.kind, source.bit, source.flying = "sum", 0, exchange(source_send, 1)
        else:
            source.start(*source_left.pop())
        panels.flying, source.flying = lax.optimization_barrier((panels.flying, source.flying))
        panels.finish()
        source.finish()
    panels.start("gather", 0)
    source.start(*source_left.pop())
    panels.finish()
    terms = panels.value
    parts = invert_first(half_index, terms, coupling_two, "level_first")
    source.flying, parts = lax.optimization_barrier((source.flying, parts))
    source.finish()
    source.start(*source_left.pop())
    inverse = invert_second(parts, "level_second")
    source.flying, inverse = lax.optimization_barrier((source.flying, inverse))
    source.finish()

    x, root = call(
        panel_solve_kernel, (SQUARE, jax.ShapeDtypeStruct((SYMMETRIC, LANES), F32)), (inverse, terms), "panel_solve"
    )
    arriving = exchange(root, 2)
    rows = b2.shape[0]
    shapes = [jax.ShapeDtypeStruct((rows, R), kind) for kind in (F32, BF16, BF16)]
    shapes.append(jax.ShapeDtypeStruct((FULL, LANES), F32))
    args = [b2, b1, sources, x, inverse, source.value]
    panel_one, level, high, low, side = update(panel_kernel, args, 8, "panel", shapes)
    side = Chain(choose(side, upper[0])[0], upper)
    side.sizes[0] = FULL
    side_flying = exchange(side.value, 2)
    arriving, side.value = lax.optimization_barrier((arriving, side.value))
    root = root + arriving
    parts = invert_first(no_index, root, coupling_one[None], "root_first")
    side_flying, parts = lax.optimization_barrier((side_flying, parts))
    side.value = side.value + side_flying
    side.start("gather", 0)
    inverse = invert_second(parts, "root_second")
    side.finish()
    (solution,) = update(field_kernel, [level, high, low, inverse, side.value], 3, "field")
    return (panel_one, solution)


def solution(mesh):
    placed = P(("group", "leaf"), None)
    return jax.shard_map(
        per_device,
        mesh=mesh,
        in_specs=(placed, placed, placed, P(), P()),
        out_specs=(placed, placed),
        check_vma=False,
    )
```

```python
import functools

import jax
import jax.numpy as jnp
from jax import lax
from jax.experimental import pallas as pl
from jax.experimental.pallas import tpu as pltpu
from jax.sharding import PartitionSpec as P

HIGH = lax.Precision.HIGHEST
AXES = ("leaf", "group")
F32 = jnp.float32
BF16 = jnp.bfloat16
R = 256
LANES = 128
TILE = 512
GROUPS = 8
VMEM_LIMIT = 16 * 1024 * 1024
SYMMETRIC, FULL = 264, 512
OWN, ROOT, CROSS, PANEL_TERMS = 0, 264, 528, 1040
PROJECTED, SIDE, SOURCE_TERMS = 0, 512, 1024


def split2(x):
    high = x.astype(BF16)
    return high, (x - high.astype(F32)).astype(BF16)


def split3(x):
    high = x.astype(BF16)
    rest = x - high.astype(F32)
    mid = rest.astype(BF16)
    return high, mid, (rest - mid.astype(F32)).astype(BF16)


def dot(left, right):
    return jnp.dot(left, right, preferred_element_type=F32)


def dot_t(left, right):
    return lax.dot_general(left, right, (((0,), (0,)), ((), ())), preferred_element_type=F32)


def dot_full(left, right):
    return jnp.dot(left, right, precision=HIGH, preferred_element_type=F32)


def dot_t_full(left, right):
    return lax.dot_general(
        left, right, (((0,), (0,)), ((), ())), precision=HIGH, preferred_element_type=F32
    )


def square_index():
    row = lax.broadcasted_iota(jnp.int32, (LANES, LANES), 0)
    return row, lax.broadcasted_iota(jnp.int32, (LANES, LANES), 1)


def store_symmetric(ref, at, block):
    row, col = square_index()
    last = block[128:, 128:]
    ref[at : at + 128, :] = block[128:, :128]
    ref[at + 128 : at + 256, :] = jnp.where(row >= col, block[:128, :128], last)
    diagonal = jnp.sum(jnp.where(row == col, last, 0.0), axis=0, keepdims=True)
    ref[at + 256 : at + 264, :] = jnp.broadcast_to(diagonal, (8, LANES))


def store_square(ref, row, block):
    ref[row : row + 256, :] = block[:, :128]
    ref[row + 256 : row + 512, :] = block[:, 128:]


def load_symmetric(ref, at):
    row, col = square_index()
    lower = ref[at : at + 128, :]
    mixed = ref[at + 128 : at + 256, :]
    turned = mixed.T
    first = jnp.where(row >= col, mixed, turned)
    last = jnp.where(row < col, mixed, turned)
    last = jnp.where(row == col, ref[at + 256 : at + 257, :], last)
    top = jnp.concatenate([first, lower.T], axis=1)
    return jnp.concatenate([top, jnp.concatenate([lower, last], axis=1)], axis=0)


def load_square(ref, row):
    return jnp.concatenate([ref[row : row + 256, :], ref[row + 256 : row + 512, :]], axis=1)


def half_of(rows):
    return (rows + 15) // 16 * 8


def store_halves(packed, keep, send):
    half = half_of(packed.shape[0])
    far = packed.shape[0] - half
    mine = lax.rem(lax.axis_index("group"), 2)
    keep[...] = packed[pl.ds(pl.multiple_of(mine * far, 8), half), :]
    send[...] = packed[pl.ds(pl.multiple_of((1 - mine) * far, 8), half), :]


def tile_at(tile):
    return pl.ds(pl.multiple_of(tile * TILE, TILE), TILE)


def panel_gram_kernel(q_two, q_one, keep, send, b2, b1, acc, packed, sems):
    tiles = b2.shape[0] // TILE
    pairs = ((q_two, b2), (q_one, b1))

    def copies(at, sem):
        return [
            pltpu.make_async_copy(source.at[at], target.at[at], sems.at[which, sem])
            for which, (source, target) in enumerate(pairs)
        ]

    small = TILE // 2
    parts = (pl.ds(0, small), pl.ds(small, small))
    for sem, at in enumerate(parts):
        for copy in copies(at, sem):
            copy.start()
    for tile in range(1, tiles):
        for copy in copies(tile_at(tile), tile + 1):
            copy.start()
    acc[...] = jnp.zeros_like(acc)

    def add_rows(at, sem):
        for copy in copies(at, sem):
            copy.wait()
        h2, l2 = split2(b2[at, :])
        h1, l1 = split2(b1[at, :])
        h2t, l2t, h1t = h2.T, l2.T, h1.T
        acc[0] += dot(h2t, h2)
        acc[1] += dot(h2t, l2)
        left = jnp.concatenate([h2t, h2t, l2t], axis=1)
        acc[2] += dot(left, jnp.concatenate([h1, l1, h1], axis=0))
        acc[3] += dot(h1t, h1)
        acc[4] += dot(h1t, l1)

    def step(tile, carry):
        add_rows(tile_at(tile), tile + 1)
        return carry

    for sem, at in enumerate(parts):
        add_rows(at, sem)
    lax.fori_loop(1, tiles, step, 0)
    low = acc[1]
    store_symmetric(packed, OWN, acc[0] + low + low.T)
    low = acc[4]
    store_symmetric(packed, ROOT, acc[3] + low + low.T)
    store_square(packed, CROSS, acc[2])
    store_halves(packed, keep, send)


def source_gram_kernel(b2, b1, sources, keep, send, acc, packed):
    acc[...] = jnp.zeros_like(acc)

    def step(tile, carry):
        hs, ls = split2(sources[tile_at(tile), :])
        right = jnp.concatenate([hs, ls, hs], axis=0)
        for which, panel in enumerate((b2, b1)):
            high, low = split2(panel[tile_at(tile), :])
            turned = high.T
            acc[which] += dot(jnp.concatenate([turned, turned, low.T], axis=1), right)
        return carry

    lax.fori_loop(0, b2.shape[0] // TILE, step, 0)
    store_square(packed, PROJECTED, acc[0])
    store_square(packed, SIDE, acc[1])
    store_halves(packed, keep, send)


def cost(passes, rows, arrays):
    return pl.CostEstimate(
        flops=2 * passes * rows * R * R, bytes_accessed=4 * arrays * rows * R, transcendentals=0
    )


def panel_gram(q_two, q_one):
    rows = q_two.shape[0]
    part = jax.ShapeDtypeStruct((half_of(PANEL_TERMS), LANES), F32)
    tall = jax.ShapeDtypeStruct((rows, R), F32)
    return pl.pallas_call(
        panel_gram_kernel,
        in_specs=[pl.BlockSpec(memory_space=pl.ANY)] * 2,
        out_shape=(part, part, tall, tall),
        scratch_shapes=[
            pltpu.VMEM((5, R, R), F32),
            pltpu.VMEM((PANEL_TERMS, LANES), F32),
            pltpu.SemaphoreType.DMA((2, rows // TILE + 1)),
        ],
        compiler_params=pltpu.CompilerParams(vmem_limit_bytes=VMEM_LIMIT),
        cost_estimate=cost(7, rows, 2),
        name="panel_gram",
    )(pltpu.with_memory_space_constraint(q_two, pltpu.HBM), pltpu.with_memory_space_constraint(q_one, pltpu.HBM))


def source_gram(b2, b1, sources):
    part = jax.ShapeDtypeStruct((half_of(SOURCE_TERMS), LANES), F32)
    return pl.pallas_call(
        source_gram_kernel,
        out_shape=(part, part),
        scratch_shapes=[pltpu.VMEM((2, R, R), F32), pltpu.VMEM((SOURCE_TERMS, LANES), F32)],
        compiler_params=pltpu.CompilerParams(vmem_limit_bytes=VMEM_LIMIT),
        cost_estimate=cost(6, b2.shape[0], 3),
        name="source_gram",
    )(b2, b1, sources)


def spread_lane(x, lane):
    return jnp.broadcast_to(x[:, lane : lane + 1], (8, LANES))


def sweep_panel(block, start, cols, rows):
    lane = lax.broadcasted_iota(jnp.int32, (8, LANES), 1)
    panel = block[start : start + GROUPS]
    left = stack_left(jnp.concatenate(panel, axis=0))
    for t in range(GROUPS):
        panel = eliminate_group(panel, t, start + t, cols, rows)
    inside = (lane >= 8 * start) & (lane < 8 * (start + GROUPS))
    panel = [jnp.where(inside, -x, x) for x in panel]
    change = dot_t(left, stack_right(jnp.concatenate(panel, axis=0)))
    swept = []
    for g in range(len(block)):
        if start <= g < start + GROUPS:
            swept.append(panel[g - start])
        else:
            swept.append(jnp.where(inside, 0.0, block[g]) - change[8 * g : 8 * g + 8, :])
    return swept


def eliminate_group(panel, t, at, cols, rows):
    lane = lax.broadcasted_iota(jnp.int32, (8, LANES), 1)
    sub = lax.broadcasted_iota(jnp.int32, (8, LANES), 0)
    for j in range(8):
        cols[64 * at + 8 * j : 64 * at + 8 * j + 8, :] = spread_lane(panel[t], 8 * at + j)
    rows[8 * at : 8 * at + 8, :] = panel[t]
    entry = {}
    for i in range(8):
        for j in range(i + 1):
            row = 64 * at + 8 * j + i
            entry[i, j] = jnp.broadcast_to(cols[row : row + 1, :], (8, LANES))
    inside = (lane >= 8 * at) & (lane < 8 * at + 8)
    line = []
    for j in range(8):
        row = jnp.broadcast_to(rows[8 * at + j : 8 * at + j + 1, :], (8, LANES))
        line.append(jnp.where(inside, jnp.where(lane == 8 * at + j, 1.0, 0.0), row))
    after = None
    if t < GROUPS - 1:
        columns = [spread_lane(panel[t + 1], 8 * at + j) for j in range(8)]
        after = [columns, jnp.where(inside, 0.0, panel[t + 1])]
    line, after = solve_small(entry, line, after)
    for g in range(GROUPS):
        if g == t + 1:
            panel[g] = after
        elif g != t:
            terms = [spread_lane(panel[g], 8 * at + j) * line[j] for j in range(8)]
            panel[g] = jnp.where(inside, 0.0, panel[g]) - tree_sum(terms)
    merged = line[0]
    for j in range(1, 8):
        merged = jnp.where(sub == j, line[j], merged)
    panel[t] = merged
    return panel


def tree_sum(terms):
    while len(terms) > 1:
        terms = [
            terms[i] + terms[i + 1] if i + 1 < len(terms) else terms[i]
            for i in range(0, len(terms), 2)
        ]
    return terms[0]


def solve_small(entry, line, after):
    columns, block = after or (None, None)
    factors, scaled = {}, {}
    for k in range(0, 8, 2):
        a, b, c = entry[k, k], entry[k + 1, k], entry[k + 1, k + 1]
        inv = pl.reciprocal(a * c - b * b, approx=True)
        below = range(k + 2, 8)
        first = {i: c * entry[i, k] - b * entry[i, k + 1] for i in below}
        second = {i: a * entry[i, k + 1] - b * entry[i, k] for i in below}
        for i in below:
            for j in range(k + 2, i + 1):
                entry[i, j] = entry[i, j] - inv * (first[i] * entry[j, k] + second[i] * entry[j, k + 1])
        top = c * line[k] - b * line[k + 1]
        bottom = a * line[k + 1] - b * line[k]
        if columns is not None:
            block = block - inv * (columns[k] * top + columns[k + 1] * bottom)
        scaled[k], scaled[k + 1] = inv * top, inv * bottom
        for i in below:
            m, n = inv * first[i], inv * second[i]
            factors[i, k] = m, n
            line[i] = line[i] - (m * line[k] + n * line[k + 1])
            if columns is not None:
                columns[i] = columns[i] - (m * columns[k] + n * columns[k + 1])
    for k in range(6, -1, -2):
        x, y = scaled[k], scaled[k + 1]
        if k < 6:
            x = x - tree_sum([factors[i, k][0] * line[i] for i in range(k + 2, 8)])
            y = y - tree_sum([factors[i, k][1] * line[i] for i in range(k + 2, 8)])
        line[k], line[k + 1] = x, y
    return line, block


def stack_left(x):
    h, m, l = split3(x)
    return jnp.concatenate([h, h, m, h, l, m], axis=0)


def stack_right(x):
    h, m, l = split3(x)
    return jnp.concatenate([h, m, h, l, h, m], axis=0)


def sweep(matrix, panels, cols, rows):
    block = [matrix[8 * i : 8 * i + 8, :] for i in range(LANES // 8)]
    for panel in panels:
        block = sweep_panel(block, panel * GROUPS, cols, rows)
    return jnp.concatenate(block, axis=0)


PANELS = LANES // (8 * GROUPS)


SQUARE = jax.ShapeDtypeStruct((R, R), F32)
CORNER = jax.ShapeDtypeStruct((LANES, LANES), F32)


def call(kernel, out_shape, args, name, scratch=(), flops=0):
    return pl.pallas_call(
        kernel,
        out_shape=out_shape,
        scratch_shapes=list(scratch),
        compiler_params=pltpu.CompilerParams(vmem_limit_bytes=VMEM_LIMIT),
        cost_estimate=pl.CostEstimate(flops=flops, bytes_accessed=R * R * 4, transcendentals=0),
        name=name,
    )(*args)


def first_kernel(which, gram_ref, coupling, first_out, across_out, rest_out, row_out, col_out, cols, rows):
    matrix = coupling[which()] + load_symmetric(gram_ref, OWN)
    eye = lax.broadcasted_iota(jnp.int32, (R, R), 0) == lax.broadcasted_iota(jnp.int32, (R, R), 1)
    diagonal = jnp.where(eye, matrix, 0.0)
    scale_row = lax.rsqrt(jnp.sum(diagonal, axis=0, keepdims=True))
    scale_col = lax.rsqrt(jnp.sum(diagonal, axis=1, keepdims=True))
    matrix = matrix * scale_col * scale_row
    side = matrix[:LANES, LANES:]
    first = -sweep(matrix[:LANES, :LANES], range(PANELS), cols, rows)
    across = dot_full(first, side)
    first_out[...] = first
    across_out[...] = across
    rest_out[...] = matrix[LANES:, LANES:] - dot_t_full(side, across)
    row_out[...] = jnp.broadcast_to(scale_row, (8, R))
    col_out[...] = jnp.broadcast_to(scale_col, (R, LANES))


def middle_kernel(rest, out, cols, rows):
    out[...] = sweep(rest[...], range(PANELS - 1), cols, rows)


def second_kernel(first, across, swept, row, col, out, cols, rows):
    second = -sweep(swept[...], range(PANELS - 1, PANELS), cols, rows)
    corner = -dot_full(across[...], second)
    top = first[...] - dot_full(corner, across[...].T)
    out[:LANES, :LANES] = top * col[:LANES, :] * row[:1, :LANES]
    out[:LANES, LANES:] = corner * col[:LANES, :] * row[:1, LANES:]
    out[LANES:, :LANES] = corner.T * col[LANES:, :] * row[:1, :LANES]
    out[LANES:, LANES:] = second * col[LANES:, :] * row[:1, LANES:]


SCRATCH = [pltpu.VMEM((1024, LANES), F32), pltpu.VMEM((LANES, LANES), F32)]
HALF_FLOPS = 5_000_000_000


def invert_first(which, packed, coupling, name):
    shapes = (
        CORNER,
        CORNER,
        CORNER,
        jax.ShapeDtypeStruct((8, R), F32),
        jax.ShapeDtypeStruct((R, LANES), F32),
    )
    kernel = functools.partial(first_kernel, which)
    return call(kernel, shapes, (packed, coupling), name, SCRATCH, HALF_FLOPS)


def invert_middle(parts, name):
    first, across, rest, row, col = parts
    rest = call(middle_kernel, CORNER, (rest,), name, SCRATCH, HALF_FLOPS // 2)
    return first, across, rest, row, col


def invert_second(parts, name):
    return call(second_kernel, SQUARE, parts, name, SCRATCH, HALF_FLOPS // 2)


def half_index():
    return lax.axis_index("group") // 2


def no_index():
    return 0


def panel_solve_kernel(inverse, terms, x_out, root_out):
    cross = load_square(terms, CROSS)
    x = dot_full(inverse[...], cross)
    x_out[...] = x
    store_symmetric(root_out, 0, load_symmetric(terms, ROOT) - dot_t_full(cross, x))


def wide(x):
    high, low = split2(x)
    return jnp.concatenate([high, high, low], axis=1)


def tall(x):
    high, low = split2(x)
    return jnp.concatenate([high, low, high], axis=0)


def by_tiles(rows, out, stage, sems, value, beside=None):
    tiles = rows // TILE

    def copy(tile):
        return pltpu.make_async_copy(stage.at[tile_at(tile)], out.at[tile_at(tile)], sems.at[tile])

    def step(tile, carry):
        stage[tile_at(tile), :] = value(tile_at(tile))
        copy(tile).start()
        return carry

    lax.fori_loop(0, tiles, step, 0)
    if beside is not None:
        beside()
    for tile in range(tiles):
        copy(tile).wait()


def panel_kernel(b2, b1, sources, x, inverse, terms, out, level, high, low, side_out, stage, sems):
    projected = load_square(terms, PROJECTED)
    y = dot_full(inverse[...], projected)
    store_square(side_out, 0, load_square(terms, SIDE) - dot_t_full(x[...], projected))
    right = jnp.concatenate([tall(x[...]), tall(y)], axis=1)

    def value(at):
        change = dot(wide(b2[at, :]), right)
        panel = b1[at, :] - change[:, :R]
        level[at, :] = sources[at, :] - change[:, R:]
        high[at, :], low[at, :] = split2(panel)
        return panel

    by_tiles(b2.shape[0], out, stage, sems, value)


def field_kernel(level, high, low, inverse, side, out, stage, sems):
    weights = tall(dot(wide(inverse[...]), tall(load_square(side, 0))))

    def value(at):
        left = jnp.concatenate([high[at, :], high[at, :], low[at, :]], axis=1)
        return level[at, :] - dot(left, weights)

    by_tiles(level.shape[0], out, stage, sems, value)


def update(kernel, args, passes, name, more=()):
    rows = args[0].shape[0]
    return pl.pallas_call(
        kernel,
        out_specs=[pl.BlockSpec(memory_space=pl.ANY)] + [pl.BlockSpec(memory_space=pltpu.VMEM)] * len(more),
        out_shape=[jax.ShapeDtypeStruct((rows, R), F32), *more],
        scratch_shapes=[pltpu.VMEM((rows, R), F32), pltpu.SemaphoreType.DMA((rows // TILE,))],
        compiler_params=pltpu.CompilerParams(vmem_limit_bytes=VMEM_LIMIT),
        cost_estimate=cost(passes, rows, 3),
        name=name,
    )(*args)


def exchange(x, mask):
    count = lax.axis_size(AXES)
    return lax.ppermute(x, AXES, [(i, i ^ mask) for i in range(count)])


def choose(x, upper):
    half = half_of(x.shape[0])
    low, high = x[:half], x[x.shape[0] - half :]
    return jnp.where(upper, high, low), jnp.where(upper, low, high)


def join(x, other, rows, upper):
    low, high = jnp.where(upper, other, x), jnp.where(upper, x, other)
    return jnp.concatenate([low[: rows - x.shape[0]], high], axis=0)


def summing_stages(bits):
    down = [("scatter", bit) for bit in bits[:-1]]
    return down + [("sum", bits[-1])] + [("gather", bit) for bit in reversed(bits[:-1])]


class Chain:
    def __init__(self, value, upper):
        self.value, self.upper, self.sizes = value, upper, {}

    def start(self, kind, bit):
        self.kind, self.bit = kind, bit
        sent = self.value
        if kind == "scatter":
            self.sizes[bit] = self.value.shape[0]
            self.value, sent = choose(self.value, self.upper[bit])
        self.flying = exchange(sent, 1 << bit)

    def finish(self):
        if self.kind == "gather":
            self.value = join(self.value, self.flying, self.sizes[self.bit], self.upper[self.bit])
        else:
            self.value = self.value + self.flying


def per_device(q_two, q_one, sources, coupling_two, coupling_one):
    index = lax.axis_index(AXES)
    places = lax.axis_size(AXES).bit_length() - 1
    flags = [(index >> bit) & 1 == 1 for bit in range(places)]
    q_two, *upper = lax.optimization_barrier((q_two, *flags))
    stages = summing_stages(list(range(2, places)))

    keep, send, b2, b1 = panel_gram(q_two, q_one)
    arriving = exchange(send, 1)
    source_keep, source_send = source_gram(b2, b1, sources)
    arriving, source_send = lax.optimization_barrier((arriving, source_send))

    panels = Chain(keep + arriving, upper)
    source = Chain(source_keep, upper)
    panels.sizes[0], source.sizes[0] = PANEL_TERMS, SOURCE_TERMS
    source_left = [("gather", 0)] + stages[::-1]
    for step, stage in enumerate(stages):
        panels.start(*stage)
        if step == 0:
            source.kind, source.bit, source.flying = "sum", 0, exchange(source_send, 1)
        else:
            source.start(*source_left.pop())
        panels.flying, source.flying = lax.optimization_barrier((panels.flying, source.flying))
        panels.finish()
        source.finish()
    panels.start("gather", 0)
    source.start(*source_left.pop())
    panels.finish()
    terms = panels.value
    parts = invert_first(half_index, terms, coupling_two, "level_first")
    parts = invert_middle(parts, "level_middle")
    source.flying, parts = lax.optimization_barrier((source.flying, parts))
    source.finish()
    source.start(*source_left.pop())
    inverse = invert_second(parts, "level_second")
    x, root = call(
        panel_solve_kernel, (SQUARE, jax.ShapeDtypeStruct((SYMMETRIC, LANES), F32)), (inverse, terms), "panel_solve"
    )
    source.flying, x = lax.optimization_barrier((source.flying, x))
    source.finish()
    arriving = exchange(root, 2)
    rows = b2.shape[0]
    shapes = [jax.ShapeDtypeStruct((rows, R), kind) for kind in (F32, BF16, BF16)]
    shapes.append(jax.ShapeDtypeStruct((FULL, LANES), F32))
    args = [b2, b1, sources, x, inverse, source.value]
    panel_one, level, high, low, side = update(panel_kernel, args, 8, "panel", shapes)
    side = Chain(choose(side, upper[0])[0], upper)
    side.sizes[0] = FULL
    side_flying = exchange(side.value, 2)
    arriving, side.value = lax.optimization_barrier((arriving, side.value))
    root = root + arriving
    parts = invert_first(no_index, root, coupling_one[None], "root_first")
    parts = invert_middle(parts, "root_middle")
    side_flying, parts = lax.optimization_barrier((side_flying, parts))
    side.value = side.value + side_flying
    side.start("gather", 0)
    inverse = invert_second(parts, "root_second")
    side.finish()
    (solution,) = update(field_kernel, [level, high, low, inverse, side.value], 3, "field")
    return (panel_one, solution)


def solution(mesh):
    placed = P(("group", "leaf"), None)
    return jax.shard_map(
        per_device,
        mesh=mesh,
        in_specs=(placed, placed, placed, P(), P()),
        out_specs=(placed, placed),
        check_vma=False,
    )
```

```python
import functools

import jax
import jax.numpy as jnp
from jax import lax
from jax.experimental import pallas as pl
from jax.experimental.pallas import tpu as pltpu
from jax.sharding import PartitionSpec as P

HIGH = lax.Precision.HIGHEST
AXES = ("leaf", "group")
F32 = jnp.float32
BF16 = jnp.bfloat16
R = 256
LANES = 128
TILE = 512
GROUPS = 8
VMEM_LIMIT = 16 * 1024 * 1024
SYMMETRIC, FULL = 264, 512
OWN, ROOT, CROSS, PANEL_TERMS = 0, 264, 528, 1040
PROJECTED, SIDE, SOURCE_TERMS = 0, 512, 1024


def split2(x):
    high = x.astype(BF16)
    return high, (x - high.astype(F32)).astype(BF16)


def split3(x):
    high = x.astype(BF16)
    rest = x - high.astype(F32)
    mid = rest.astype(BF16)
    return high, mid, (rest - mid.astype(F32)).astype(BF16)


def dot(left, right):
    return jnp.dot(left, right, preferred_element_type=F32)


def dot_t(left, right):
    return lax.dot_general(left, right, (((0,), (0,)), ((), ())), preferred_element_type=F32)


def dot_full(left, right):
    return jnp.dot(left, right, precision=HIGH, preferred_element_type=F32)


def dot_t_full(left, right):
    return lax.dot_general(
        left, right, (((0,), (0,)), ((), ())), precision=HIGH, preferred_element_type=F32
    )


def square_index():
    row = lax.broadcasted_iota(jnp.int32, (LANES, LANES), 0)
    return row, lax.broadcasted_iota(jnp.int32, (LANES, LANES), 1)


def store_symmetric(ref, at, block):
    row, col = square_index()
    last = block[128:, 128:]
    ref[at : at + 128, :] = block[128:, :128]
    ref[at + 128 : at + 256, :] = jnp.where(row >= col, block[:128, :128], last)
    diagonal = jnp.sum(jnp.where(row == col, last, 0.0), axis=0, keepdims=True)
    ref[at + 256 : at + 264, :] = jnp.broadcast_to(diagonal, (8, LANES))


def store_square(ref, row, block):
    ref[row : row + 256, :] = block[:, :128]
    ref[row + 256 : row + 512, :] = block[:, 128:]


def load_symmetric(ref, at):
    row, col = square_index()
    lower = ref[at : at + 128, :]
    mixed = ref[at + 128 : at + 256, :]
    turned = mixed.T
    first = jnp.where(row >= col, mixed, turned)
    last = jnp.where(row < col, mixed, turned)
    last = jnp.where(row == col, ref[at + 256 : at + 257, :], last)
    top = jnp.concatenate([first, lower.T], axis=1)
    return jnp.concatenate([top, jnp.concatenate([lower, last], axis=1)], axis=0)


def load_square(ref, row):
    return jnp.concatenate([ref[row : row + 256, :], ref[row + 256 : row + 512, :]], axis=1)


def half_of(rows):
    return (rows + 15) // 16 * 8


def store_halves(packed, keep, send):
    half = half_of(packed.shape[0])
    far = packed.shape[0] - half
    mine = lax.rem(lax.axis_index("group"), 2)
    keep[...] = packed[pl.ds(pl.multiple_of(mine * far, 8), half), :]
    send[...] = packed[pl.ds(pl.multiple_of((1 - mine) * far, 8), half), :]


def tile_at(tile):
    return pl.ds(pl.multiple_of(tile * TILE, TILE), TILE)


def panel_gram_kernel(q_two, q_one, keep, send, b2, b1, acc, packed, sems):
    tiles = b2.shape[0] // TILE
    pairs = ((q_two, b2), (q_one, b1))

    def copies(at, sem):
        return [
            pltpu.make_async_copy(source.at[at], target.at[at], sems.at[which, sem])
            for which, (source, target) in enumerate(pairs)
        ]

    small = TILE // 2
    parts = (pl.ds(0, small), pl.ds(small, small))
    for sem, at in enumerate(parts):
        for copy in copies(at, sem):
            copy.start()
    for tile in range(1, tiles):
        for copy in copies(tile_at(tile), tile + 1):
            copy.start()
    acc[...] = jnp.zeros_like(acc)

    def add_rows(at, sem):
        for copy in copies(at, sem):
            copy.wait()
        h2, l2 = split2(b2[at, :])
        h1, l1 = split2(b1[at, :])
        h2t, l2t, h1t = h2.T, l2.T, h1.T
        acc[0] += dot(h2t, h2)
        acc[1] += dot(h2t, l2)
        left = jnp.concatenate([h2t, h2t, l2t], axis=1)
        acc[2] += dot(left, jnp.concatenate([h1, l1, h1], axis=0))
        acc[3] += dot(h1t, h1)
        acc[4] += dot(h1t, l1)

    def step(tile, carry):
        add_rows(tile_at(tile), tile + 1)
        return carry

    for sem, at in enumerate(parts):
        add_rows(at, sem)
    lax.fori_loop(1, tiles, step, 0)
    low = acc[1]
    store_symmetric(packed, OWN, acc[0] + low + low.T)
    low = acc[4]
    store_symmetric(packed, ROOT, acc[3] + low + low.T)
    store_square(packed, CROSS, acc[2])
    store_halves(packed, keep, send)


def source_gram_kernel(b2, b1, sources, packed, acc):
    acc[...] = jnp.zeros_like(acc)

    def step(tile, carry):
        hs, ls = split2(sources[tile_at(tile), :])
        right = jnp.concatenate([hs, ls, hs], axis=0)
        for which, panel in enumerate((b2, b1)):
            high, low = split2(panel[tile_at(tile), :])
            turned = high.T
            acc[which] += dot(jnp.concatenate([turned, turned, low.T], axis=1), right)
        return carry

    lax.fori_loop(0, b2.shape[0] // TILE, step, 0)
    store_square(packed, PROJECTED, acc[0])
    store_square(packed, SIDE, acc[1])


def cost(passes, rows, arrays):
    return pl.CostEstimate(
        flops=2 * passes * rows * R * R, bytes_accessed=4 * arrays * rows * R, transcendentals=0
    )


def panel_gram(q_two, q_one):
    rows = q_two.shape[0]
    part = jax.ShapeDtypeStruct((half_of(PANEL_TERMS), LANES), F32)
    tall = jax.ShapeDtypeStruct((rows, R), F32)
    return pl.pallas_call(
        panel_gram_kernel,
        in_specs=[pl.BlockSpec(memory_space=pl.ANY)] * 2,
        out_shape=(part, part, tall, tall),
        scratch_shapes=[
            pltpu.VMEM((5, R, R), F32),
            pltpu.VMEM((PANEL_TERMS, LANES), F32),
            pltpu.SemaphoreType.DMA((2, rows // TILE + 1)),
        ],
        compiler_params=pltpu.CompilerParams(vmem_limit_bytes=VMEM_LIMIT),
        cost_estimate=cost(7, rows, 2),
        name="panel_gram",
    )(pltpu.with_memory_space_constraint(q_two, pltpu.HBM), pltpu.with_memory_space_constraint(q_one, pltpu.HBM))


def source_gram(b2, b1, sources):
    return pl.pallas_call(
        source_gram_kernel,
        out_shape=jax.ShapeDtypeStruct((SOURCE_TERMS, LANES), F32),
        scratch_shapes=[pltpu.VMEM((2, R, R), F32)],
        compiler_params=pltpu.CompilerParams(vmem_limit_bytes=VMEM_LIMIT),
        cost_estimate=cost(6, b2.shape[0], 3),
        name="source_gram",
    )(b2, b1, sources)


def spread_lane(x, lane):
    return jnp.broadcast_to(x[:, lane : lane + 1], (8, LANES))


def sweep_panel(block, start, cols, rows):
    lane = lax.broadcasted_iota(jnp.int32, (8, LANES), 1)
    panel = block[start : start + GROUPS]
    left = stack_left(jnp.concatenate(panel, axis=0))
    for t in range(GROUPS):
        panel = eliminate_group(panel, t, start + t, cols, rows)
    inside = (lane >= 8 * start) & (lane < 8 * (start + GROUPS))
    panel = [jnp.where(inside, -x, x) for x in panel]
    change = dot_t(left, stack_right(jnp.concatenate(panel, axis=0)))
    swept = []
    for g in range(len(block)):
        if start <= g < start + GROUPS:
            swept.append(panel[g - start])
        else:
            swept.append(jnp.where(inside, 0.0, block[g]) - change[8 * g : 8 * g + 8, :])
    return swept


def eliminate_group(panel, t, at, cols, rows):
    lane = lax.broadcasted_iota(jnp.int32, (8, LANES), 1)
    sub = lax.broadcasted_iota(jnp.int32, (8, LANES), 0)
    for j in range(8):
        cols[64 * at + 8 * j : 64 * at + 8 * j + 8, :] = spread_lane(panel[t], 8 * at + j)
    rows[8 * at : 8 * at + 8, :] = panel[t]
    entry = {}
    for i in range(8):
        for j in range(i + 1):
            row = 64 * at + 8 * j + i
            entry[i, j] = jnp.broadcast_to(cols[row : row + 1, :], (8, LANES))
    inside = (lane >= 8 * at) & (lane < 8 * at + 8)
    line = []
    for j in range(8):
        row = jnp.broadcast_to(rows[8 * at + j : 8 * at + j + 1, :], (8, LANES))
        line.append(jnp.where(inside, jnp.where(lane == 8 * at + j, 1.0, 0.0), row))
    after = None
    if t < GROUPS - 1:
        columns = [spread_lane(panel[t + 1], 8 * at + j) for j in range(8)]
        after = [columns, jnp.where(inside, 0.0, panel[t + 1])]
    line, after = solve_small(entry, line, after)
    for g in range(GROUPS):
        if g == t + 1:
            panel[g] = after
        elif g != t:
            terms = [spread_lane(panel[g], 8 * at + j) * line[j] for j in range(8)]
            panel[g] = jnp.where(inside, 0.0, panel[g]) - tree_sum(terms)
    merged = line[0]
    for j in range(1, 8):
        merged = jnp.where(sub == j, line[j], merged)
    panel[t] = merged
    return panel


def tree_sum(terms):
    while len(terms) > 1:
        terms = [
            terms[i] + terms[i + 1] if i + 1 < len(terms) else terms[i]
            for i in range(0, len(terms), 2)
        ]
    return terms[0]


def solve_small(entry, line, after):
    columns, block = after or (None, None)
    factors, scaled = {}, {}
    for k in range(0, 8, 2):
        a, b, c = entry[k, k], entry[k + 1, k], entry[k + 1, k + 1]
        inv = pl.reciprocal(a * c - b * b, approx=True)
        below = range(k + 2, 8)
        first = {i: c * entry[i, k] - b * entry[i, k + 1] for i in below}
        second = {i: a * entry[i, k + 1] - b * entry[i, k] for i in below}
        for i in below:
            for j in range(k + 2, i + 1):
                entry[i, j] = entry[i, j] - inv * (first[i] * entry[j, k] + second[i] * entry[j, k + 1])
        top = c * line[k] - b * line[k + 1]
        bottom = a * line[k + 1] - b * line[k]
        if columns is not None:
            block = block - inv * (columns[k] * top + columns[k + 1] * bottom)
        scaled[k], scaled[k + 1] = inv * top, inv * bottom
        for i in below:
            m, n = inv * first[i], inv * second[i]
            factors[i, k] = m, n
            line[i] = line[i] - (m * line[k] + n * line[k + 1])
            if columns is not None:
                columns[i] = columns[i] - (m * columns[k] + n * columns[k + 1])
    for k in range(6, -1, -2):
        x, y = scaled[k], scaled[k + 1]
        if k < 6:
            x = x - tree_sum([factors[i, k][0] * line[i] for i in range(k + 2, 8)])
            y = y - tree_sum([factors[i, k][1] * line[i] for i in range(k + 2, 8)])
        line[k], line[k + 1] = x, y
    return line, block


def stack_left(x):
    h, m, l = split3(x)
    return jnp.concatenate([h, h, m, h, l, m], axis=0)


def stack_right(x):
    h, m, l = split3(x)
    return jnp.concatenate([h, m, h, l, h, m], axis=0)


def sweep(matrix, panels, cols, rows):
    block = [matrix[8 * i : 8 * i + 8, :] for i in range(LANES // 8)]
    for panel in panels:
        block = sweep_panel(block, panel * GROUPS, cols, rows)
    return jnp.concatenate(block, axis=0)


PANELS = LANES // (8 * GROUPS)


SQUARE = jax.ShapeDtypeStruct((R, R), F32)
CORNER = jax.ShapeDtypeStruct((LANES, LANES), F32)


def call(kernel, out_shape, args, name, scratch=(), flops=0):
    return pl.pallas_call(
        kernel,
        out_shape=out_shape,
        scratch_shapes=list(scratch),
        compiler_params=pltpu.CompilerParams(vmem_limit_bytes=VMEM_LIMIT),
        cost_estimate=pl.CostEstimate(flops=flops, bytes_accessed=R * R * 4, transcendentals=0),
        name=name,
    )(*args)


def first_kernel(which, gram_ref, coupling, first_out, across_out, rest_out, row_out, col_out, cols, rows):
    matrix = coupling[which()] + load_symmetric(gram_ref, OWN)
    eye = lax.broadcasted_iota(jnp.int32, (R, R), 0) == lax.broadcasted_iota(jnp.int32, (R, R), 1)
    diagonal = jnp.where(eye, matrix, 0.0)
    scale_row = lax.rsqrt(jnp.sum(diagonal, axis=0, keepdims=True))
    scale_col = lax.rsqrt(jnp.sum(diagonal, axis=1, keepdims=True))
    matrix = matrix * scale_col * scale_row
    side = matrix[:LANES, LANES:]
    first = -sweep(matrix[:LANES, :LANES], range(PANELS), cols, rows)
    across = dot_full(first, side)
    first_out[...] = first
    across_out[...] = across
    rest_out[...] = matrix[LANES:, LANES:] - dot_t_full(side, across)
    row_out[...] = jnp.broadcast_to(scale_row, (8, R))
    col_out[...] = jnp.broadcast_to(scale_col, (R, LANES))


def middle_kernel(rest, out, cols, rows):
    out[...] = sweep(rest[...], range(PANELS - 1), cols, rows)


def second_kernel(first, across, swept, row, col, out, cols, rows):
    second = -sweep(swept[...], range(PANELS - 1, PANELS), cols, rows)
    corner = -dot_full(across[...], second)
    top = first[...] - dot_full(corner, across[...].T)
    out[:LANES, :LANES] = top * col[:LANES, :] * row[:1, :LANES]
    out[:LANES, LANES:] = corner * col[:LANES, :] * row[:1, LANES:]
    out[LANES:, :LANES] = corner.T * col[LANES:, :] * row[:1, :LANES]
    out[LANES:, LANES:] = second * col[LANES:, :] * row[:1, LANES:]


SCRATCH = [pltpu.VMEM((1024, LANES), F32), pltpu.VMEM((LANES, LANES), F32)]
HALF_FLOPS = 5_000_000_000


def invert_first(which, packed, coupling, name):
    shapes = (
        CORNER,
        CORNER,
        CORNER,
        jax.ShapeDtypeStruct((8, R), F32),
        jax.ShapeDtypeStruct((R, LANES), F32),
    )
    kernel = functools.partial(first_kernel, which)
    return call(kernel, shapes, (packed, coupling), name, SCRATCH, HALF_FLOPS)


def invert_middle(parts, name):
    first, across, rest, row, col = parts
    rest = call(middle_kernel, CORNER, (rest,), name, SCRATCH, HALF_FLOPS // 2)
    return first, across, rest, row, col


def invert_second(parts, name):
    return call(second_kernel, SQUARE, parts, name, SCRATCH, HALF_FLOPS // 2)


def half_index():
    return lax.axis_index("group") // 2


def no_index():
    return 0


def panel_solve_kernel(inverse, terms, x_out, root_out):
    cross = load_square(terms, CROSS)
    x = dot_full(inverse[...], cross)
    x_out[...] = x
    store_symmetric(root_out, 0, load_symmetric(terms, ROOT) - dot_t_full(cross, x))


def wide(x):
    high, low = split2(x)
    return jnp.concatenate([high, high, low], axis=1)


def tall(x):
    high, low = split2(x)
    return jnp.concatenate([high, low, high], axis=0)


def by_tiles(rows, out, stage, sems, value, beside=None):
    tiles = rows // TILE

    def copy(tile):
        return pltpu.make_async_copy(stage.at[tile_at(tile)], out.at[tile_at(tile)], sems.at[tile])

    def step(tile, carry):
        stage[tile_at(tile), :] = value(tile_at(tile))
        copy(tile).start()
        return carry

    lax.fori_loop(0, tiles, step, 0)
    if beside is not None:
        beside()
    for tile in range(tiles):
        copy(tile).wait()


def panel_kernel(b2, b1, sources, x, inverse, terms, out, level, high, low, side_out, stage, sems):
    projected = load_square(terms, PROJECTED)
    y = dot_full(inverse[...], projected)
    store_square(side_out, 0, load_square(terms, SIDE) - dot_t_full(x[...], projected))
    right = jnp.concatenate([tall(x[...]), tall(y)], axis=1)

    def value(at):
        change = dot(wide(b2[at, :]), right)
        panel = b1[at, :] - change[:, :R]
        level[at, :] = sources[at, :] - change[:, R:]
        high[at, :], low[at, :] = split2(panel)
        return panel

    by_tiles(b2.shape[0], out, stage, sems, value)


def field_kernel(level, high, low, inverse, side, out, stage, sems):
    weights = tall(dot(wide(inverse[...]), tall(load_square(side, 0))))

    def value(at):
        left = jnp.concatenate([high[at, :], high[at, :], low[at, :]], axis=1)
        return level[at, :] - dot(left, weights)

    by_tiles(level.shape[0], out, stage, sems, value)


def update(kernel, args, passes, name, more=()):
    rows = args[0].shape[0]
    return pl.pallas_call(
        kernel,
        out_specs=[pl.BlockSpec(memory_space=pl.ANY)] + [pl.BlockSpec(memory_space=pltpu.VMEM)] * len(more),
        out_shape=[jax.ShapeDtypeStruct((rows, R), F32), *more],
        scratch_shapes=[pltpu.VMEM((rows, R), F32), pltpu.SemaphoreType.DMA((rows // TILE,))],
        compiler_params=pltpu.CompilerParams(vmem_limit_bytes=VMEM_LIMIT),
        cost_estimate=cost(passes, rows, 3),
        name=name,
    )(*args)


def exchange(x, mask, senders=(0, 1)):
    count = lax.axis_size(AXES)
    return lax.ppermute(x, AXES, [(i, i ^ mask) for i in range(count) if i & 1 in senders])


def choose(x, upper):
    half = half_of(x.shape[0])
    low, high = x[:half], x[x.shape[0] - half :]
    return jnp.where(upper, high, low), jnp.where(upper, low, high)


def join(x, other, rows, upper):
    low, high = jnp.where(upper, other, x), jnp.where(upper, x, other)
    return jnp.concatenate([low[: rows - x.shape[0]], high], axis=0)


def summing_stages(bits):
    down = [("scatter", bit) for bit in bits[:-1]]
    return down + [("sum", bits[-1])] + [("gather", bit) for bit in reversed(bits[:-1])]


class Chain:
    def __init__(self, value, upper, senders=(0, 1)):
        self.value, self.upper, self.senders, self.sizes = value, upper, senders, {}

    def start(self, kind, bit):
        self.kind, self.bit = kind, bit
        sent = self.value
        if kind == "scatter":
            self.sizes[bit] = self.value.shape[0]
            self.value, sent = choose(self.value, self.upper[bit])
        self.flying = exchange(sent, 1 << bit, self.senders)

    def finish(self):
        if self.kind == "gather":
            self.value = join(self.value, self.flying, self.sizes[self.bit], self.upper[self.bit])
        else:
            self.value = self.value + self.flying


def per_device(q_two, q_one, sources, coupling_two, coupling_one):
    index = lax.axis_index(AXES)
    places = lax.axis_size(AXES).bit_length() - 1
    flags = [(index >> bit) & 1 == 1 for bit in range(places)]
    q_two, *upper = lax.optimization_barrier((q_two, *flags))
    stages = summing_stages(list(range(2, places)))

    keep, send, b2, b1 = panel_gram(q_two, q_one)
    arriving = exchange(send, 1)
    source_terms = source_gram(b2, b1, sources)
    arriving, source_terms = lax.optimization_barrier((arriving, source_terms))

    panels = Chain(keep + arriving, upper)
    source = Chain(source_terms, upper, (1,))
    panels.sizes[0] = PANEL_TERMS
    source_left = stages[::-1]
    for step, stage in enumerate(stages):
        panels.start(*stage)
        if step == 0:
            source.kind, source.bit, source.flying = "sum", 0, exchange(source_terms, 1, (0,))
        else:
            source.start(*source_left.pop())
        panels.flying, source.flying = lax.optimization_barrier((panels.flying, source.flying))
        panels.finish()
        source.finish()
    panels.start("gather", 0)
    source.start(*source_left.pop())
    panels.finish()
    terms = panels.value
    parts = invert_first(half_index, terms, coupling_two, "level_first")
    parts = invert_middle(parts, "level_middle")
    source.flying, parts = lax.optimization_barrier((source.flying, parts))
    source.finish()
    source_arriving = exchange(source.value, 1, (1,))
    inverse = invert_second(parts, "level_second")
    x, root = call(
        panel_solve_kernel, (SQUARE, jax.ShapeDtypeStruct((SYMMETRIC, LANES), F32)), (inverse, terms), "panel_solve"
    )
    source_arriving, x = lax.optimization_barrier((source_arriving, x))
    source_sums = jnp.where(upper[0], source.value, source_arriving)
    arriving = exchange(root, 2)
    rows = b2.shape[0]
    shapes = [jax.ShapeDtypeStruct((rows, R), kind) for kind in (F32, BF16, BF16)]
    shapes.append(jax.ShapeDtypeStruct((FULL, LANES), F32))
    args = [b2, b1, sources, x, inverse, source_sums]
    panel_one, level, high, low, side = update(panel_kernel, args, 8, "panel", shapes)
    side = Chain(choose(side, upper[0])[0], upper)
    side.sizes[0] = FULL
    side_flying = exchange(side.value, 2)
    arriving, side.value = lax.optimization_barrier((arriving, side.value))
    root = root + arriving
    parts = invert_first(no_index, root, coupling_one[None], "root_first")
    parts = invert_middle(parts, "root_middle")
    side_flying, parts = lax.optimization_barrier((side_flying, parts))
    side.value = side.value + side_flying
    side.start("gather", 0)
    inverse = invert_second(parts, "root_second")
    side.finish()
    (solution,) = update(field_kernel, [level, high, low, inverse, side.value], 3, "field")
    return (panel_one, solution)


def solution(mesh):
    placed = P(("group", "leaf"), None)
    return jax.shard_map(
        per_device,
        mesh=mesh,
        in_specs=(placed, placed, placed, P(), P()),
        out_specs=(placed, placed),
        check_vma=False,
    )
```

```python
import functools

import jax
import jax.numpy as jnp
from jax import lax
from jax.experimental import pallas as pl
from jax.experimental.pallas import tpu as pltpu
from jax.sharding import PartitionSpec as P

HIGH = lax.Precision.HIGHEST
AXES = ("leaf", "group")
F32 = jnp.float32
BF16 = jnp.bfloat16
R = 256
LANES = 128
TILE = 512
OUT_TILE = 256
VMEM_LIMIT = 16 * 1024 * 1024
SYMMETRIC, FULL = 264, 512
OWN, ROOT, CROSS, PANEL_TERMS = 0, 264, 528, 1040
PROJECTED, SIDE, SOURCE_TERMS = 0, 512, 1024


def split2(x):
    high = x.astype(BF16)
    return high, (x - high.astype(F32)).astype(BF16)


def split3(x):
    high = x.astype(BF16)
    rest = x - high.astype(F32)
    mid = rest.astype(BF16)
    return high, mid, (rest - mid.astype(F32)).astype(BF16)


def dot(left, right):
    return jnp.dot(left, right, preferred_element_type=F32)


def dot_t(left, right):
    return lax.dot_general(left, right, (((0,), (0,)), ((), ())), preferred_element_type=F32)


def dot_full(left, right):
    return jnp.dot(left, right, precision=HIGH, preferred_element_type=F32)


def dot_t_full(left, right):
    return lax.dot_general(
        left, right, (((0,), (0,)), ((), ())), precision=HIGH, preferred_element_type=F32
    )


def square_index():
    row = lax.broadcasted_iota(jnp.int32, (LANES, LANES), 0)
    return row, lax.broadcasted_iota(jnp.int32, (LANES, LANES), 1)


def store_symmetric(ref, at, block):
    row, col = square_index()
    last = block[128:, 128:]
    ref[at : at + 128, :] = block[128:, :128]
    ref[at + 128 : at + 256, :] = jnp.where(row >= col, block[:128, :128], last)
    diagonal = jnp.sum(jnp.where(row == col, last, 0.0), axis=0, keepdims=True)
    ref[at + 256 : at + 264, :] = jnp.broadcast_to(diagonal, (8, LANES))


def store_square(ref, row, block):
    ref[row : row + 256, :] = block[:, :128]
    ref[row + 256 : row + 512, :] = block[:, 128:]


def load_symmetric(ref, at):
    row, col = square_index()
    lower = ref[at : at + 128, :]
    mixed = ref[at + 128 : at + 256, :]
    turned = mixed.T
    first = jnp.where(row >= col, mixed, turned)
    last = jnp.where(row < col, mixed, turned)
    last = jnp.where(row == col, ref[at + 256 : at + 257, :], last)
    top = jnp.concatenate([first, lower.T], axis=1)
    return jnp.concatenate([top, jnp.concatenate([lower, last], axis=1)], axis=0)


def load_square(ref, row):
    return jnp.concatenate([ref[row : row + 256, :], ref[row + 256 : row + 512, :]], axis=1)


def half_of(rows):
    return (rows + 15) // 16 * 8


def store_halves(packed, keep, send):
    half = half_of(packed.shape[0])
    far = packed.shape[0] - half
    mine = lax.rem(lax.axis_index("group"), 2)
    keep[...] = packed[pl.ds(pl.multiple_of(mine * far, 8), half), :]
    send[...] = packed[pl.ds(pl.multiple_of((1 - mine) * far, 8), half), :]


def tile_at(tile):
    return pl.ds(pl.multiple_of(tile * TILE, TILE), TILE)


def panel_gram_kernel(q_two, q_one, keep, send, b2, b1, acc, packed, sems):
    tiles = b2.shape[0] // TILE
    pairs = ((q_two, b2), (q_one, b1))

    def copies(at, sem):
        return [
            pltpu.make_async_copy(source.at[at], target.at[at], sems.at[which, sem])
            for which, (source, target) in enumerate(pairs)
        ]

    small = TILE // 2
    parts = (pl.ds(0, small), pl.ds(small, small))
    for sem, at in enumerate(parts):
        for copy in copies(at, sem):
            copy.start()
    for tile in range(1, tiles):
        for copy in copies(tile_at(tile), tile + 1):
            copy.start()
    acc[...] = jnp.zeros_like(acc)

    def add_rows(at, sem):
        for copy in copies(at, sem):
            copy.wait()
        h2, l2 = split2(b2[at, :])
        h1, l1 = split2(b1[at, :])
        h2t, h1t = h2.T, h1.T
        acc[0] += dot(h2t, h2)
        acc[1] += dot(h2t, l2)
        acc[2] += dot(jnp.concatenate([h2t, h2t], axis=1), jnp.concatenate([h1, l1], axis=0))
        acc[5] += dot(h1t, l2)
        acc[3] += dot(h1t, h1)
        acc[4] += dot(h1t, l1)

    def step(tile, carry):
        add_rows(tile_at(tile), tile + 1)
        return carry

    for sem, at in enumerate(parts):
        add_rows(at, sem)
    lax.fori_loop(1, tiles, step, 0)
    low = acc[1]
    store_symmetric(packed, OWN, acc[0] + low + low.T)
    low = acc[4]
    store_symmetric(packed, ROOT, acc[3] + low + low.T)
    store_square(packed, CROSS, acc[2] + acc[5].T)
    store_halves(packed, keep, send)


def source_gram_kernel(b2, b1, sources, keep, send, acc, packed):
    acc[...] = jnp.zeros_like(acc)

    def step(tile, carry):
        hs, ls = split2(sources[tile_at(tile), :])
        right = jnp.concatenate([hs, ls, hs], axis=0)
        for which, panel in enumerate((b2, b1)):
            high, low = split2(panel[tile_at(tile), :])
            turned = high.T
            acc[which] += dot(jnp.concatenate([turned, turned, low.T], axis=1), right)
        return carry

    lax.fori_loop(0, b2.shape[0] // TILE, step, 0)
    store_square(packed, PROJECTED, acc[0])
    store_square(packed, SIDE, acc[1])
    store_halves(packed, keep, send)


def cost(passes, rows, arrays):
    return pl.CostEstimate(
        flops=2 * passes * rows * R * R, bytes_accessed=4 * arrays * rows * R, transcendentals=0
    )


def panel_gram(q_two, q_one):
    rows = q_two.shape[0]
    part = jax.ShapeDtypeStruct((half_of(PANEL_TERMS), LANES), F32)
    tall = jax.ShapeDtypeStruct((rows, R), F32)
    return pl.pallas_call(
        panel_gram_kernel,
        in_specs=[pl.BlockSpec(memory_space=pl.ANY)] * 2,
        out_shape=(part, part, tall, tall),
        scratch_shapes=[
            pltpu.VMEM((6, R, R), F32),
            pltpu.VMEM((PANEL_TERMS, LANES), F32),
            pltpu.SemaphoreType.DMA((2, rows // TILE + 1)),
        ],
        compiler_params=pltpu.CompilerParams(vmem_limit_bytes=VMEM_LIMIT),
        cost_estimate=cost(7, rows, 2),
        name="panel_gram",
    )(pltpu.with_memory_space_constraint(q_two, pltpu.HBM), pltpu.with_memory_space_constraint(q_one, pltpu.HBM))


def source_gram(b2, b1, sources):
    part = jax.ShapeDtypeStruct((half_of(SOURCE_TERMS), LANES), F32)
    return pl.pallas_call(
        source_gram_kernel,
        out_shape=(part, part),
        scratch_shapes=[pltpu.VMEM((2, R, R), F32), pltpu.VMEM((SOURCE_TERMS, LANES), F32)],
        compiler_params=pltpu.CompilerParams(vmem_limit_bytes=VMEM_LIMIT),
        cost_estimate=cost(6, b2.shape[0], 3),
        name="source_gram",
    )(b2, b1, sources)


def spread_lane(x, lane):
    return jnp.broadcast_to(x[:, lane : lane + 1], (8, LANES))


def eliminate_group(panel, t, cols, rows):
    at, count = t, len(panel)
    lane = lax.broadcasted_iota(jnp.int32, (8, LANES), 1)
    sub = lax.broadcasted_iota(jnp.int32, (8, LANES), 0)
    for j in range(8):
        cols[64 * at + 8 * j : 64 * at + 8 * j + 8, :] = spread_lane(panel[t], 8 * at + j)
    rows[8 * at : 8 * at + 8, :] = panel[t]
    entry = {}
    for i in range(8):
        for j in range(i + 1):
            row = 64 * at + 8 * j + i
            entry[i, j] = jnp.broadcast_to(cols[row : row + 1, :], (8, LANES))
    inside = (lane >= 8 * at) & (lane < 8 * at + 8)
    line = []
    for j in range(8):
        row = jnp.broadcast_to(rows[8 * at + j : 8 * at + j + 1, :], (8, LANES))
        line.append(jnp.where(inside, jnp.where(lane == 8 * at + j, 1.0, 0.0), row))
    after = None
    if t < count - 1:
        columns = [spread_lane(panel[t + 1], 8 * at + j) for j in range(8)]
        after = [columns, jnp.where(inside, 0.0, panel[t + 1])]
    line, after = solve_small(entry, line, after)
    for g in range(count):
        if g == t + 1:
            panel[g] = after
        elif g != t:
            terms = [spread_lane(panel[g], 8 * at + j) * line[j] for j in range(8)]
            panel[g] = jnp.where(inside, 0.0, panel[g]) - tree_sum(terms)
    merged = line[0]
    for j in range(1, 8):
        merged = jnp.where(sub == j, line[j], merged)
    panel[t] = merged
    return panel


def tree_sum(terms):
    while len(terms) > 1:
        terms = [
            terms[i] + terms[i + 1] if i + 1 < len(terms) else terms[i]
            for i in range(0, len(terms), 2)
        ]
    return terms[0]


def solve_small(entry, line, after):
    columns, block = after or (None, None)
    factors, scaled = {}, {}
    for k in range(0, 8, 2):
        a, b, c = entry[k, k], entry[k + 1, k], entry[k + 1, k + 1]
        inv = pl.reciprocal(a * c - b * b, approx=True)
        below = range(k + 2, 8)
        first = {i: c * entry[i, k] - b * entry[i, k + 1] for i in below}
        second = {i: a * entry[i, k + 1] - b * entry[i, k] for i in below}
        for i in below:
            for j in range(k + 2, i + 1):
                entry[i, j] = entry[i, j] - inv * (first[i] * entry[j, k] + second[i] * entry[j, k + 1])
        top = c * line[k] - b * line[k + 1]
        bottom = a * line[k + 1] - b * line[k]
        if columns is not None:
            block = block - inv * (columns[k] * top + columns[k + 1] * bottom)
        scaled[k], scaled[k + 1] = inv * top, inv * bottom
        for i in below:
            m, n = inv * first[i], inv * second[i]
            factors[i, k] = m, n
            line[i] = line[i] - (m * line[k] + n * line[k + 1])
            if columns is not None:
                columns[i] = columns[i] - (m * columns[k] + n * columns[k + 1])
    for k in range(6, -1, -2):
        x, y = scaled[k], scaled[k + 1]
        if k < 6:
            x = x - tree_sum([factors[i, k][0] * line[i] for i in range(k + 2, 8)])
            y = y - tree_sum([factors[i, k][1] * line[i] for i in range(k + 2, 8)])
        line[k], line[k + 1] = x, y
    return line, block


def eliminate(matrix, groups, cols, rows):
    block = [matrix[8 * i : 8 * i + 8, :] for i in range(LANES // 8)]
    for t in groups:
        block = eliminate_group(block, t, cols, rows)
    return jnp.concatenate(block, axis=0)


GROUPS = LANES // 8


SQUARE = jax.ShapeDtypeStruct((R, R), F32)
CORNER = jax.ShapeDtypeStruct((LANES, LANES), F32)


def call(kernel, out_shape, args, name, scratch=(), flops=0):
    return pl.pallas_call(
        kernel,
        out_shape=out_shape,
        scratch_shapes=list(scratch),
        compiler_params=pltpu.CompilerParams(vmem_limit_bytes=VMEM_LIMIT),
        cost_estimate=pl.CostEstimate(flops=flops, bytes_accessed=R * R * 4, transcendentals=0),
        name=name,
    )(*args)


def first_kernel(which, gram_ref, coupling, first_out, across_out, rest_out, row_out, col_out, cols, rows):
    matrix = coupling[which()] + load_symmetric(gram_ref, OWN)
    eye = lax.broadcasted_iota(jnp.int32, (R, R), 0) == lax.broadcasted_iota(jnp.int32, (R, R), 1)
    diagonal = jnp.where(eye, matrix, 0.0)
    scale_row = lax.rsqrt(jnp.sum(diagonal, axis=0, keepdims=True))
    scale_col = lax.rsqrt(jnp.sum(diagonal, axis=1, keepdims=True))
    matrix = matrix * scale_col * scale_row
    side = matrix[:LANES, LANES:]
    first = eliminate(matrix[:LANES, :LANES], range(GROUPS), cols, rows)
    across = dot_full(first, side)
    first_out[...] = first
    across_out[...] = across
    rest_out[...] = matrix[LANES:, LANES:] - dot_t_full(side, across)
    row_out[...] = jnp.broadcast_to(scale_row, (8, R))
    col_out[...] = jnp.broadcast_to(scale_col, (R, LANES))


def middle_kernel(rest, out, cols, rows):
    out[...] = eliminate(rest[...], range(GROUPS // 2), cols, rows)


def finish_inverse(first, across, begun, row, col, cols, rows):
    second = eliminate(begun[...], range(GROUPS // 2, GROUPS), cols, rows)
    corner = -dot_full(across[...], second)
    top = first[...] - dot_full(corner, across[...].T)
    upper = jnp.concatenate([top, corner], axis=1)
    lower = jnp.concatenate([corner.T, second], axis=1)
    scale_col = jnp.concatenate([col[...], col[...]], axis=1)
    return jnp.concatenate([upper, lower], axis=0) * scale_col * row[:1, :]


def root_second_kernel(first, across, begun, row, col, out, cols, rows):
    out[...] = finish_inverse(first, across, begun, row, col, cols, rows)


def level_second_kernel(first, across, begun, row, col, terms, out, x_out, root_out, cols, rows):
    inverse = finish_inverse(first, across, begun, row, col, cols, rows)
    out[...] = inverse
    cross = load_square(terms, CROSS)
    x = dot_full(inverse, cross)
    x_out[...] = x
    store_symmetric(root_out, 0, load_symmetric(terms, ROOT) - dot_t_full(cross, x))


SCRATCH = [pltpu.VMEM((1024, LANES), F32), pltpu.VMEM((LANES, LANES), F32)]
HALF_FLOPS = 5_000_000_000


def invert_first(which, packed, coupling, name):
    shapes = (
        CORNER,
        CORNER,
        CORNER,
        jax.ShapeDtypeStruct((8, R), F32),
        jax.ShapeDtypeStruct((R, LANES), F32),
    )
    kernel = functools.partial(first_kernel, which)
    return call(kernel, shapes, (packed, coupling), name, SCRATCH, HALF_FLOPS)


def invert_middle(parts, name):
    first, across, rest, row, col = parts
    rest = call(middle_kernel, CORNER, (rest,), name, SCRATCH, HALF_FLOPS // 2)
    return first, across, rest, row, col


def half_index():
    return lax.axis_index("group") // 2


def no_index():
    return 0


def wide(x):
    high, low = split2(x)
    return jnp.concatenate([high, high, low], axis=1)


def tall(x):
    high, low = split2(x)
    return jnp.concatenate([high, low, high], axis=0)


def by_tiles(rows, out, stage, sems, value, beside=None):
    tiles = rows // OUT_TILE

    def at(tile):
        return pl.ds(pl.multiple_of(tile * OUT_TILE, OUT_TILE), OUT_TILE)

    def copy(tile):
        return pltpu.make_async_copy(stage.at[at(tile)], out.at[at(tile)], sems.at[tile])

    def step(tile, carry):
        stage[at(tile), :] = value(at(tile))
        copy(tile).start()
        return carry

    lax.fori_loop(0, tiles, step, 0)
    if beside is not None:
        beside()
    for tile in range(tiles):
        copy(tile).wait()


def panel_kernel(b2, b1, sources, x, inverse, terms, out, level, high, low, side_out, stage, sems):
    projected = load_square(terms, PROJECTED)
    y = dot_full(inverse[...], projected)
    store_square(side_out, 0, load_square(terms, SIDE) - dot_t_full(x[...], projected))
    right = jnp.concatenate([tall(x[...]), tall(y)], axis=1)

    def value(at):
        change = dot(wide(b2[at, :]), right)
        panel = b1[at, :] - change[:, :R]
        level[at, :] = sources[at, :] - change[:, R:]
        high[at, :], low[at, :] = split2(panel)
        return panel

    by_tiles(b2.shape[0], out, stage, sems, value)


def field_kernel(level, high, low, inverse, side, out, stage, sems):
    weights = tall(dot(wide(inverse[...]), tall(load_square(side, 0))))

    def value(at):
        left = jnp.concatenate([high[at, :], high[at, :], low[at, :]], axis=1)
        return level[at, :] - dot(left, weights)

    by_tiles(level.shape[0], out, stage, sems, value)


def update(kernel, args, passes, name, more=()):
    rows = args[0].shape[0]
    return pl.pallas_call(
        kernel,
        out_specs=[pl.BlockSpec(memory_space=pl.ANY)] + [pl.BlockSpec(memory_space=pltpu.VMEM)] * len(more),
        out_shape=[jax.ShapeDtypeStruct((rows, R), F32), *more],
        scratch_shapes=[pltpu.VMEM((rows, R), F32), pltpu.SemaphoreType.DMA((rows // OUT_TILE,))],
        compiler_params=pltpu.CompilerParams(vmem_limit_bytes=VMEM_LIMIT),
        cost_estimate=cost(passes, rows, 3),
        name=name,
    )(*args)


def exchange(x, mask):
    count = lax.axis_size(AXES)
    return lax.ppermute(x, AXES, [(i, i ^ mask) for i in range(count)])


def choose(x, upper):
    half = half_of(x.shape[0])
    low, high = x[:half], x[x.shape[0] - half :]
    return jnp.where(upper, high, low), jnp.where(upper, low, high)


def join(x, other, rows, upper):
    low, high = jnp.where(upper, other, x), jnp.where(upper, x, other)
    return jnp.concatenate([low[: rows - x.shape[0]], high], axis=0)


def summing_stages(bits):
    down = [("scatter", bit) for bit in bits[:-1]]
    return down + [("sum", bits[-1])] + [("gather", bit) for bit in reversed(bits[:-1])]


class Chain:
    def __init__(self, value, upper):
        self.value, self.upper, self.sizes = value, upper, {}

    def start(self, kind, bit):
        self.kind, self.bit = kind, bit
        sent = self.value
        if kind == "scatter":
            self.sizes[bit] = self.value.shape[0]
            self.value, sent = choose(self.value, self.upper[bit])
        self.flying = exchange(sent, 1 << bit)

    def finish(self):
        if self.kind == "gather":
            self.value = join(self.value, self.flying, self.sizes[self.bit], self.upper[self.bit])
        else:
            self.value = self.value + self.flying


def per_device(q_two, q_one, sources, coupling_two, coupling_one):
    index = lax.axis_index(AXES)
    places = lax.axis_size(AXES).bit_length() - 1
    flags = [(index >> bit) & 1 == 1 for bit in range(places)]
    q_two, *upper = lax.optimization_barrier((q_two, *flags))
    stages = summing_stages(list(range(2, places)))

    keep, send, b2, b1 = panel_gram(q_two, q_one)
    arriving = exchange(send, 1)
    source_keep, source_send = source_gram(b2, b1, sources)
    arriving, source_send = lax.optimization_barrier((arriving, source_send))

    panels = Chain(keep + arriving, upper)
    source = Chain(source_keep, upper)
    panels.sizes[0], source.sizes[0] = PANEL_TERMS, SOURCE_TERMS
    source_left = [("gather", 0)] + stages[::-1]
    for step, stage in enumerate(stages):
        panels.start(*stage)
        if step == 0:
            source.kind, source.bit, source.flying = "sum", 0, exchange(source_send, 1)
        else:
            source.start(*source_left.pop())
        panels.flying, source.flying = lax.optimization_barrier((panels.flying, source.flying))
        panels.finish()
        source.finish()
    panels.start("gather", 0)
    source.start(*source_left.pop())
    panels.finish()
    terms = panels.value
    parts = invert_first(half_index, terms, coupling_two, "level_first")
    parts = invert_middle(parts, "level_middle")
    source.flying, parts = lax.optimization_barrier((source.flying, parts))
    source.finish()
    source.start(*source_left.pop())
    shapes = (SQUARE, SQUARE, jax.ShapeDtypeStruct((SYMMETRIC, LANES), F32))
    inverse, x, root = call(
        level_second_kernel, shapes, (*parts, terms), "level_second", SCRATCH, HALF_FLOPS // 2
    )
    source.flying, x = lax.optimization_barrier((source.flying, x))
    source.finish()
    arriving = exchange(root, 2)
    rows = b2.shape[0]
    shapes = [jax.ShapeDtypeStruct((rows, R), kind) for kind in (F32, BF16, BF16)]
    shapes.append(jax.ShapeDtypeStruct((FULL, LANES), F32))
    args = [b2, b1, sources, x, inverse, source.value]
    panel_one, level, high, low, side = update(panel_kernel, args, 8, "panel", shapes)
    side = Chain(choose(side, upper[0])[0], upper)
    side.sizes[0] = FULL
    side_flying = exchange(side.value, 2)
    arriving, side.value = lax.optimization_barrier((arriving, side.value))
    root = root + arriving
    parts = invert_first(no_index, root, coupling_one[None], "root_first")
    parts = invert_middle(parts, "root_middle")
    side_flying, parts = lax.optimization_barrier((side_flying, parts))
    side.value = side.value + side_flying
    side.start("gather", 0)
    inverse = call(root_second_kernel, SQUARE, parts, "root_second", SCRATCH, HALF_FLOPS // 2)
    side.finish()
    (solution,) = update(field_kernel, [level, high, low, inverse, side.value], 3, "field")
    return (panel_one, solution)


def solution(mesh):
    placed = P(("group", "leaf"), None)
    return jax.shard_map(
        per_device,
        mesh=mesh,
        in_specs=(placed, placed, placed, P(), P()),
        out_specs=(placed, placed),
        check_vma=False,
    )
```

```python
import functools

import jax
import jax.numpy as jnp
from jax import lax
from jax.experimental import pallas as pl
from jax.experimental.pallas import tpu as pltpu
from jax.sharding import PartitionSpec as P

HIGH = lax.Precision.HIGHEST
AXES = ("leaf", "group")
F32 = jnp.float32
BF16 = jnp.bfloat16
R = 256
LANES = 128
TILE = 512
OUT_TILE = 1024
GROUPS = 8
VMEM_LIMIT = 16 * 1024 * 1024
SYMMETRIC, FULL = 264, 512
OWN, ROOT, CROSS, PANEL_TERMS = 0, 264, 528, 1040
PROJECTED, SIDE, SOURCE_TERMS = 0, 512, 1024


def split2(x):
    high = x.astype(BF16)
    return high, (x - high.astype(F32)).astype(BF16)


def split3(x):
    high = x.astype(BF16)
    rest = x - high.astype(F32)
    mid = rest.astype(BF16)
    return high, mid, (rest - mid.astype(F32)).astype(BF16)


def dot(left, right):
    return jnp.dot(left, right, preferred_element_type=F32)


def dot_t(left, right):
    return lax.dot_general(left, right, (((0,), (0,)), ((), ())), preferred_element_type=F32)


def dot_full(left, right):
    return jnp.dot(left, right, precision=HIGH, preferred_element_type=F32)


def dot_t_full(left, right):
    return lax.dot_general(
        left, right, (((0,), (0,)), ((), ())), precision=HIGH, preferred_element_type=F32
    )


def square_index():
    row = lax.broadcasted_iota(jnp.int32, (LANES, LANES), 0)
    return row, lax.broadcasted_iota(jnp.int32, (LANES, LANES), 1)


def store_symmetric(ref, at, block):
    row, col = square_index()
    last = block[128:, 128:]
    ref[at : at + 128, :] = block[128:, :128]
    ref[at + 128 : at + 256, :] = jnp.where(row >= col, block[:128, :128], last)
    diagonal = jnp.sum(jnp.where(row == col, last, 0.0), axis=0, keepdims=True)
    ref[at + 256 : at + 264, :] = jnp.broadcast_to(diagonal, (8, LANES))


def store_square(ref, row, block):
    ref[row : row + 256, :] = block[:, :128]
    ref[row + 256 : row + 512, :] = block[:, 128:]


def load_symmetric(ref, at):
    row, col = square_index()
    lower = ref[at : at + 128, :]
    mixed = ref[at + 128 : at + 256, :]
    turned = mixed.T
    first = jnp.where(row >= col, mixed, turned)
    last = jnp.where(row < col, mixed, turned)
    last = jnp.where(row == col, ref[at + 256 : at + 257, :], last)
    top = jnp.concatenate([first, lower.T], axis=1)
    return jnp.concatenate([top, jnp.concatenate([lower, last], axis=1)], axis=0)


def load_square(ref, row):
    return jnp.concatenate([ref[row : row + 256, :], ref[row + 256 : row + 512, :]], axis=1)


def half_of(rows):
    return (rows + 15) // 16 * 8


def store_halves(packed, keep, send):
    half = half_of(packed.shape[0])
    far = packed.shape[0] - half
    mine = lax.rem(lax.axis_index("group"), 2)
    keep[...] = packed[pl.ds(pl.multiple_of(mine * far, 8), half), :]
    send[...] = packed[pl.ds(pl.multiple_of((1 - mine) * far, 8), half), :]


def tile_at(tile):
    return pl.ds(pl.multiple_of(tile * TILE, TILE), TILE)


def panel_gram_kernel(q_two, q_one, keep, send, b2, b1, acc, packed, sems):
    tiles = b2.shape[0] // TILE
    pairs = ((q_two, b2), (q_one, b1))

    def copies(at, sem):
        return [
            pltpu.make_async_copy(source.at[at], target.at[at], sems.at[which, sem])
            for which, (source, target) in enumerate(pairs)
        ]

    small = TILE // 2
    parts = (pl.ds(0, small), pl.ds(small, small))
    for sem, at in enumerate(parts):
        for copy in copies(at, sem):
            copy.start()
    for tile in range(1, tiles):
        for copy in copies(tile_at(tile), tile + 1):
            copy.start()
    acc[...] = jnp.zeros_like(acc)

    def add_rows(at, sem):
        for copy in copies(at, sem):
            copy.wait()
        h2, l2 = split2(b2[at, :])
        h1, l1 = split2(b1[at, :])
        h2t = h2.T
        left = jnp.concatenate([h2t, h1.T], axis=0)
        acc[:R, :] += dot(h2t, h2)
        acc[R : 3 * R, :] += dot(left, l2)
        acc[3 * R : 5 * R, :] += dot(left, h1)
        acc[5 * R :, :] += dot(left, l1)

    def step(tile, carry):
        add_rows(tile_at(tile), tile + 1)
        return carry

    for sem, at in enumerate(parts):
        add_rows(at, sem)
    lax.fori_loop(1, tiles, step, 0)
    parts = [acc[i * R : i * R + R, :] for i in range(7)]
    store_symmetric(packed, OWN, parts[0] + parts[1] + parts[1].T)
    store_symmetric(packed, ROOT, parts[4] + parts[6] + parts[6].T)
    store_square(packed, CROSS, parts[3] + parts[5] + parts[2].T)
    store_halves(packed, keep, send)


def source_gram_kernel(b2, b1, sources, keep, send, acc, packed):
    acc[...] = jnp.zeros_like(acc)

    def step(tile, carry):
        hs, ls = split2(sources[tile_at(tile), :])
        hst = hs.T
        left = jnp.concatenate([hst, ls.T], axis=0)
        for which, panel in enumerate((b2, b1)):
            high, low = split2(panel[tile_at(tile), :])
            acc[which, : 2 * R, :] += dot(left, high)
            acc[which, 2 * R :, :] += dot(hst, low)
        return carry

    lax.fori_loop(0, b2.shape[0] // TILE, step, 0)
    for which, at in enumerate((PROJECTED, SIDE)):
        total = acc[which, :R, :] + acc[which, R : 2 * R, :] + acc[which, 2 * R :, :]
        store_square(packed, at, total.T)
    store_halves(packed, keep, send)


def cost(passes, rows, arrays):
    return pl.CostEstimate(
        flops=2 * passes * rows * R * R, bytes_accessed=4 * arrays * rows * R, transcendentals=0
    )


def panel_gram(q_two, q_one):
    rows = q_two.shape[0]
    part = jax.ShapeDtypeStruct((half_of(PANEL_TERMS), LANES), F32)
    tall = jax.ShapeDtypeStruct((rows, R), F32)
    return pl.pallas_call(
        panel_gram_kernel,
        in_specs=[pl.BlockSpec(memory_space=pl.ANY)] * 2,
        out_shape=(part, part, tall, tall),
        scratch_shapes=[
            pltpu.VMEM((7 * R, R), F32),
            pltpu.VMEM((PANEL_TERMS, LANES), F32),
            pltpu.SemaphoreType.DMA((2, rows // TILE + 1)),
        ],
        compiler_params=pltpu.CompilerParams(vmem_limit_bytes=VMEM_LIMIT),
        cost_estimate=cost(7, rows, 2),
        name="panel_gram",
    )(pltpu.with_memory_space_constraint(q_two, pltpu.HBM), pltpu.with_memory_space_constraint(q_one, pltpu.HBM))


def source_gram(b2, b1, sources):
    part = jax.ShapeDtypeStruct((half_of(SOURCE_TERMS), LANES), F32)
    return pl.pallas_call(
        source_gram_kernel,
        out_shape=(part, part),
        scratch_shapes=[pltpu.VMEM((2, 3 * R, R), F32), pltpu.VMEM((SOURCE_TERMS, LANES), F32)],
        compiler_params=pltpu.CompilerParams(vmem_limit_bytes=VMEM_LIMIT),
        cost_estimate=cost(6, b2.shape[0], 3),
        name="source_gram",
    )(b2, b1, sources)


def spread_lane(x, lane):
    return jnp.broadcast_to(x[:, lane : lane + 1], (8, LANES))


def sweep_panel(block, start, cols, rows):
    lane = lax.broadcasted_iota(jnp.int32, (8, LANES), 1)
    panel = block[start : start + GROUPS]
    left = stack_left(jnp.concatenate(panel, axis=0))
    for t in range(GROUPS):
        panel = eliminate_group(panel, t, start + t, cols, rows)
    inside = (lane >= 8 * start) & (lane < 8 * (start + GROUPS))
    panel = [jnp.where(inside, -x, x) for x in panel]
    change = dot_t(left, stack_right(jnp.concatenate(panel, axis=0)))
    swept = []
    for g in range(len(block)):
        if start <= g < start + GROUPS:
            swept.append(panel[g - start])
        else:
            swept.append(jnp.where(inside, 0.0, block[g]) - change[8 * g : 8 * g + 8, :])
    return swept


def eliminate_group(panel, t, at, cols, rows):
    lane = lax.broadcasted_iota(jnp.int32, (8, LANES), 1)
    sub = lax.broadcasted_iota(jnp.int32, (8, LANES), 0)
    for j in range(8):
        cols[64 * at + 8 * j : 64 * at + 8 * j + 8, :] = spread_lane(panel[t], 8 * at + j)
    rows[8 * at : 8 * at + 8, :] = panel[t]
    entry = {}
    for i in range(8):
        for j in range(i + 1):
            row = 64 * at + 8 * j + i
            entry[i, j] = jnp.broadcast_to(cols[row : row + 1, :], (8, LANES))
    inside = (lane >= 8 * at) & (lane < 8 * at + 8)
    line = []
    for j in range(8):
        row = jnp.broadcast_to(rows[8 * at + j : 8 * at + j + 1, :], (8, LANES))
        line.append(jnp.where(inside, jnp.where(lane == 8 * at + j, 1.0, 0.0), row))
    after = None
    if t < GROUPS - 1:
        columns = [spread_lane(panel[t + 1], 8 * at + j) for j in range(8)]
        after = [columns, jnp.where(inside, 0.0, panel[t + 1])]
    line, after = solve_small(entry, line, after)
    for g in range(GROUPS):
        if g == t + 1:
            panel[g] = after
        elif g != t:
            terms = [spread_lane(panel[g], 8 * at + j) * line[j] for j in range(8)]
            panel[g] = jnp.where(inside, 0.0, panel[g]) - tree_sum(terms)
    merged = line[0]
    for j in range(1, 8):
        merged = jnp.where(sub == j, line[j], merged)
    panel[t] = merged
    return panel


def tree_sum(terms):
    while len(terms) > 1:
        terms = [
            terms[i] + terms[i + 1] if i + 1 < len(terms) else terms[i]
            for i in range(0, len(terms), 2)
        ]
    return terms[0]


def solve_small(entry, line, after):
    columns, block = after or (None, None)
    factors, scaled = {}, {}
    for k in range(0, 8, 2):
        a, b, c = entry[k, k], entry[k + 1, k], entry[k + 1, k + 1]
        inv = pl.reciprocal(a * c - b * b, approx=True)
        below = range(k + 2, 8)
        first = {i: c * entry[i, k] - b * entry[i, k + 1] for i in below}
        second = {i: a * entry[i, k + 1] - b * entry[i, k] for i in below}
        for i in below:
            for j in range(k + 2, i + 1):
                entry[i, j] = entry[i, j] - inv * (first[i] * entry[j, k] + second[i] * entry[j, k + 1])
        top = c * line[k] - b * line[k + 1]
        bottom = a * line[k + 1] - b * line[k]
        if columns is not None:
            block = block - inv * (columns[k] * top + columns[k + 1] * bottom)
        scaled[k], scaled[k + 1] = inv * top, inv * bottom
        for i in below:
            m, n = inv * first[i], inv * second[i]
            factors[i, k] = m, n
            line[i] = line[i] - (m * line[k] + n * line[k + 1])
            if columns is not None:
                columns[i] = columns[i] - (m * columns[k] + n * columns[k + 1])
    for k in range(6, -1, -2):
        x, y = scaled[k], scaled[k + 1]
        if k < 6:
            x = x - tree_sum([factors[i, k][0] * line[i] for i in range(k + 2, 8)])
            y = y - tree_sum([factors[i, k][1] * line[i] for i in range(k + 2, 8)])
        line[k], line[k + 1] = x, y
    return line, block


def stack_left(x):
    h, m, l = split3(x)
    return jnp.concatenate([h, h, m, h, l, m], axis=0)


def stack_right(x):
    h, m, l = split3(x)
    return jnp.concatenate([h, m, h, l, h, m], axis=0)


def sweep(matrix, panels, cols, rows):
    block = [matrix[8 * i : 8 * i + 8, :] for i in range(LANES // 8)]
    for panel in panels:
        block = sweep_panel(block, panel * GROUPS, cols, rows)
    return jnp.concatenate(block, axis=0)


PANELS = LANES // (8 * GROUPS)


SQUARE = jax.ShapeDtypeStruct((R, R), F32)
CORNER = jax.ShapeDtypeStruct((LANES, LANES), F32)


def call(kernel, out_shape, args, name, scratch=(), flops=0):
    return pl.pallas_call(
        kernel,
        out_shape=out_shape,
        scratch_shapes=list(scratch),
        compiler_params=pltpu.CompilerParams(vmem_limit_bytes=VMEM_LIMIT),
        cost_estimate=pl.CostEstimate(flops=flops, bytes_accessed=R * R * 4, transcendentals=0),
        name=name,
    )(*args)


def first_kernel(which, gram_ref, coupling, first_out, across_out, rest_out, row_out, col_out, cols, rows):
    matrix = coupling[which()] + load_symmetric(gram_ref, OWN)
    eye = lax.broadcasted_iota(jnp.int32, (R, R), 0) == lax.broadcasted_iota(jnp.int32, (R, R), 1)
    diagonal = jnp.where(eye, matrix, 0.0)
    scale_row = lax.rsqrt(jnp.sum(diagonal, axis=0, keepdims=True))
    scale_col = lax.rsqrt(jnp.sum(diagonal, axis=1, keepdims=True))
    matrix = matrix * scale_col * scale_row
    side = matrix[:LANES, LANES:]
    first = -sweep(matrix[:LANES, :LANES], range(PANELS), cols, rows)
    across = dot_full(first, side)
    first_out[...] = first
    across_out[...] = across
    rest_out[...] = matrix[LANES:, LANES:] - dot_t_full(side, across)
    row_out[...] = jnp.broadcast_to(scale_row, (8, R))
    col_out[...] = jnp.broadcast_to(scale_col, (R, LANES))


def middle_kernel(rest, out, cols, rows):
    out[...] = sweep(rest[...], range(PANELS - 1), cols, rows)


def second_kernel(first, across, swept, row, col, out, cols, rows):
    second = -sweep(swept[...], range(PANELS - 1, PANELS), cols, rows)
    corner = -dot_full(across[...], second)
    top = first[...] - dot_full(corner, across[...].T)
    out[:LANES, :LANES] = top * col[:LANES, :] * row[:1, :LANES]
    out[:LANES, LANES:] = corner * col[:LANES, :] * row[:1, LANES:]
    out[LANES:, :LANES] = corner.T * col[LANES:, :] * row[:1, :LANES]
    out[LANES:, LANES:] = second * col[LANES:, :] * row[:1, LANES:]


SCRATCH = [pltpu.VMEM((1024, LANES), F32), pltpu.VMEM((LANES, LANES), F32)]
HALF_FLOPS = 5_000_000_000


def invert_first(which, packed, coupling, name):
    shapes = (
        CORNER,
        CORNER,
        CORNER,
        jax.ShapeDtypeStruct((8, R), F32),
        jax.ShapeDtypeStruct((R, LANES), F32),
    )
    kernel = functools.partial(first_kernel, which)
    return call(kernel, shapes, (packed, coupling), name, SCRATCH, HALF_FLOPS)


def invert_middle(parts, name):
    first, across, rest, row, col = parts
    rest = call(middle_kernel, CORNER, (rest,), name, SCRATCH, HALF_FLOPS // 2)
    return first, across, rest, row, col


def invert_second(parts, name):
    return call(second_kernel, SQUARE, parts, name, SCRATCH, HALF_FLOPS // 2)


def half_index():
    return lax.axis_index("group") // 2


def no_index():
    return 0


def panel_solve_kernel(inverse, terms, x_out, root_out):
    cross = load_square(terms, CROSS)
    x = dot_full(inverse[...], cross)
    x_out[...] = x
    store_symmetric(root_out, 0, load_symmetric(terms, ROOT) - dot_t_full(cross, x))


def wide(x):
    high, low = split2(x)
    return jnp.concatenate([high, high, low], axis=1)


def tall(x):
    high, low = split2(x)
    return jnp.concatenate([high, low, high], axis=0)


def by_tiles(rows, out, stage, sems, value, beside=None):
    tiles = rows // OUT_TILE

    def at(tile):
        return pl.ds(pl.multiple_of(tile * OUT_TILE, OUT_TILE), OUT_TILE)

    def copy(tile):
        return pltpu.make_async_copy(stage.at[at(tile)], out.at[at(tile)], sems.at[tile])

    def step(tile, carry):
        stage[at(tile), :] = value(at(tile))
        copy(tile).start()
        return carry

    lax.fori_loop(0, tiles, step, 0)
    if beside is not None:
        beside()
    for tile in range(tiles):
        copy(tile).wait()


def panel_kernel(b2, b1, sources, x, inverse, terms, out, level, high, low, side_out, stage, sems):
    projected = load_square(terms, PROJECTED)
    y = dot_full(inverse[...], projected)
    store_square(side_out, 0, load_square(terms, SIDE) - dot_t_full(x[...], projected))
    right = jnp.concatenate([tall(x[...]), tall(y)], axis=1)

    def value(at):
        change = dot(wide(b2[at, :]), right)
        panel = b1[at, :] - change[:, :R]
        level[at, :] = sources[at, :] - change[:, R:]
        high[at, :], low[at, :] = split2(panel)
        return panel

    by_tiles(b2.shape[0], out, stage, sems, value)


def field_kernel(level, high, low, inverse, side, out, stage, sems):
    weights = tall(dot(wide(inverse[...]), tall(load_square(side, 0))))

    def value(at):
        left = jnp.concatenate([high[at, :], high[at, :], low[at, :]], axis=1)
        return level[at, :] - dot(left, weights)

    by_tiles(level.shape[0], out, stage, sems, value)


def update(kernel, args, passes, name, more=()):
    rows = args[0].shape[0]
    return pl.pallas_call(
        kernel,
        out_specs=[pl.BlockSpec(memory_space=pl.ANY)] + [pl.BlockSpec(memory_space=pltpu.VMEM)] * len(more),
        out_shape=[jax.ShapeDtypeStruct((rows, R), F32), *more],
        scratch_shapes=[pltpu.VMEM((rows, R), F32), pltpu.SemaphoreType.DMA((rows // OUT_TILE,))],
        compiler_params=pltpu.CompilerParams(vmem_limit_bytes=VMEM_LIMIT),
        cost_estimate=cost(passes, rows, 3),
        name=name,
    )(*args)


def exchange(x, mask):
    count = lax.axis_size(AXES)
    return lax.ppermute(x, AXES, [(i, i ^ mask) for i in range(count)])


def choose(x, upper):
    half = half_of(x.shape[0])
    low, high = x[:half], x[x.shape[0] - half :]
    return jnp.where(upper, high, low), jnp.where(upper, low, high)


def join(x, other, rows, upper):
    low, high = jnp.where(upper, other, x), jnp.where(upper, x, other)
    return jnp.concatenate([low[: rows - x.shape[0]], high], axis=0)


def summing_stages(bits):
    down = [("scatter", bit) for bit in bits[:-1]]
    return down + [("sum", bits[-1])] + [("gather", bit) for bit in reversed(bits[:-1])]


class Chain:
    def __init__(self, value, upper):
        self.value, self.upper, self.sizes = value, upper, {}

    def start(self, kind, bit):
        self.kind, self.bit = kind, bit
        sent = self.value
        if kind == "scatter":
            self.sizes[bit] = self.value.shape[0]
            self.value, sent = choose(self.value, self.upper[bit])
        self.flying = exchange(sent, 1 << bit)

    def finish(self):
        if self.kind == "gather":
            self.value = join(self.value, self.flying, self.sizes[self.bit], self.upper[self.bit])
        else:
            self.value = self.value + self.flying


def per_device(q_two, q_one, sources, coupling_two, coupling_one):
    index = lax.axis_index(AXES)
    places = lax.axis_size(AXES).bit_length() - 1
    flags = [(index >> bit) & 1 == 1 for bit in range(places)]
    q_two, *upper = lax.optimization_barrier((q_two, *flags))
    stages = summing_stages(list(range(2, places)))

    keep, send, b2, b1 = panel_gram(q_two, q_one)
    arriving = exchange(send, 1)
    source_keep, source_send = source_gram(b2, b1, sources)
    arriving, source_send = lax.optimization_barrier((arriving, source_send))

    panels = Chain(keep + arriving, upper)
    source = Chain(source_keep, upper)
    panels.sizes[0], source.sizes[0] = PANEL_TERMS, SOURCE_TERMS
    source_left = [("gather", 0)] + stages[::-1]
    for step, stage in enumerate(stages):
        panels.start(*stage)
        if step == 0:
            source.kind, source.bit, source.flying = "sum", 0, exchange(source_send, 1)
        else:
            source.start(*source_left.pop())
        panels.flying, source.flying = lax.optimization_barrier((panels.flying, source.flying))
        panels.finish()
        source.finish()
    panels.start("gather", 0)
    source.start(*source_left.pop())
    panels.finish()
    terms = panels.value
    parts = invert_first(half_index, terms, coupling_two, "level_first")
    parts = invert_middle(parts, "level_middle")
    source.flying, parts = lax.optimization_barrier((source.flying, parts))
    source.finish()
    source.start(*source_left.pop())
    inverse = invert_second(parts, "level_second")
    x, root = call(
        panel_solve_kernel, (SQUARE, jax.ShapeDtypeStruct((SYMMETRIC, LANES), F32)), (inverse, terms), "panel_solve"
    )
    source.flying, x = lax.optimization_barrier((source.flying, x))
    source.finish()
    arriving = exchange(root, 2)
    rows = b2.shape[0]
    shapes = [jax.ShapeDtypeStruct((rows, R), kind) for kind in (F32, BF16, BF16)]
    shapes.append(jax.ShapeDtypeStruct((FULL, LANES), F32))
    args = [b2, b1, sources, x, inverse, source.value]
    panel_one, level, high, low, side = update(panel_kernel, args, 8, "panel", shapes)
    side = Chain(choose(side, upper[0])[0], upper)
    side.sizes[0] = FULL
    side_flying = exchange(side.value, 2)
    arriving, side.value = lax.optimization_barrier((arriving, side.value))
    root = root + arriving
    parts = invert_first(no_index, root, coupling_one[None], "root_first")
    parts = invert_middle(parts, "root_middle")
    side_flying, parts = lax.optimization_barrier((side_flying, parts))
    side.value = side.value + side_flying
    side.start("gather", 0)
    inverse = invert_second(parts, "root_second")
    side.finish()
    (solution,) = update(field_kernel, [level, high, low, inverse, side.value], 3, "field")
    return (panel_one, solution)


def solution(mesh):
    placed = P(("group", "leaf"), None)
    return jax.shard_map(
        per_device,
        mesh=mesh,
        in_specs=(placed, placed, placed, P(), P()),
        out_specs=(placed, placed),
        check_vma=False,
    )
```

```python
import functools

import jax
import jax.numpy as jnp
from jax import lax
from jax.experimental import pallas as pl
from jax.experimental.pallas import tpu as pltpu
from jax.sharding import PartitionSpec as P

HIGH = lax.Precision.HIGHEST
AXES = ("leaf", "group")
F32 = jnp.float32
BF16 = jnp.bfloat16
R = 256
LANES = 128
TILE = 512
OUT_TILE = 1024
GROUPS = 8
VMEM_LIMIT = 16 * 1024 * 1024
SYMMETRIC, FULL = 264, 512
OWN, ROOT, CROSS, PANEL_TERMS = 0, 264, 528, 1040
PROJECTED, SIDE, SOURCE_TERMS = 0, 512, 1024


def split2(x):
    high = x.astype(BF16)
    return high, (x - high.astype(F32)).astype(BF16)


def split3(x):
    high = x.astype(BF16)
    rest = x - high.astype(F32)
    mid = rest.astype(BF16)
    return high, mid, (rest - mid.astype(F32)).astype(BF16)


def dot(left, right):
    return jnp.dot(left, right, preferred_element_type=F32)


def dot_t(left, right):
    return lax.dot_general(left, right, (((0,), (0,)), ((), ())), preferred_element_type=F32)


def dot_full(left, right):
    return jnp.dot(left, right, precision=HIGH, preferred_element_type=F32)


def dot_t_full(left, right):
    return lax.dot_general(
        left, right, (((0,), (0,)), ((), ())), precision=HIGH, preferred_element_type=F32
    )


def square_index():
    row = lax.broadcasted_iota(jnp.int32, (LANES, LANES), 0)
    return row, lax.broadcasted_iota(jnp.int32, (LANES, LANES), 1)


def store_symmetric(ref, at, block):
    row, col = square_index()
    last = block[128:, 128:]
    ref[at : at + 128, :] = block[128:, :128]
    ref[at + 128 : at + 256, :] = jnp.where(row >= col, block[:128, :128], last)
    diagonal = jnp.sum(jnp.where(row == col, last, 0.0), axis=0, keepdims=True)
    ref[at + 256 : at + 264, :] = jnp.broadcast_to(diagonal, (8, LANES))


def store_square(ref, row, block):
    ref[row : row + 256, :] = block[:, :128]
    ref[row + 256 : row + 512, :] = block[:, 128:]


def load_symmetric(ref, at):
    row, col = square_index()
    lower = ref[at : at + 128, :]
    mixed = ref[at + 128 : at + 256, :]
    turned = mixed.T
    first = jnp.where(row >= col, mixed, turned)
    last = jnp.where(row < col, mixed, turned)
    last = jnp.where(row == col, ref[at + 256 : at + 257, :], last)
    top = jnp.concatenate([first, lower.T], axis=1)
    return jnp.concatenate([top, jnp.concatenate([lower, last], axis=1)], axis=0)


def load_square(ref, row):
    return jnp.concatenate([ref[row : row + 256, :], ref[row + 256 : row + 512, :]], axis=1)


def half_of(rows):
    return (rows + 15) // 16 * 8


def store_halves(packed, keep, send):
    half = half_of(packed.shape[0])
    far = packed.shape[0] - half
    mine = lax.rem(lax.axis_index("group"), 2)
    keep[...] = packed[pl.ds(pl.multiple_of(mine * far, 8), half), :]
    send[...] = packed[pl.ds(pl.multiple_of((1 - mine) * far, 8), half), :]


def tile_at(tile):
    return pl.ds(pl.multiple_of(tile * TILE, TILE), TILE)


def panel_gram_kernel(q_two, q_one, keep, send, b2, b1, acc, packed, sems):
    tiles = b2.shape[0] // TILE
    pairs = ((q_two, b2), (q_one, b1))

    def copies(at, sem):
        return [
            pltpu.make_async_copy(source.at[at], target.at[at], sems.at[which, sem])
            for which, (source, target) in enumerate(pairs)
        ]

    for tile in range(tiles):
        for copy in copies(tile_at(tile), tile):
            copy.start()
    acc[...] = jnp.zeros_like(acc)

    def step(tile, carry):
        for copy in copies(tile_at(tile), tile):
            copy.wait()
        h2, l2 = split2(b2[tile_at(tile), :])
        h1, l1 = split2(b1[tile_at(tile), :])
        h2t, l2t, h1t = h2.T, l2.T, h1.T
        acc[0] += dot(h2t, h2)
        acc[1] += dot(h2t, l2)
        left = jnp.concatenate([h2t, h2t, l2t], axis=1)
        acc[2] += dot(left, jnp.concatenate([h1, l1, h1], axis=0))
        acc[3] += dot(h1t, h1)
        acc[4] += dot(h1t, l1)
        return carry

    lax.fori_loop(0, tiles, step, 0)
    low = acc[1]
    store_symmetric(packed, OWN, acc[0] + low + low.T)
    low = acc[4]
    store_symmetric(packed, ROOT, acc[3] + low + low.T)
    store_square(packed, CROSS, acc[2])
    store_halves(packed, keep, send)


def source_gram_kernel(b2, b1, sources, keep, send, acc, packed):
    acc[...] = jnp.zeros_like(acc)

    def step(tile, carry):
        hs, ls = split2(sources[tile_at(tile), :])
        right = jnp.concatenate([hs, ls, hs], axis=0)
        for which, panel in enumerate((b2, b1)):
            high, low = split2(panel[tile_at(tile), :])
            turned = high.T
            acc[which] += dot(jnp.concatenate([turned, turned, low.T], axis=1), right)
        return carry

    lax.fori_loop(0, b2.shape[0] // TILE, step, 0)
    store_square(packed, PROJECTED, acc[0])
    store_square(packed, SIDE, acc[1])
    store_halves(packed, keep, send)


def cost(passes, rows, arrays):
    return pl.CostEstimate(
        flops=2 * passes * rows * R * R, bytes_accessed=4 * arrays * rows * R, transcendentals=0
    )


def panel_gram(q_two, q_one):
    rows = q_two.shape[0]
    part = jax.ShapeDtypeStruct((half_of(PANEL_TERMS), LANES), F32)
    tall = jax.ShapeDtypeStruct((rows, R), F32)
    return pl.pallas_call(
        panel_gram_kernel,
        in_specs=[pl.BlockSpec(memory_space=pl.ANY)] * 2,
        out_shape=(part, part, tall, tall),
        scratch_shapes=[
            pltpu.VMEM((5, R, R), F32),
            pltpu.VMEM((PANEL_TERMS, LANES), F32),
            pltpu.SemaphoreType.DMA((2, rows // TILE)),
        ],
        compiler_params=pltpu.CompilerParams(vmem_limit_bytes=VMEM_LIMIT),
        cost_estimate=cost(7, rows, 2),
        name="panel_gram",
    )(pltpu.with_memory_space_constraint(q_two, pltpu.HBM), pltpu.with_memory_space_constraint(q_one, pltpu.HBM))


def source_gram(b2, b1, sources):
    part = jax.ShapeDtypeStruct((half_of(SOURCE_TERMS), LANES), F32)
    return pl.pallas_call(
        source_gram_kernel,
        out_shape=(part, part),
        scratch_shapes=[pltpu.VMEM((2, R, R), F32), pltpu.VMEM((SOURCE_TERMS, LANES), F32)],
        compiler_params=pltpu.CompilerParams(vmem_limit_bytes=VMEM_LIMIT),
        cost_estimate=cost(6, b2.shape[0], 3),
        name="source_gram",
    )(b2, b1, sources)


def spread_lane(x, lane):
    return jnp.broadcast_to(x[:, lane : lane + 1], (8, LANES))


def sweep_panel(block, start, cols, rows):
    lane = lax.broadcasted_iota(jnp.int32, (8, LANES), 1)
    panel = block[start : start + GROUPS]
    left = stack_left(jnp.concatenate(panel, axis=0))
    for t in range(GROUPS):
        panel = eliminate_group(panel, t, start + t, cols, rows)
    inside = (lane >= 8 * start) & (lane < 8 * (start + GROUPS))
    panel = [jnp.where(inside, -x, x) for x in panel]
    change = dot_t(left, stack_right(jnp.concatenate(panel, axis=0)))
    swept = []
    for g in range(len(block)):
        if start <= g < start + GROUPS:
            swept.append(panel[g - start])
        else:
            swept.append(jnp.where(inside, 0.0, block[g]) - change[8 * g : 8 * g + 8, :])
    return swept


def eliminate_group(panel, t, at, cols, rows):
    lane = lax.broadcasted_iota(jnp.int32, (8, LANES), 1)
    sub = lax.broadcasted_iota(jnp.int32, (8, LANES), 0)
    for j in range(8):
        cols[64 * at + 8 * j : 64 * at + 8 * j + 8, :] = spread_lane(panel[t], 8 * at + j)
    rows[8 * at : 8 * at + 8, :] = panel[t]
    entry = {}
    for i in range(8):
        for j in range(i + 1):
            row = 64 * at + 8 * j + i
            entry[i, j] = jnp.broadcast_to(cols[row : row + 1, :], (8, LANES))
    inside = (lane >= 8 * at) & (lane < 8 * at + 8)
    line = []
    for j in range(8):
        row = jnp.broadcast_to(rows[8 * at + j : 8 * at + j + 1, :], (8, LANES))
        line.append(jnp.where(inside, jnp.where(lane == 8 * at + j, 1.0, 0.0), row))
    after = None
    if t < GROUPS - 1:
        columns = [spread_lane(panel[t + 1], 8 * at + j) for j in range(8)]
        after = [columns, jnp.where(inside, 0.0, panel[t + 1])]
    line, after = solve_small(entry, line, after)
    for g in range(GROUPS):
        if g == t + 1:
            panel[g] = after
        elif g != t:
            terms = [spread_lane(panel[g], 8 * at + j) * line[j] for j in range(8)]
            panel[g] = jnp.where(inside, 0.0, panel[g]) - tree_sum(terms)
    merged = line[0]
    for j in range(1, 8):
        merged = jnp.where(sub == j, line[j], merged)
    panel[t] = merged
    return panel


def tree_sum(terms):
    while len(terms) > 1:
        terms = [
            terms[i] + terms[i + 1] if i + 1 < len(terms) else terms[i]
            for i in range(0, len(terms), 2)
        ]
    return terms[0]


def solve_small(entry, line, after):
    columns, block = after or (None, None)
    factors, scaled = {}, {}
    for k in range(0, 8, 2):
        a, b, c = entry[k, k], entry[k + 1, k], entry[k + 1, k + 1]
        inv = pl.reciprocal(a * c - b * b, approx=True)
        below = range(k + 2, 8)
        first = {i: c * entry[i, k] - b * entry[i, k + 1] for i in below}
        second = {i: a * entry[i, k + 1] - b * entry[i, k] for i in below}
        for i in below:
            for j in range(k + 2, i + 1):
                entry[i, j] = entry[i, j] - inv * (first[i] * entry[j, k] + second[i] * entry[j, k + 1])
        top = c * line[k] - b * line[k + 1]
        bottom = a * line[k + 1] - b * line[k]
        if columns is not None:
            block = block - inv * (columns[k] * top + columns[k + 1] * bottom)
        scaled[k], scaled[k + 1] = inv * top, inv * bottom
        for i in below:
            m, n = inv * first[i], inv * second[i]
            factors[i, k] = m, n
            line[i] = line[i] - (m * line[k] + n * line[k + 1])
            if columns is not None:
                columns[i] = columns[i] - (m * columns[k] + n * columns[k + 1])
    for k in range(6, -1, -2):
        x, y = scaled[k], scaled[k + 1]
        if k < 6:
            x = x - tree_sum([factors[i, k][0] * line[i] for i in range(k + 2, 8)])
            y = y - tree_sum([factors[i, k][1] * line[i] for i in range(k + 2, 8)])
        line[k], line[k + 1] = x, y
    return line, block


def stack_left(x):
    h, m, l = split3(x)
    return jnp.concatenate([h, h, m, h, l, m], axis=0)


def stack_right(x):
    h, m, l = split3(x)
    return jnp.concatenate([h, m, h, l, h, m], axis=0)


def sweep(matrix, panels, cols, rows):
    block = [matrix[8 * i : 8 * i + 8, :] for i in range(LANES // 8)]
    for panel in panels:
        block = sweep_panel(block, panel * GROUPS, cols, rows)
    return jnp.concatenate(block, axis=0)


PANELS = LANES // (8 * GROUPS)


SQUARE = jax.ShapeDtypeStruct((R, R), F32)
CORNER = jax.ShapeDtypeStruct((LANES, LANES), F32)


def call(kernel, out_shape, args, name, scratch=(), flops=0):
    return pl.pallas_call(
        kernel,
        out_shape=out_shape,
        scratch_shapes=list(scratch),
        compiler_params=pltpu.CompilerParams(vmem_limit_bytes=VMEM_LIMIT),
        cost_estimate=pl.CostEstimate(flops=flops, bytes_accessed=R * R * 4, transcendentals=0),
        name=name,
    )(*args)


def first_kernel(which, gram_ref, coupling, first_out, across_out, rest_out, row_out, col_out, cols, rows):
    matrix = coupling[which()] + load_symmetric(gram_ref, OWN)
    eye = lax.broadcasted_iota(jnp.int32, (R, R), 0) == lax.broadcasted_iota(jnp.int32, (R, R), 1)
    diagonal = jnp.where(eye, matrix, 0.0)
    scale_row = lax.rsqrt(jnp.sum(diagonal, axis=0, keepdims=True))
    scale_col = lax.rsqrt(jnp.sum(diagonal, axis=1, keepdims=True))
    matrix = matrix * scale_col * scale_row
    side = matrix[:LANES, LANES:]
    first = -sweep(matrix[:LANES, :LANES], range(PANELS), cols, rows)
    across = dot_full(first, side)
    first_out[...] = first
    across_out[...] = across
    rest_out[...] = matrix[LANES:, LANES:] - dot_t_full(side, across)
    row_out[...] = jnp.broadcast_to(scale_row, (8, R))
    col_out[...] = jnp.broadcast_to(scale_col, (R, LANES))


def middle_kernel(rest, out, cols, rows):
    out[...] = sweep(rest[...], range(PANELS - 1), cols, rows)


def second_kernel(first, across, swept, row, col, out, cols, rows):
    second = -sweep(swept[...], range(PANELS - 1, PANELS), cols, rows)
    corner = -dot_full(across[...], second)
    top = first[...] - dot_full(corner, across[...].T)
    out[:LANES, :LANES] = top * col[:LANES, :] * row[:1, :LANES]
    out[:LANES, LANES:] = corner * col[:LANES, :] * row[:1, LANES:]
    out[LANES:, :LANES] = corner.T * col[LANES:, :] * row[:1, :LANES]
    out[LANES:, LANES:] = second * col[LANES:, :] * row[:1, LANES:]


SCRATCH = [pltpu.VMEM((1024, LANES), F32), pltpu.VMEM((LANES, LANES), F32)]
HALF_FLOPS = 5_000_000_000


def invert_first(which, packed, coupling, name):
    shapes = (
        CORNER,
        CORNER,
        CORNER,
        jax.ShapeDtypeStruct((8, R), F32),
        jax.ShapeDtypeStruct((R, LANES), F32),
    )
    kernel = functools.partial(first_kernel, which)
    return call(kernel, shapes, (packed, coupling), name, SCRATCH, HALF_FLOPS)


def invert_middle(parts, name):
    first, across, rest, row, col = parts
    rest = call(middle_kernel, CORNER, (rest,), name, SCRATCH, HALF_FLOPS // 2)
    return first, across, rest, row, col


def invert_second(parts, name):
    return call(second_kernel, SQUARE, parts, name, SCRATCH, HALF_FLOPS // 2)


def half_index():
    return lax.axis_index("group") // 2


def no_index():
    return 0


def panel_solve_kernel(inverse, terms, x_out, root_out):
    cross = load_square(terms, CROSS)
    x = dot_full(inverse[...], cross)
    x_out[...] = x
    store_symmetric(root_out, 0, load_symmetric(terms, ROOT) - dot_t_full(cross, x))


def wide(x):
    high, low = split2(x)
    return jnp.concatenate([high, high, low], axis=1)


def tall(x):
    high, low = split2(x)
    return jnp.concatenate([high, low, high], axis=0)


def by_tiles(rows, out, stage, sems, value, beside=None):
    tiles = rows // OUT_TILE

    def at(tile):
        return pl.ds(pl.multiple_of(tile * OUT_TILE, OUT_TILE), OUT_TILE)

    def copy(tile):
        return pltpu.make_async_copy(stage.at[at(tile)], out.at[at(tile)], sems.at[tile])

    def step(tile, carry):
        stage[at(tile), :] = value(at(tile))
        copy(tile).start()
        return carry

    lax.fori_loop(0, tiles, step, 0)
    if beside is not None:
        beside()
    for tile in range(tiles):
        copy(tile).wait()


def panel_kernel(b2, b1, sources, x, inverse, terms, out, level, high, low, side_out, stage, sems):
    projected = load_square(terms, PROJECTED)
    y = dot_full(inverse[...], projected)
    store_square(side_out, 0, load_square(terms, SIDE) - dot_t_full(x[...], projected))
    right = jnp.concatenate([tall(x[...]), tall(y)], axis=1)

    def value(at):
        change = dot(wide(b2[at, :]), right)
        panel = b1[at, :] - change[:, :R]
        level[at, :] = sources[at, :] - change[:, R:]
        high[at, :], low[at, :] = split2(panel)
        return panel

    by_tiles(b2.shape[0], out, stage, sems, value)


def field_kernel(level, high, low, inverse, side, out, stage, sems):
    weights = tall(dot(wide(inverse[...]), tall(load_square(side, 0))))

    def value(at):
        left = jnp.concatenate([high[at, :], high[at, :], low[at, :]], axis=1)
        return level[at, :] - dot(left, weights)

    by_tiles(level.shape[0], out, stage, sems, value)


def update(kernel, args, passes, name, more=()):
    rows = args[0].shape[0]
    return pl.pallas_call(
        kernel,
        out_specs=[pl.BlockSpec(memory_space=pl.ANY)] + [pl.BlockSpec(memory_space=pltpu.VMEM)] * len(more),
        out_shape=[jax.ShapeDtypeStruct((rows, R), F32), *more],
        scratch_shapes=[pltpu.VMEM((rows, R), F32), pltpu.SemaphoreType.DMA((rows // OUT_TILE,))],
        compiler_params=pltpu.CompilerParams(vmem_limit_bytes=VMEM_LIMIT),
        cost_estimate=cost(passes, rows, 3),
        name=name,
    )(*args)


def exchange(x, mask):
    count = lax.axis_size(AXES)
    return lax.ppermute(x, AXES, [(i, i ^ mask) for i in range(count)])


def choose(x, upper):
    half = half_of(x.shape[0])
    low, high = x[:half], x[x.shape[0] - half :]
    return jnp.where(upper, high, low), jnp.where(upper, low, high)


def join(x, other, rows, upper):
    low, high = jnp.where(upper, other, x), jnp.where(upper, x, other)
    return jnp.concatenate([low[: rows - x.shape[0]], high], axis=0)


def summing_stages(bits):
    down = [("scatter", bit) for bit in bits[:-1]]
    return down + [("sum", bits[-1])] + [("gather", bit) for bit in reversed(bits[:-1])]


class Chain:
    def __init__(self, value, upper):
        self.value, self.upper, self.sizes = value, upper, {}

    def start(self, kind, bit):
        self.kind, self.bit = kind, bit
        sent = self.value
        if kind == "scatter":
            self.sizes[bit] = self.value.shape[0]
            self.value, sent = choose(self.value, self.upper[bit])
        self.flying = exchange(sent, 1 << bit)

    def finish(self):
        if self.kind == "gather":
            self.value = join(self.value, self.flying, self.sizes[self.bit], self.upper[self.bit])
        else:
            self.value = self.value + self.flying


def per_device(q_two, q_one, sources, coupling_two, coupling_one):
    index = lax.axis_index(AXES)
    places = lax.axis_size(AXES).bit_length() - 1
    flags = [(index >> bit) & 1 == 1 for bit in range(places)]
    q_two, *upper = lax.optimization_barrier((q_two, *flags))
    stages = summing_stages(list(range(2, places)))

    keep, send, b2, b1 = panel_gram(q_two, q_one)
    arriving = exchange(send, 1)
    source_keep, source_send = source_gram(b2, b1, sources)
    arriving, source_send = lax.optimization_barrier((arriving, source_send))

    panels = Chain(keep + arriving, upper)
    source = Chain(source_keep, upper)
    panels.sizes[0], source.sizes[0] = PANEL_TERMS, SOURCE_TERMS
    source_left = [("gather", 0)] + stages[::-1]
    for step, stage in enumerate(stages):
        panels.start(*stage)
        if step == 0:
            source.kind, source.bit, source.flying = "sum", 0, exchange(source_send, 1)
        else:
            source.start(*source_left.pop())
        panels.flying, source.flying = lax.optimization_barrier((panels.flying, source.flying))
        panels.finish()
        source.finish()
    panels.start("gather", 0)
    source.start(*source_left.pop())
    panels.finish()
    terms = panels.value
    parts = invert_first(half_index, terms, coupling_two, "level_first")
    parts = invert_middle(parts, "level_middle")
    source.flying, parts = lax.optimization_barrier((source.flying, parts))
    source.finish()
    source.start(*source_left.pop())
    inverse = invert_second(parts, "level_second")
    x, root = call(
        panel_solve_kernel, (SQUARE, jax.ShapeDtypeStruct((SYMMETRIC, LANES), F32)), (inverse, terms), "panel_solve"
    )
    source.flying, x = lax.optimization_barrier((source.flying, x))
    source.finish()
    arriving = exchange(root, 2)
    rows = b2.shape[0]
    shapes = [jax.ShapeDtypeStruct((rows, R), kind) for kind in (F32, BF16, BF16)]
    shapes.append(jax.ShapeDtypeStruct((FULL, LANES), F32))
    args = [b2, b1, sources, x, inverse, source.value]
    panel_one, level, high, low, side = update(panel_kernel, args, 8, "panel", shapes)
    side = Chain(choose(side, upper[0])[0], upper)
    side.sizes[0] = FULL
    side_flying = exchange(side.value, 2)
    arriving, side.value = lax.optimization_barrier((arriving, side.value))
    root = root + arriving
    parts = invert_first(no_index, root, coupling_one[None], "root_first")
    parts = invert_middle(parts, "root_middle")
    side_flying, parts = lax.optimization_barrier((side_flying, parts))
    side.value = side.value + side_flying
    side.start("gather", 0)
    inverse = invert_second(parts, "root_second")
    side.finish()
    (solution,) = update(field_kernel, [level, high, low, inverse, side.value], 3, "field")
    return (panel_one, solution)


def solution(mesh):
    placed = P(("group", "leaf"), None)
    return jax.shard_map(
        per_device,
        mesh=mesh,
        in_specs=(placed, placed, placed, P(), P()),
        out_specs=(placed, placed),
        check_vma=False,
    )
```

```python
import functools

import jax
import jax.numpy as jnp
from jax import lax
from jax.experimental import pallas as pl
from jax.experimental.pallas import tpu as pltpu
from jax.sharding import PartitionSpec as P

HIGH = lax.Precision.HIGHEST
AXES = ("leaf", "group")
F32 = jnp.float32
BF16 = jnp.bfloat16
R = 256
LANES = 128
TILE = 512
OUT_TILE = 1024
GROUPS = 8
VMEM_LIMIT = 16 * 1024 * 1024
SYMMETRIC, FULL = 264, 512
OWN, ROOT, CROSS, PANEL_TERMS = 0, 264, 528, 1040
PROJECTED, SIDE, SOURCE_TERMS = 0, 512, 1024


def split2(x):
    high = x.astype(BF16)
    return high, (x - high.astype(F32)).astype(BF16)


def split3(x):
    high = x.astype(BF16)
    rest = x - high.astype(F32)
    mid = rest.astype(BF16)
    return high, mid, (rest - mid.astype(F32)).astype(BF16)


def dot(left, right):
    return jnp.dot(left, right, preferred_element_type=F32)


def dot_t(left, right):
    return lax.dot_general(left, right, (((0,), (0,)), ((), ())), preferred_element_type=F32)


def dot_full(left, right):
    return jnp.dot(left, right, precision=HIGH, preferred_element_type=F32)


def dot_t_full(left, right):
    return lax.dot_general(
        left, right, (((0,), (0,)), ((), ())), precision=HIGH, preferred_element_type=F32
    )


def square_index():
    row = lax.broadcasted_iota(jnp.int32, (LANES, LANES), 0)
    return row, lax.broadcasted_iota(jnp.int32, (LANES, LANES), 1)


def store_symmetric(ref, at, block):
    row, col = square_index()
    last = block[128:, 128:]
    ref[at : at + 128, :] = block[128:, :128]
    ref[at + 128 : at + 256, :] = jnp.where(row >= col, block[:128, :128], last)
    diagonal = jnp.sum(jnp.where(row == col, last, 0.0), axis=0, keepdims=True)
    ref[at + 256 : at + 264, :] = jnp.broadcast_to(diagonal, (8, LANES))


def store_square(ref, row, block):
    ref[row : row + 256, :] = block[:, :128]
    ref[row + 256 : row + 512, :] = block[:, 128:]


def load_symmetric(ref, at):
    row, col = square_index()
    lower = ref[at : at + 128, :]
    mixed = ref[at + 128 : at + 256, :]
    turned = mixed.T
    first = jnp.where(row >= col, mixed, turned)
    last = jnp.where(row < col, mixed, turned)
    last = jnp.where(row == col, ref[at + 256 : at + 257, :], last)
    top = jnp.concatenate([first, lower.T], axis=1)
    return jnp.concatenate([top, jnp.concatenate([lower, last], axis=1)], axis=0)


def load_square(ref, row):
    return jnp.concatenate([ref[row : row + 256, :], ref[row + 256 : row + 512, :]], axis=1)


def half_of(rows):
    return (rows + 15) // 16 * 8


def store_halves(packed, keep, send):
    half = half_of(packed.shape[0])
    far = packed.shape[0] - half
    mine = lax.rem(lax.axis_index("group"), 2)
    keep[...] = packed[pl.ds(pl.multiple_of(mine * far, 8), half), :]
    send[...] = packed[pl.ds(pl.multiple_of((1 - mine) * far, 8), half), :]


def tile_at(tile, size=TILE):
    return pl.ds(pl.multiple_of(tile * size, size), size)


def panel_gram_kernel(q_two, q_one, keep, send, b2, b1, acc, packed, sems):
    tiles = b2.shape[0] // TILE
    pairs = ((q_two, b2), (q_one, b1))

    def copies(at, sem):
        return [
            pltpu.make_async_copy(source.at[at], target.at[at], sems.at[which, sem])
            for which, (source, target) in enumerate(pairs)
        ]

    for tile in range(tiles):
        for copy in copies(tile_at(tile), tile):
            copy.start()
    acc[...] = jnp.zeros_like(acc)

    def step(tile, carry):
        for copy in copies(tile_at(tile), tile):
            copy.wait()
        h2, l2 = split2(b2[tile_at(tile), :])
        h1, l1 = split2(b1[tile_at(tile), :])
        h2t, l2t, h1t = h2.T, l2.T, h1.T
        acc[0] += dot(h2t, h2)
        acc[1] += dot(h2t, l2)
        left = jnp.concatenate([h2t, h2t, l2t], axis=1)
        acc[2] += dot(left, jnp.concatenate([h1, l1, h1], axis=0))
        acc[3] += dot(h1t, h1)
        acc[4] += dot(h1t, l1)
        return carry

    lax.fori_loop(0, tiles, step, 0)
    low = acc[1]
    store_symmetric(packed, OWN, acc[0] + low + low.T)
    low = acc[4]
    store_symmetric(packed, ROOT, acc[3] + low + low.T)
    store_square(packed, CROSS, acc[2])
    store_halves(packed, keep, send)


def source_gram_kernel(b2, b1, sources, keep, send, acc, packed):
    acc[...] = jnp.zeros_like(acc)

    def step(tile, carry):
        hs, ls = split2(sources[tile_at(tile, OUT_TILE), :])
        right = jnp.concatenate([hs, ls, hs], axis=0)
        for which, panel in enumerate((b2, b1)):
            high, low = split2(panel[tile_at(tile, OUT_TILE), :])
            turned = high.T
            acc[which] += dot(jnp.concatenate([turned, turned, low.T], axis=1), right)
        return carry

    lax.fori_loop(0, b2.shape[0] // OUT_TILE, step, 0)
    store_square(packed, PROJECTED, acc[0])
    store_square(packed, SIDE, acc[1])
    store_halves(packed, keep, send)


def cost(passes, rows, arrays):
    return pl.CostEstimate(
        flops=2 * passes * rows * R * R, bytes_accessed=4 * arrays * rows * R, transcendentals=0
    )


def panel_gram(q_two, q_one):
    rows = q_two.shape[0]
    part = jax.ShapeDtypeStruct((half_of(PANEL_TERMS), LANES), F32)
    tall = jax.ShapeDtypeStruct((rows, R), F32)
    return pl.pallas_call(
        panel_gram_kernel,
        in_specs=[pl.BlockSpec(memory_space=pl.ANY)] * 2,
        out_shape=(part, part, tall, tall),
        scratch_shapes=[
            pltpu.VMEM((5, R, R), F32),
            pltpu.VMEM((PANEL_TERMS, LANES), F32),
            pltpu.SemaphoreType.DMA((2, rows // TILE)),
        ],
        compiler_params=pltpu.CompilerParams(vmem_limit_bytes=VMEM_LIMIT),
        cost_estimate=cost(7, rows, 2),
        name="panel_gram",
    )(pltpu.with_memory_space_constraint(q_two, pltpu.HBM), pltpu.with_memory_space_constraint(q_one, pltpu.HBM))


def source_gram(b2, b1, sources):
    part = jax.ShapeDtypeStruct((half_of(SOURCE_TERMS), LANES), F32)
    return pl.pallas_call(
        source_gram_kernel,
        out_shape=(part, part),
        scratch_shapes=[pltpu.VMEM((2, R, R), F32), pltpu.VMEM((SOURCE_TERMS, LANES), F32)],
        compiler_params=pltpu.CompilerParams(vmem_limit_bytes=VMEM_LIMIT),
        cost_estimate=cost(6, b2.shape[0], 3),
        name="source_gram",
    )(b2, b1, sources)


def spread_lane(x, lane):
    return jnp.broadcast_to(x[:, lane : lane + 1], (8, LANES))


def sweep_panel(block, start, cols, rows):
    lane = lax.broadcasted_iota(jnp.int32, (8, LANES), 1)
    panel = block[start : start + GROUPS]
    left = stack_left(jnp.concatenate(panel, axis=0))
    for t in range(GROUPS):
        panel = eliminate_group(panel, t, start + t, cols, rows)
    inside = (lane >= 8 * start) & (lane < 8 * (start + GROUPS))
    panel = [jnp.where(inside, -x, x) for x in panel]
    change = dot_t(left, stack_right(jnp.concatenate(panel, axis=0)))
    swept = []
    for g in range(len(block)):
        if start <= g < start + GROUPS:
            swept.append(panel[g - start])
        else:
            swept.append(jnp.where(inside, 0.0, block[g]) - change[8 * g : 8 * g + 8, :])
    return swept


def eliminate_group(panel, t, at, cols, rows):
    lane = lax.broadcasted_iota(jnp.int32, (8, LANES), 1)
    sub = lax.broadcasted_iota(jnp.int32, (8, LANES), 0)
    for j in range(8):
        cols[64 * at + 8 * j : 64 * at + 8 * j + 8, :] = spread_lane(panel[t], 8 * at + j)
    rows[8 * at : 8 * at + 8, :] = panel[t]
    entry = {}
    for i in range(8):
        for j in range(i + 1):
            row = 64 * at + 8 * j + i
            entry[i, j] = jnp.broadcast_to(cols[row : row + 1, :], (8, LANES))
    inside = (lane >= 8 * at) & (lane < 8 * at + 8)
    line = []
    for j in range(8):
        row = jnp.broadcast_to(rows[8 * at + j : 8 * at + j + 1, :], (8, LANES))
        line.append(jnp.where(inside, jnp.where(lane == 8 * at + j, 1.0, 0.0), row))
    after = None
    if t < GROUPS - 1:
        columns = [spread_lane(panel[t + 1], 8 * at + j) for j in range(8)]
        after = [columns, jnp.where(inside, 0.0, panel[t + 1])]
    line, after = solve_small(entry, line, after)
    for g in range(GROUPS):
        if g == t + 1:
            panel[g] = after
        elif g != t:
            terms = [spread_lane(panel[g], 8 * at + j) * line[j] for j in range(8)]
            panel[g] = jnp.where(inside, 0.0, panel[g]) - tree_sum(terms)
    merged = line[0]
    for j in range(1, 8):
        merged = jnp.where(sub == j, line[j], merged)
    panel[t] = merged
    return panel


def tree_sum(terms):
    while len(terms) > 1:
        terms = [
            terms[i] + terms[i + 1] if i + 1 < len(terms) else terms[i]
            for i in range(0, len(terms), 2)
        ]
    return terms[0]


def solve_small(entry, line, after):
    columns, block = after or (None, None)
    factors, scaled = {}, {}
    for k in range(0, 8, 2):
        a, b, c = entry[k, k], entry[k + 1, k], entry[k + 1, k + 1]
        inv = pl.reciprocal(a * c - b * b, approx=True)
        below = range(k + 2, 8)
        first = {i: c * entry[i, k] - b * entry[i, k + 1] for i in below}
        second = {i: a * entry[i, k + 1] - b * entry[i, k] for i in below}
        for i in below:
            for j in range(k + 2, i + 1):
                entry[i, j] = entry[i, j] - inv * (first[i] * entry[j, k] + second[i] * entry[j, k + 1])
        top = c * line[k] - b * line[k + 1]
        bottom = a * line[k + 1] - b * line[k]
        if columns is not None:
            block = block - inv * (columns[k] * top + columns[k + 1] * bottom)
        scaled[k], scaled[k + 1] = inv * top, inv * bottom
        for i in below:
            m, n = inv * first[i], inv * second[i]
            factors[i, k] = m, n
            line[i] = line[i] - (m * line[k] + n * line[k + 1])
            if columns is not None:
                columns[i] = columns[i] - (m * columns[k] + n * columns[k + 1])
    for k in range(6, -1, -2):
        x, y = scaled[k], scaled[k + 1]
        if k < 6:
            x = x - tree_sum([factors[i, k][0] * line[i] for i in range(k + 2, 8)])
            y = y - tree_sum([factors[i, k][1] * line[i] for i in range(k + 2, 8)])
        line[k], line[k + 1] = x, y
    return line, block


def stack_left(x):
    h, m, l = split3(x)
    return jnp.concatenate([h, h, m, h, l, m], axis=0)


def stack_right(x):
    h, m, l = split3(x)
    return jnp.concatenate([h, m, h, l, h, m], axis=0)


def sweep(matrix, panels, cols, rows):
    block = [matrix[8 * i : 8 * i + 8, :] for i in range(LANES // 8)]
    for panel in panels:
        block = sweep_panel(block, panel * GROUPS, cols, rows)
    return jnp.concatenate(block, axis=0)


PANELS = LANES // (8 * GROUPS)


SQUARE = jax.ShapeDtypeStruct((R, R), F32)
CORNER = jax.ShapeDtypeStruct((LANES, LANES), F32)


def call(kernel, out_shape, args, name, scratch=(), flops=0):
    return pl.pallas_call(
        kernel,
        out_shape=out_shape,
        scratch_shapes=list(scratch),
        compiler_params=pltpu.CompilerParams(vmem_limit_bytes=VMEM_LIMIT),
        cost_estimate=pl.CostEstimate(flops=flops, bytes_accessed=R * R * 4, transcendentals=0),
        name=name,
    )(*args)


def first_kernel(which, gram_ref, coupling, first_out, across_out, rest_out, row_out, col_out, cols, rows):
    matrix = coupling[which()] + load_symmetric(gram_ref, OWN)
    eye = lax.broadcasted_iota(jnp.int32, (R, R), 0) == lax.broadcasted_iota(jnp.int32, (R, R), 1)
    diagonal = jnp.where(eye, matrix, 0.0)
    scale_row = lax.rsqrt(jnp.sum(diagonal, axis=0, keepdims=True))
    scale_col = lax.rsqrt(jnp.sum(diagonal, axis=1, keepdims=True))
    matrix = matrix * scale_col * scale_row
    side = matrix[:LANES, LANES:]
    first = -sweep(matrix[:LANES, :LANES], range(PANELS), cols, rows)
    across = dot_full(first, side)
    first_out[...] = first
    across_out[...] = across
    rest_out[...] = matrix[LANES:, LANES:] - dot_t_full(side, across)
    row_out[...] = jnp.broadcast_to(scale_row, (8, R))
    col_out[...] = jnp.broadcast_to(scale_col, (R, LANES))


def middle_kernel(rest, out, cols, rows):
    out[...] = sweep(rest[...], range(PANELS - 1), cols, rows)


def second_kernel(first, across, swept, row, col, out, cols, rows):
    second = -sweep(swept[...], range(PANELS - 1, PANELS), cols, rows)
    corner = -dot_full(across[...], second)
    top = first[...] - dot_full(corner, across[...].T)
    out[:LANES, :LANES] = top * col[:LANES, :] * row[:1, :LANES]
    out[:LANES, LANES:] = corner * col[:LANES, :] * row[:1, LANES:]
    out[LANES:, :LANES] = corner.T * col[LANES:, :] * row[:1, :LANES]
    out[LANES:, LANES:] = second * col[LANES:, :] * row[:1, LANES:]


SCRATCH = [pltpu.VMEM((1024, LANES), F32), pltpu.VMEM((LANES, LANES), F32)]
HALF_FLOPS = 5_000_000_000


def invert_first(which, packed, coupling, name):
    shapes = (
        CORNER,
        CORNER,
        CORNER,
        jax.ShapeDtypeStruct((8, R), F32),
        jax.ShapeDtypeStruct((R, LANES), F32),
    )
    kernel = functools.partial(first_kernel, which)
    return call(kernel, shapes, (packed, coupling), name, SCRATCH, HALF_FLOPS)


def invert_middle(parts, name):
    first, across, rest, row, col = parts
    rest = call(middle_kernel, CORNER, (rest,), name, SCRATCH, HALF_FLOPS // 2)
    return first, across, rest, row, col


def invert_second(parts, name):
    return call(second_kernel, SQUARE, parts, name, SCRATCH, HALF_FLOPS // 2)


def half_index():
    return lax.axis_index("group") // 2


def no_index():
    return 0


def panel_solve_kernel(inverse, terms, x_out, root_out):
    cross = load_square(terms, CROSS)
    x = dot_full(inverse[...], cross)
    x_out[...] = x
    store_symmetric(root_out, 0, load_symmetric(terms, ROOT) - dot_t_full(cross, x))


def wide(x):
    high, low = split2(x)
    return jnp.concatenate([high, high, low], axis=1)


def tall(x):
    high, low = split2(x)
    return jnp.concatenate([high, low, high], axis=0)


def by_tiles(rows, out, stage, sems, value, beside=None):
    tiles = rows // OUT_TILE

    def at(tile):
        return pl.ds(pl.multiple_of(tile * OUT_TILE, OUT_TILE), OUT_TILE)

    def copy(tile):
        return pltpu.make_async_copy(stage.at[at(tile)], out.at[at(tile)], sems.at[tile])

    def step(tile, carry):
        stage[at(tile), :] = value(at(tile))
        copy(tile).start()
        return carry

    lax.fori_loop(0, tiles, step, 0)
    if beside is not None:
        beside()
    for tile in range(tiles):
        copy(tile).wait()


def panel_kernel(b2, b1, sources, x, inverse, terms, out, level, high, low, side_out, stage, sems):
    projected = load_square(terms, PROJECTED)
    pieces = tall(projected)
    y = dot(wide(inverse[...]), pieces)
    store_square(side_out, 0, load_square(terms, SIDE) - dot(wide(x[...].T), pieces))
    right = jnp.concatenate([tall(x[...]), tall(y)], axis=1)

    def value(at):
        change = dot(wide(b2[at, :]), right)
        panel = b1[at, :] - change[:, :R]
        level[at, :] = sources[at, :] - change[:, R:]
        high[at, :], low[at, :] = split2(panel)
        return panel

    by_tiles(b2.shape[0], out, stage, sems, value)


def field_kernel(level, high, low, inverse, side, out, stage, sems):
    weights = tall(dot(wide(inverse[...]), tall(load_square(side, 0))))

    def value(at):
        left = jnp.concatenate([high[at, :], high[at, :], low[at, :]], axis=1)
        return level[at, :] - dot(left, weights)

    by_tiles(level.shape[0], out, stage, sems, value)


def update(kernel, args, passes, name, more=()):
    rows = args[0].shape[0]
    return pl.pallas_call(
        kernel,
        out_specs=[pl.BlockSpec(memory_space=pl.ANY)] + [pl.BlockSpec(memory_space=pltpu.VMEM)] * len(more),
        out_shape=[jax.ShapeDtypeStruct((rows, R), F32), *more],
        scratch_shapes=[pltpu.VMEM((rows, R), F32), pltpu.SemaphoreType.DMA((rows // OUT_TILE,))],
        compiler_params=pltpu.CompilerParams(vmem_limit_bytes=VMEM_LIMIT),
        cost_estimate=cost(passes, rows, 3),
        name=name,
    )(*args)


def exchange(x, mask):
    count = lax.axis_size(AXES)
    return lax.ppermute(x, AXES, [(i, i ^ mask) for i in range(count)])


def choose(x, upper):
    half = half_of(x.shape[0])
    low, high = x[:half], x[x.shape[0] - half :]
    return jnp.where(upper, high, low), jnp.where(upper, low, high)


def join(x, other, rows, upper):
    low, high = jnp.where(upper, other, x), jnp.where(upper, x, other)
    return jnp.concatenate([low[: rows - x.shape[0]], high], axis=0)


def summing_stages(bits):
    down = [("scatter", bit) for bit in bits[:-1]]
    return down + [("sum", bits[-1])] + [("gather", bit) for bit in reversed(bits[:-1])]


class Chain:
    def __init__(self, value, upper):
        self.value, self.upper, self.sizes = value, upper, {}

    def start(self, kind, bit):
        self.kind, self.bit = kind, bit
        sent = self.value
        if kind == "scatter":
            self.sizes[bit] = self.value.shape[0]
            self.value, sent = choose(self.value, self.upper[bit])
        self.flying = exchange(sent, 1 << bit)

    def finish(self):
        if self.kind == "gather":
            self.value = join(self.value, self.flying, self.sizes[self.bit], self.upper[self.bit])
        else:
            self.value = self.value + self.flying


def per_device(q_two, q_one, sources, coupling_two, coupling_one):
    index = lax.axis_index(AXES)
    places = lax.axis_size(AXES).bit_length() - 1
    flags = [(index >> bit) & 1 == 1 for bit in range(places)]
    q_two, *upper = lax.optimization_barrier((q_two, *flags))
    stages = summing_stages(list(range(2, places)))

    keep, send, b2, b1 = panel_gram(q_two, q_one)
    arriving = exchange(send, 1)
    source_keep, source_send = source_gram(b2, b1, sources)
    arriving, source_send = lax.optimization_barrier((arriving, source_send))

    panels = Chain(keep + arriving, upper)
    source = Chain(source_keep, upper)
    panels.sizes[0], source.sizes[0] = PANEL_TERMS, SOURCE_TERMS
    source_left = [("gather", 0)] + stages[::-1]
    for step, stage in enumerate(stages):
        panels.start(*stage)
        if step == 0:
            source.kind, source.bit, source.flying = "sum", 0, exchange(source_send, 1)
        else:
            source.start(*source_left.pop())
        panels.flying, source.flying = lax.optimization_barrier((panels.flying, source.flying))
        panels.finish()
        source.finish()
    panels.start("gather", 0)
    source.start(*source_left.pop())
    panels.finish()
    terms = panels.value
    parts = invert_first(half_index, terms, coupling_two, "level_first")
    parts = invert_middle(parts, "level_middle")
    source.flying, parts = lax.optimization_barrier((source.flying, parts))
    source.finish()
    source.start(*source_left.pop())
    inverse = invert_second(parts, "level_second")
    x, root = call(
        panel_solve_kernel, (SQUARE, jax.ShapeDtypeStruct((SYMMETRIC, LANES), F32)), (inverse, terms), "panel_solve"
    )
    source.flying, x = lax.optimization_barrier((source.flying, x))
    source.finish()
    arriving = exchange(root, 2)
    rows = b2.shape[0]
    shapes = [jax.ShapeDtypeStruct((rows, R), kind) for kind in (F32, BF16, BF16)]
    shapes.append(jax.ShapeDtypeStruct((FULL, LANES), F32))
    args = [b2, b1, sources, x, inverse, source.value]
    panel_one, level, high, low, side = update(panel_kernel, args, 8, "panel", shapes)
    side = Chain(choose(side, upper[0])[0], upper)
    side.sizes[0] = FULL
    side_flying = exchange(side.value, 2)
    arriving, side.value = lax.optimization_barrier((arriving, side.value))
    root = root + arriving
    parts = invert_first(no_index, root, coupling_one[None], "root_first")
    parts = invert_middle(parts, "root_middle")
    side_flying, parts = lax.optimization_barrier((side_flying, parts))
    side.value = side.value + side_flying
    side.start("gather", 0)
    inverse = invert_second(parts, "root_second")
    side.finish()
    (solution,) = update(field_kernel, [level, high, low, inverse, side.value], 3, "field")
    return (panel_one, solution)


def solution(mesh):
    placed = P(("group", "leaf"), None)
    return jax.shard_map(
        per_device,
        mesh=mesh,
        in_specs=(placed, placed, placed, P(), P()),
        out_specs=(placed, placed),
        check_vma=False,
    )
```
